256 devices in a mesh: sub: 64 (over y, z, core), rhs: 4 (over x).
Axes of the slice: x: 4, y: 4, z: 8, core: 2. Of those that a mesh axis runs over, the one named last changes fastest.
Arguments:
- right_side: float32 [256, 252, 512], P('sub', None, 'rhs'), parts along dimension 2, may hold values from -70 to 70
- coupling: bfloat16 [256, 508032], P('sub'), may hold values from -0.0625 to 0.0625
- neighbours: int32 [256, 8], P('sub'), may hold values from 0 to 255, as said below
- inverse: bfloat16 [64, 1512, 1512], P('sub'), may hold values from -1 to 1
- margin: int32 [64, 2], P('sub'), may hold values from 0 to 255, as said below
- counts: int32 [64], P('sub'), may hold values from 1 to 4, as said below
Outputs:
- solution: float32 [256, 252, 512], P('sub', None, 'rhs'), parts along dimension 2
The draws below stay inside these ranges and needn't reach their ends.
There are 4 independent parts, one for each index of `rhs`. The reference program is written for one: setup_inputs(seed, part) draws one part's arguments, and reference() takes and returns one part's arrays. A program takes and returns all parts, laid end to end along the dimension named above; an argument that names none is the same for every part. Nothing has to cross between parts.
Inputs may be any that keep to these rules, and one draw needn't show every extreme that they name: `counts`: every subdomain holds 1 to 4 live spheres, and some subdomain holds exactly 4. `neighbours`: every entry of row i is a live sphere slot of the subdomain of i or of a subdomain adjacent to it (index one lower or one higher). `margin`: for subdomain d the first 1 entries are live slots of subdomain d - 1 (of subdomain 0 itself for d = 0), the last 1 live slots of subdomain d + 1 (of the last subdomain itself for the last one).
All inputs are finite; a program needn't handle non-finite values.
Results may differ from the reference program's by a relative error of at most 0.0055.
Values may be sent and summed in bfloat16 or wider, within the bound.
No kernel may reach another device: no remote copies, remote signals or barrier semaphores. Data moves between devices by JAX's collectives and lax.ppermute only.
A program may use at most 64 MiB of HBM per device.

```python
import math
import jax
import jax.numpy as jnp
from jax import lax

W = 252
P_SIZE = 4
NB = 8
OV_SIDE = 1
RHS = 128
NSUB = 64
S = 256
Q = 6


def packing(key):
    key = jax.random.fold_in(key, 11)
    first, second, third = jax.random.split(key, 3)
    factor_a = jax.random.randint(first, (NSUB,), 0, P_SIZE)
    factor_b = jax.random.randint(second, (NSUB,), 0, P_SIZE)
    filled = 1 + factor_a * factor_b // P_SIZE
    fullest = jax.random.randint(third, (), 0, NSUB)
    return jnp.where(jnp.arange(NSUB, dtype=jnp.int32) == fullest, P_SIZE, filled).astype(jnp.int32)


def draw_counts(key, part):
    return packing(key)


def draw_neighbours(key, part):
    filled = packing(key)
    key = jax.random.fold_in(key, 21)
    first, second = jax.random.split(key)
    offsets = jax.random.randint(first, (S, NB), -1, 2)
    owners = jnp.arange(S, dtype=jnp.int32) // P_SIZE
    domains = jnp.clip(owners[:, None] + offsets, 0, NSUB - 1)
    raw = jax.random.randint(second, (S, NB), 0, 1 << 20)
    return (domains * P_SIZE + raw % filled[domains]).astype(jnp.int32)


def draw_margin(key, part):
    filled = packing(key)
    key = jax.random.fold_in(key, 31)
    places = jnp.arange(NSUB, dtype=jnp.int32)
    lower = jnp.maximum(places - 1, 0)
    upper = jnp.minimum(places + 1, NSUB - 1)
    domains = jnp.concatenate([jnp.tile(lower[:, None], (1, OV_SIDE)), jnp.tile(upper[:, None], (1, OV_SIDE))], axis=1)
    raw = jax.random.randint(key, (NSUB, 2 * OV_SIDE), 0, 1 << 20)
    return (domains * P_SIZE + raw % filled[domains]).astype(jnp.int32)


def draw_right_side(key, part):
    key = jax.random.fold_in(key, 41)
    first, second = jax.random.split(key)
    owners = jnp.arange(S, dtype=jnp.int32) // P_SIZE
    rising = 1.0 + 2.0 * owners.astype(jnp.float32) / max(NSUB - 1, 1)
    values = jnp.clip(jax.random.normal(first, (S, W, RHS), jnp.float32), -4.0, 4.0)
    scales = jnp.exp(jax.random.uniform(second, (S, 1, RHS), jnp.float32, -0.7, 0.7))
    return values * scales * rising[:, None, None]


def draw_inverse(key, part):
    key = jax.random.fold_in(key, 51)
    extent = Q * W
    noise = jnp.clip(jax.random.normal(key, (NSUB, extent, extent), jnp.float32), -4.0, 4.0)
    return (0.8 * jnp.eye(extent, dtype=jnp.float32)[None] + noise * (0.4 / math.sqrt(extent))).astype(jnp.bfloat16)


def block_levels(key, shape, cuts, least, top_value):
    def one(position, blocks):
        steps = jax.random.uniform(jax.random.fold_in(jax.random.fold_in(key, 6), position), (blocks,), jnp.float32, least / len(cuts), top_value / len(cuts))
        return jnp.repeat(jnp.exp(steps), shape[position] // blocks).reshape((-1,) + (1,) * (len(shape) - position - 1))

    gain = one(*cuts[0])
    for cut in cuts[1:]:
        gain = gain * one(*cut)
    return gain


def centred(own_key, shape, spread, most, shards=(), kind=jnp.bfloat16):
    factor_of = block_levels(own_key, shape, shards, -0.22, 0.18) if shards else 1.0
    result = jax.random.normal(own_key, shape, jnp.float32) * spread * factor_of
    return jnp.minimum(jnp.maximum(result, -most), most).astype(kind)


def setup_inputs(seed: int = 0, part: int = 0) -> dict:
    splits = jax.random.split(jax.random.key(seed), 7)
    own_keys = jax.random.split(jax.random.fold_in(splits[6], part), 7)
    right_side = draw_right_side(jax.random.fold_in(jax.random.fold_in(splits[6], part), 71), part)
    coupling = centred(splits[1], (S, NB * W * W), (4 * NB * W) ** -0.5, 0.0625, ((0, 64),))
    neighbours = draw_neighbours(jax.random.fold_in(splits[6], 71), part)
    inverse = draw_inverse(jax.random.fold_in(splits[6], 71), part)
    margin = draw_margin(jax.random.fold_in(splits[6], 71), part)
    counts = draw_counts(jax.random.fold_in(splits[6], 71), part)
    return dict(right_side=right_side, coupling=coupling, neighbours=neighbours, inverse=inverse, margin=margin, counts=counts)


epsilon = 1e-06

def live_mask(counts):
    slots = jnp.arange(P_SIZE, dtype=jnp.int32)
    return (slots[None, :] < counts[:, None]).astype(jnp.float32).reshape(NSUB * P_SIZE)

def apply_system(vector, coupling, neighbours, live_rows):
    rounded = lax.optimization_barrier(vector.astype(jnp.bfloat16)).astype(jnp.float32)
    fields = vector.shape[2]

    def domain_product(domain):
        matrices = lax.dynamic_slice_in_dim(coupling, domain * P_SIZE, P_SIZE, 0).astype(jnp.float32).reshape(P_SIZE, NB, W, W)
        indices = lax.dynamic_slice_in_dim(neighbours, domain * P_SIZE, P_SIZE, 0).reshape(P_SIZE * NB).astype(jnp.int32)
        nearby = jnp.take(rounded, indices, axis=0).reshape(P_SIZE, NB, W, fields)
        return jnp.einsum('pkvw,pkwr->pvr', matrices, nearby, precision=lax.Precision.HIGHEST)
    contrib = lax.map(domain_product, jnp.arange(NSUB, dtype=jnp.int32))
    contrib = contrib.reshape(vector.shape)
    return (vector + contrib) * live_rows[:, None, None]

def precondition(vector, inverse, margin, live_rows):
    rounded = vector.astype(jnp.bfloat16)
    fields = vector.shape[2]

    def advance(running, item):
        domain, matrix, extra = item
        indices = jnp.concatenate([domain * P_SIZE + jnp.arange(P_SIZE, dtype=jnp.int32), extra.astype(jnp.int32)])
        local_rows = jnp.take(rounded, indices, axis=0).reshape(Q * W, fields)
        output = jnp.dot(matrix, local_rows, preferred_element_type=jnp.float32)
        return (running.at[indices].add(output.reshape(Q, W, fields)), None)
    summed, unused = lax.scan(advance, jnp.zeros(vector.shape, jnp.float32), (jnp.arange(NSUB, dtype=jnp.int32), inverse, margin))
    return summed * live_rows[:, None, None]

def inner(left, right):
    return lax.optimization_barrier(jnp.sum(left * right, axis=(0, 1)))

def reference(right_side, coupling, neighbours, inverse, margin, counts):
    live_rows = live_mask(counts)
    start = right_side * live_rows[:, None, None]
    initial = jnp.sqrt(inner(start, start) + epsilon)
    basis_one = start / initial[None, None, :]
    pre_one = precondition(basis_one, inverse, margin, live_rows)
    image = apply_system(pre_one, coupling, neighbours, live_rows)
    h_one_one = inner(basis_one, image)
    image = image - h_one_one[None, None, :] * basis_one
    h_two_one = jnp.sqrt(inner(image, image) + epsilon)
    basis_two = image / h_two_one[None, None, :]
    pre_two = precondition(basis_two, inverse, margin, live_rows)
    image = apply_system(pre_two, coupling, neighbours, live_rows)
    h_one_two = inner(basis_one, image)
    image = image - h_one_two[None, None, :] * basis_one
    h_two_two = inner(basis_two, image)
    image = image - h_two_two[None, None, :] * basis_two
    h_three_two = jnp.sqrt(inner(image, image) + epsilon)
    gram_aa = h_one_one * h_one_one + h_two_one * h_two_one
    gram_ab = h_one_one * h_one_two + h_two_one * h_two_two
    gram_bb = h_one_two * h_one_two + h_two_two * h_two_two + h_three_two * h_three_two
    determinant = gram_aa * gram_bb - gram_ab * gram_ab
    weight_one = initial * (gram_bb * h_one_one - gram_ab * h_one_two) / determinant
    weight_two = initial * (gram_aa * h_one_two - gram_ab * h_one_one) / determinant
    return weight_one[None, None, :] * pre_one + weight_two[None, None, :] * pre_two
```

```python
import functools
import jax
import jax.numpy as jnp
from jax import lax
from jax.experimental import pallas as pl
from jax.experimental.pallas import tpu as pltpu
from jax.sharding import PartitionSpec as P

EPS = 1e-06
W = 252
WP = 256
NS = 4
NB = 8
R = 128
NSUB = 64
SHIFT = 1.0
ROWS = NB * W
GROUP = 32
F32 = jnp.float32
BF16 = jnp.bfloat16
VM = pl.BlockSpec(memory_space=pltpu.VMEM)
SM = pl.BlockSpec(memory_space=pltpu.SMEM)


def call(kernel, outs, ins, scratch=(), limit=24, **cost):
    return pl.pallas_call(
        kernel,
        out_shape=[jax.ShapeDtypeStruct(s, d) for s, d in outs],
        in_specs=ins,
        out_specs=[VM] * len(outs),
        scratch_shapes=list(scratch),
        compiler_params=pltpu.CompilerParams(vmem_limit_bytes=limit << 20),
    )


def start_kernel(counts, right, v0_ref, v0b_ref):
    for s in range(NS):
        alive = jnp.where(counts[0] > s, 1.0, 0.0)
        v0_ref[s, :W, :] = right[pl.ds(s, W, stride=NS), :] * alive
        v0_ref[s, W:, :] = jnp.zeros((WP - W, R), F32)
        v0b_ref[s] = v0_ref[s].astype(BF16)


def coupling_kernel(flat, c_ref, lo, hi):
    lanes = GROUP * W

    def group(g, carry):
        x = flat[:, pl.ds(pl.multiple_of(g * lanes, 128), lanes)].astype(F32)
        base = pl.multiple_of(g * GROUP * NS, 8)
        for s in range(0, GROUP, 2):
            a = x[:, s * W : (s + 1) * W]
            b = x[:, (s + 1) * W : (s + 2) * W]
            lo[pl.ds(base + s * NS, 2 * NS), :] = jnp.concatenate([a[:, :128], b[:, :128]], axis=0)
            hi[pl.ds(base + s * NS, 2 * NS), : W - 128] = jnp.concatenate([a[:, 128:], b[:, 128:]], axis=0)
        return carry

    lax.fori_loop(0, ROWS // GROUP, group, 0)
    keep = lax.broadcasted_iota(jnp.int32, (WP, 128), 1) < W - 128
    pad = jnp.zeros((WP - W, 128), F32)

    def place(k, carry):
        for p in range(NS):
            first = k * (W * NS) + p
            left = lo[pl.ds(first, W, stride=NS), :]
            right = hi[pl.ds(first, W, stride=NS), :]
            left = jnp.concatenate([left, pad], axis=0)
            right = jnp.where(keep, jnp.concatenate([right, pad], axis=0), 0.0)
            c_ref[p * NB + k, :, :128] = left.astype(BF16)
            c_ref[p * NB + k, :, 128:] = right.astype(BF16)
        return carry

    lax.fori_loop(0, NB, place, 0)


def solve_kernel(
    place, margin, inverse, own, left, right,
    out_ref, up_ref, down_ref, ext, res,
):
    here = place[0]
    low = jnp.clip(margin[0, 0] - NS * jnp.maximum(here - 1, 0), 0, NS - 1)
    high = jnp.clip(margin[0, 1] - NS * jnp.minimum(here + 1, NSUB - 1), 0, NS - 1)
    for s in range(NS):
        ext[s * W : (s + 1) * W, :] = own[s, :W, :]
    some = left.shape[0] > 1

    def put(first, from_own, got, index):
        @pl.when(from_own)
        def _():
            ext[first : first + W, :] = own[index][:W]

        @pl.when(jnp.logical_not(from_own))
        def _():
            ext[first : first + W, :] = got[index if some else 0].astype(F32)[:W]

    put(NS * W, here == 0, left, low)
    put((NS + 1) * W, here == NSUB - 1, right, high)
    res[...] = jnp.dot(inverse[0], ext[...].astype(BF16), preferred_element_type=F32)
    pad = jnp.zeros((WP - W, R), F32)
    for s in range(NS):
        out_ref[s] = jnp.concatenate([res[s * W : (s + 1) * W, :], pad], axis=0)
    spill_low = res[NS * W : (NS + 1) * W, :]
    spill_high = res[(NS + 1) * W : (NS + 2) * W, :]

    @pl.when(here == 0)
    def _():
        out_ref[low] += jnp.concatenate([spill_low, pad], axis=0)

    @pl.when(here == NSUB - 1)
    def _():
        out_ref[high] += jnp.concatenate([spill_high, pad], axis=0)

    for s in range(NS):
        block = out_ref[s].astype(BF16)
        up_ref[s] = block
        down_ref[s] = block
    mark = jnp.ones((WP - W, R), F32)
    up_ref[NS] = jnp.concatenate([spill_high, mark * high.astype(F32)], axis=0).astype(BF16)
    down_ref[NS] = jnp.concatenate([spill_low, mark * low.astype(F32)], axis=0).astype(BF16)


def opened(block):
    x = block.astype(F32)
    rows = lax.broadcasted_iota(jnp.int32, x.shape, 0)
    return jnp.where(rows < W, x, 0.0), x[W : W + 1, :]


def system_kernel(
    first, place, counts, neighbours, c_ref, out, up, down, low, high, low2, high2, v0, *rest
):
    if first:
        p_ref, w_ref, wup_ref, wdown_ref, sums_ref, u = rest
    else:
        w, p_ref, sums_ref, u = rest
    here = place[0]
    spill_low = opened(low[NS])
    spill_high = opened(high[NS])
    mine_low = opened(down[NS])
    mine_high = opened(up[NS])
    far_low = opened(low2[0])
    far_high = opened(high2[0])
    rows = lax.broadcasted_iota(jnp.int32, (WP, R), 0) < W

    def added(x, spill, s):
        return x + jnp.where(spill[1] == s, spill[0], 0.0)

    for s in range(NS):
        u[s] = added(added(low[s].astype(F32), mine_low, s), far_low, s).astype(BF16)
        u[2 * NS + s] = added(added(high[s].astype(F32), mine_high, s), far_high, s).astype(BF16)
        alive = jnp.where(counts[0] > s, 1.0, 0.0)
        mine = added(added(out[s], spill_low, s), spill_high, s) * alive
        p_ref[s] = mine
        u[NS + s] = mine.astype(BF16)
    del rows
    zero = jnp.zeros((1, R), F32)
    sums = [zero] * 3
    for s in range(NS):
        acc = jnp.zeros((WP, R), F32)
        for k in range(NB):
            slot = jnp.clip(neighbours[s, k] - NS * (here - 1), 0, 3 * NS - 1)
            acc += jnp.dot(c_ref[s * NB + k], u[slot], preferred_element_type=F32)
        alive = jnp.where(counts[0] > s, 1.0, 0.0)
        image = (p_ref[s] + acc) * alive
        start = v0[s]
        if first:
            image = image - SHIFT * start
            w_ref[s] = image
            terms = (start * start, start * image, image * image)
        else:
            terms = (start * image, w[s] * image, image * image)
        sums = [t + jnp.sum(x, axis=0, keepdims=True) for t, x in zip(sums, terms)]
    if first:
        for ref, index in ((wup_ref, spill_high[1]), (wdown_ref, spill_low[1])):
            chosen = jnp.zeros((WP, R), F32)
            for s in range(NS):
                chosen = chosen + jnp.where(index == s, w_ref[s], 0.0)
            ref[0] = chosen.astype(BF16)
    sums_ref[...] = jnp.concatenate(sums + [zero] * 5, axis=0)


def finish_kernel(gathered, p0, q, out):
    total = jnp.sum(gathered[...], axis=0)
    s00, s01, s11, s02, s12, s22 = (total[i : i + 1, :] for i in range(6))
    c = SHIFT
    bb = s00 + EPS
    beta = jnp.sqrt(bb)
    h11 = (s01 + c * s00) / bb
    a = c - h11
    n2 = (s11 + 2 * a * s01 + a * a * s00) / bb
    h21s = jnp.maximum(n2, 0.0) + EPS
    h21 = jnp.sqrt(h21s)
    full = bb * h21s
    v0i = s01 + c * s00
    h12 = (s02 + a * v0i) / (bb * h21)
    cross = (s01 + a * s00) / (bb * h21)
    b2i = (s12 + a * s02 + a * (s11 + c * s01) + a * a * v0i) / full
    h22 = b2i - h12 * cross
    ii = (s22 + 2 * a * (s12 + c * s02) + a * a * (s11 + 2 * c * s01 + c * c * s00)) / full
    rest = (
        ii + h12 * h12 * (s00 / bb) + h22 * h22 * (n2 / h21s)
        - 2 * h12 * h12 - 2 * h22 * b2i + 2 * h12 * h22 * cross
    )
    h32s = jnp.maximum(rest, 0.0) + EPS
    g00 = h11 * h11 + h21s
    g01 = h11 * h12 + h21 * h22
    g11 = h12 * h12 + h22 * h22 + h32s
    det = g00 * g11 - g01 * g01
    y1 = beta * (g11 * h11 - g01 * h12) / det
    y2 = beta * (g00 * h12 - g01 * h11) / det
    two = y2 / (beta * h21)
    one = y1 / beta + a * two
    for s in range(NS):
        out[pl.ds(s, W, stride=NS), :] = one * p0[s, :W, :] + two * q[s, :W, :]


def shifted(x, by):
    pairs = [(i, i + by) for i in range(NSUB) if 0 <= i + by < NSUB]
    return lax.ppermute(x, "sub", pairs)


def body(right_side, coupling, neighbours, inverse, margin, counts):
    here = lax.axis_index("sub").astype(jnp.int32).reshape(1)
    flat_right = right_side.transpose(1, 0, 2).reshape(W * NS, R)
    block = (NS, WP, R)
    v0, v0b = call(start_kernel, [(block, F32), (block, BF16)], [SM, VM])(counts, flat_right)
    (mats,) = call(
        coupling_kernel,
        [((NS * NB, WP, WP), BF16)],
        [VM],
        [pltpu.VMEM((ROWS * NS, 128), F32)] * 2,
        limit=32,
    )(coupling)

    def solve(own, left, right):
        return call(
            solve_kernel,
            [(block, F32), ((NS + 1, WP, R), BF16), ((NS + 1, WP, R), BF16)],
            [SM, SM, VM, VM, VM, VM],
            [pltpu.VMEM((6 * W, R), F32)] * 2,
        )(here, margin, inverse, own, left, right)

    def system(first, out, up, down, *more):
        low, high = shifted(up, 1), shifted(down, -1)
        low2, high2 = shifted(up[NS:], 2), shifted(down[NS:], -2)
        if first:
            outs = [(block, F32)] * 2 + [((1, WP, R), BF16)] * 2 + [((8, R), F32)]
        else:
            outs = [(block, F32), ((8, R), F32)]
        return call(
            functools.partial(system_kernel, first),
            outs,
            [SM, SM, SM] + [VM] * (8 + len(more)),
            [pltpu.VMEM((3 * NS, WP, R), BF16)],
        )(here, counts, neighbours, mats, out, up, down, low, high, low2, high2, *more)

    out, up, down = solve(v0, shifted(v0b, 1), shifted(v0b, -1))
    p0, w, wup, wdown, sums_one = system(True, out, up, down, v0)
    out, up, down = solve(w, shifted(wup, 1), shifted(wdown, -1))
    q, sums_two = system(False, out, up, down, v0, w)
    sums = jnp.concatenate([sums_one[:3], sums_two[:3]], axis=0)
    gathered = lax.all_to_all(jnp.broadcast_to(sums[None], (NSUB, 6, R)), "sub", 0, 0)
    (flat,) = call(finish_kernel, [((W * NS, R), F32)], [VM] * 3)(gathered, p0, q)
    return flat.reshape(W, NS, R).transpose(1, 0, 2)


def solution(mesh):
    placed = (
        P("sub", None, "rhs"),
        P("sub", None),
        P("sub", None),
        P("sub", None, None),
        P("sub", None),
        P("sub"),
    )
    return jax.shard_map(
        body, mesh=mesh, in_specs=placed, out_specs=P("sub", None, "rhs"), check_vma=False
    )
```

```python
import functools
import jax
import jax.numpy as jnp
from jax import lax
from jax.experimental import pallas as pl
from jax.experimental.pallas import tpu as pltpu
from jax.sharding import PartitionSpec as P

EPS = 1e-06
W = 252
WP = 256
NS = 4
NB = 8
R = 128
NSUB = 64
SHIFT = 1.0
ROWS = NB * W
GROUP = 32
F32 = jnp.float32
BF16 = jnp.bfloat16
GROUPS = 32
CHUNKS = 4
ANY = pl.BlockSpec(memory_space=pl.ANY)
VM = pl.BlockSpec(memory_space=pltpu.VMEM)
SM = pl.BlockSpec(memory_space=pltpu.SMEM)


def call(kernel, outs, ins, scratch=(), limit=24, cost=None):
    return pl.pallas_call(
        kernel,
        out_shape=[pltpu.VMEM(s, d) if keep else jax.ShapeDtypeStruct(s, d) for s, d, *keep in outs],
        in_specs=ins,
        out_specs=[VM] * len(outs),
        scratch_shapes=list(scratch),
        compiler_params=pltpu.CompilerParams(vmem_limit_bytes=limit << 20),
        cost_estimate=cost,
    )


def start_kernel(counts, right, v0_ref, v0b_ref):
    for s in range(NS):
        alive = jnp.where(counts[0] > s, 1.0, 0.0)
        v0_ref[s, :W, :] = right[pl.ds(s, W, stride=NS), :] * alive
        v0_ref[s, W:, :] = jnp.zeros((WP - W, R), F32)
        v0b_ref[s] = v0_ref[s].astype(BF16)


def coupling_kernel(half, flat, *rest):
    if half == 0:
        inverse, c_ref, inverse_ref, raw, x, lo, hi, sems = rest
    else:
        _, c_ref, raw, x, lo, hi, sems = rest
    lanes = GROUP * W
    offset = half * (ROWS // GROUP // 2) * lanes
    step = GROUPS // CHUNKS * lanes
    copies = [
        pltpu.make_async_copy(
            flat.at[:, pl.ds(offset + c * step, step)], raw.at[:, pl.ds(c * step, step)], sems.at[c]
        )
        for c in range(CHUNKS)
    ]
    if half == 0:
        copies.append(pltpu.make_async_copy(inverse.at[0], inverse_ref, sems.at[CHUNKS]))
    for copy in copies:
        copy.start()
    lane = lax.broadcasted_iota(jnp.int32, (8, 128), 1)

    def pair(i, carry):
        for h in range(2):
            at = pl.multiple_of((2 * i + h) * lanes, 128)
            x[4 * h : 4 * h + 4, :] = raw[:, pl.ds(at, lanes)].astype(F32)
        base = pl.multiple_of(2 * i * (GROUP * NS), 8)
        for s in range(GROUP):
            def rolled(t):
                piece = x[:, 128 * t : 128 * t + 128]
                return pltpu.roll(piece, 4 * s, 1) if s else piece

            middle = rolled(2 * s)
            if s == 0:
                left, right = middle, rolled(1)
            else:
                early = lane < 4 * s
                left = jnp.where(early, rolled(2 * s - 1), middle)
                right = jnp.where(early, middle, rolled(2 * s + 1)) if s < GROUP - 1 else middle
            for h in range(2):
                at = base + (h * GROUP + s) * NS
                lo[pl.ds(at, NS), :] = left[4 * h : 4 * h + 4]
                hi[pl.ds(at, NS), :] = right[4 * h : 4 * h + 4]
        return carry

    for c in range(CHUNKS):
        copies[c].wait()
        pairs = GROUPS // CHUNKS // 2
        lax.fori_loop(c * pairs, (c + 1) * pairs, pair, 0)
    keep = lax.broadcasted_iota(jnp.int32, (WP, 128), 1) < W - 128
    pad = jnp.zeros((WP - W, 128), F32)
    skip = half * (NB // 2 * W - (ROWS // GROUP // 2) * GROUP) * NS

    def place(k, carry):
        for p in range(NS):
            first = skip + k * (W * NS) + p
            left = lo[pl.ds(first, W, stride=NS), :]
            right = hi[pl.ds(first, W, stride=NS), :]
            right = jnp.where(keep, jnp.concatenate([right, pad], axis=0), 0.0)
            c_ref[p * (NB // 2) + k, :, :128] = jnp.concatenate([left, pad], axis=0).astype(BF16)
            c_ref[p * (NB // 2) + k, :, 128:] = right.astype(BF16)
        return carry

    lax.fori_loop(0, NB // 2, place, 0)
    if half == 0:
        copies[CHUNKS].wait()


def solve_kernel(
    place, margin, inverse, own, inner, outer,
    out_ref, in_ref, out2_ref, ext, res,
):
    here = place[0]
    even = here % 2 == 0
    low = jnp.clip(margin[0, 0] - NS * jnp.maximum(here - 1, 0), 0, NS - 1)
    high = jnp.clip(margin[0, 1] - NS * jnp.minimum(here + 1, NSUB - 1), 0, NS - 1)
    first, last = here == 0, here == NSUB - 1
    for s in range(NS):
        ext[s * W : (s + 1) * W, :] = own[s, :W, :]
    some = inner.shape[0] > 1

    def put(when, block, source, index):
        @pl.when(when)
        def _():
            ext[block * W : (block + 1) * W, :] = source[index].astype(F32)[:W]

    put(first, NS, own, low)
    put(jnp.logical_and(even, jnp.logical_not(first)), NS, outer, low if some else 0)
    put(jnp.logical_not(even), NS, inner, low if some else 0)
    put(last, NS + 1, own, high)
    put(jnp.logical_not(jnp.logical_or(even, last)), NS + 1, outer, high if some else 0)
    put(even, NS + 1, inner, high if some else 0)
    res[...] = jnp.dot(inverse[...], ext[...].astype(BF16), preferred_element_type=F32)
    pad = jnp.zeros((WP - W, R), F32)
    mark = jnp.ones((WP - W, R), F32)
    for s in range(NS):
        out_ref[s] = jnp.concatenate([res[s * W : (s + 1) * W, :], pad], axis=0)

    def spill(block):
        return res[block * W : (block + 1) * W, :]

    def marked(block, index):
        return jnp.concatenate([spill(block), mark * index.astype(F32)], axis=0).astype(BF16)

    @pl.when(first)
    def _():
        out_ref[low] += jnp.concatenate([spill(NS), pad], axis=0)

    @pl.when(last)
    def _():
        out_ref[high] += jnp.concatenate([spill(NS + 1), pad], axis=0)

    @pl.when(even)
    def _():
        in_ref[0] = marked(NS + 1, high)
        out2_ref[0] = marked(NS, low)

    @pl.when(jnp.logical_not(even))
    def _():
        in_ref[0] = marked(NS, low)
        out2_ref[0] = marked(NS + 1, high)


def opened(block):
    x = block.astype(F32)
    rows = lax.broadcasted_iota(jnp.int32, x.shape, 0)
    return jnp.where(rows < W, x, 0.0), x[W : W + 1, :]


def inner_kernel(out, spill_in, spill_out, part_ref, sent_ref):
    values, index = opened(spill_in[0])
    for s in range(NS):
        part = out[s] + jnp.where(index == s, values, 0.0)
        part_ref[s] = part
        sent_ref[s] = part.astype(BF16)
    sent_ref[NS] = spill_out[0]


def outer_kernel(place, counts, part, got, spill_in, spill_out, p_ref, own_ref, outer_ref, marks_ref):
    here = place[0]
    ends = jnp.logical_or(here == 0, here == NSUB - 1)
    got_values, got_index = opened(got[NS])
    got_index = jnp.where(ends, -1.0, got_index)
    values, index = opened(spill_out[0])
    for s in range(NS):
        alive = jnp.where(counts[0] > s, 1.0, 0.0)
        p = (part[s] + jnp.where(got_index == s, got_values, 0.0)) * alive
        p_ref[s] = p
        own_ref[s] = p.astype(BF16)
        outer_ref[s] = (got[s].astype(F32) + jnp.where(index == s, values, 0.0)).astype(BF16)
    marks_ref[...] = jnp.concatenate([spill_in[0][WP - 8 :].astype(F32)[4:5]] * 4 + [got_index] * 4, axis=0)


def system_kernel(first, place, counts, neighbours, ca, cb, p, own, outer, inner, marks, v0, *rest):
    if first:
        w_ref, win_ref, wout_ref, sums_ref, u = rest
    else:
        w, sums_ref, u = rest
    here = place[0]
    odd = here % 2 == 1
    for s in range(NS):
        u[s] = outer[s]
        u[NS + s] = own[s]
        u[2 * NS + s] = inner[s]
    zero = jnp.zeros((1, R), F32)
    sums = [zero] * 3
    for s in range(NS):
        acc = jnp.zeros((WP, R), F32)
        for k in range(NB):
            slot = jnp.clip(neighbours[s, k] - NS * (here - 1), 0, 3 * NS - 1)
            slot = jnp.where(odd, slot + 2 * NS * (1 - slot // NS), slot)
            c_ref = ca if k < NB // 2 else cb
            acc += jnp.dot(c_ref[s * (NB // 2) + k % (NB // 2)], u[slot], preferred_element_type=F32)
        alive = jnp.where(counts[0] > s, 1.0, 0.0)
        image = (p[s] + acc) * alive
        start = v0[s]
        if first:
            image = image - SHIFT * start
            w_ref[s] = image
            terms = (start * start, start * image, image * image)
        else:
            terms = (start * image, w[s] * image, image * image)
        sums = [t + jnp.sum(x, axis=0, keepdims=True) for t, x in zip(sums, terms)]
    if first:
        for ref, index in ((win_ref, marks[0:1, :]), (wout_ref, marks[4:5, :])):
            chosen = jnp.zeros((WP, R), F32)
            for s in range(NS):
                chosen = chosen + jnp.where(index == s, w_ref[s], 0.0)
            ref[0] = chosen.astype(BF16)
    sums_ref[...] = jnp.concatenate(sums + [zero] * 5, axis=0)


def finish_kernel(gathered, p0, q, out):
    total = jnp.sum(gathered[...], axis=0)
    s00, s01, s11, s02, s12, s22 = (total[i : i + 1, :] for i in range(6))
    c = SHIFT
    bb = s00 + EPS
    beta = jnp.sqrt(bb)
    h11 = (s01 + c * s00) / bb
    a = c - h11
    n2 = (s11 + 2 * a * s01 + a * a * s00) / bb
    h21s = jnp.maximum(n2, 0.0) + EPS
    h21 = jnp.sqrt(h21s)
    full = bb * h21s
    v0i = s01 + c * s00
    h12 = (s02 + a * v0i) / (bb * h21)
    cross = (s01 + a * s00) / (bb * h21)
    b2i = (s12 + a * s02 + a * (s11 + c * s01) + a * a * v0i) / full
    h22 = b2i - h12 * cross
    ii = (s22 + 2 * a * (s12 + c * s02) + a * a * (s11 + 2 * c * s01 + c * c * s00)) / full
    rest = (
        ii + h12 * h12 * (s00 / bb) + h22 * h22 * (n2 / h21s)
        - 2 * h12 * h12 - 2 * h22 * b2i + 2 * h12 * h22 * cross
    )
    h32s = jnp.maximum(rest, 0.0) + EPS
    g00 = h11 * h11 + h21s
    g01 = h11 * h12 + h21 * h22
    g11 = h12 * h12 + h22 * h22 + h32s
    det = g00 * g11 - g01 * g01
    y1 = beta * (g11 * h11 - g01 * h12) / det
    y2 = beta * (g00 * h12 - g01 * h11) / det
    two = y2 / (beta * h21)
    one = y1 / beta + a * two
    for s in range(NS):
        out[pl.ds(s, W, stride=NS), :] = one * p0[s, :W, :] + two * q[s, :W, :]


def to_inner(x):
    return lax.ppermute(x, "sub", [(i, i ^ 1) for i in range(NSUB)])


def to_outer(x):
    return lax.ppermute(x, "sub", [(i, (((i + 1) ^ 1) - 1) % NSUB) for i in range(NSUB)])


def body(right_side, coupling, neighbours, inverse, margin, counts):
    here = lax.axis_index("sub").astype(jnp.int32).reshape(1)
    flat_right = right_side.transpose(1, 0, 2).reshape(W * NS, R)
    block, one = (NS, WP, R), (1, WP, R)
    v0, v0b = call(start_kernel, [(block, F32), (block, BF16)], [SM, VM])(counts, flat_right)
    outer, inner = to_outer(v0b), to_inner(v0b)

    def matrices(half, *more):
        lanes = GROUP * W
        outs = [((NS * NB // 2, WP, WP), BF16, True)]
        if half == 0:
            outs.append(((6 * W, 6 * W), BF16, True))
        return call(
            functools.partial(coupling_kernel, half),
            outs,
            [ANY, ANY],
            [
                pltpu.VMEM((NS, GROUPS * lanes), BF16),
                pltpu.VMEM((2 * NS, lanes), F32),
                pltpu.VMEM((GROUPS * GROUP * NS, 128), F32),
                pltpu.VMEM((GROUPS * GROUP * NS, 128), F32),
                pltpu.SemaphoreType.DMA((CHUNKS + 1,)),
            ],
            limit=24,
            cost=pl.CostEstimate(flops=1 << 20, bytes_accessed=12 << 20, transcendentals=0),
        )(coupling, *more)

    first_half, held = matrices(0, inverse)
    held = pltpu.with_memory_space_constraint(held, pltpu.VMEM)
    first_half = pltpu.with_memory_space_constraint(first_half, pltpu.VMEM)

    def solve(own, inner, outer):
        return call(
            solve_kernel,
            [(block, F32), (one, BF16), (one, BF16)],
            [SM, SM, VM, VM, VM, VM],
            [pltpu.VMEM((6 * W, R), F32)] * 2,
        )(here, margin, held, own, inner, outer)

    def joined(out, spill_in, spill_out):
        got_in = to_inner(spill_in)
        part, sent = call(inner_kernel, [(block, F32), ((NS + 1, WP, R), BF16)], [VM] * 3)(
            out, got_in, spill_out
        )
        got = to_outer(sent)
        p, own, outer, marks = call(
            outer_kernel,
            [(block, F32), (block, BF16), (block, BF16), ((8, R), F32)],
            [SM, SM] + [VM] * 4,
        )(here, counts, part, got, got_in, spill_out)
        return sent, p, own, outer, to_inner(own), marks

    def system(first, halves, p, own, outer, inner, marks, *more):
        outs = [(block, F32), (one, BF16), (one, BF16)] if first else []
        return call(
            functools.partial(system_kernel, first),
            outs + [((8, R), F32)],
            [SM, SM, SM] + [VM] * (7 + len(more)),
            [pltpu.VMEM((3 * NS, WP, R), BF16)],
        )(here, counts, neighbours, *halves, p, own, outer, inner, marks, *more)

    sent, p0, *rest = joined(*solve(v0, inner, outer))
    (second_half,) = matrices(1, sent)
    second_half = pltpu.with_memory_space_constraint(second_half, pltpu.VMEM)
    halves = first_half, second_half
    w, w_in, w_out, sums_one = system(True, halves, p0, *rest, v0)
    _, q, *rest = joined(*solve(w, to_inner(w_in), to_outer(w_out)))
    (sums_two,) = system(False, halves, q, *rest, v0, w)
    sums = jnp.concatenate([sums_one[:3], sums_two[:3]], axis=0)
    sums = sums + to_inner(sums)
    gathered = lax.all_to_all(
        jnp.broadcast_to(sums[None], (NSUB // 2, 6, R)), "sub", 0, 0,
        axis_index_groups=[list(range(c, NSUB, 2)) for c in range(2)],
    )
    (flat,) = call(finish_kernel, [((W * NS, R), F32)], [VM] * 3)(gathered, p0, q)
    return flat.reshape(W, NS, R).transpose(1, 0, 2)


def solution(mesh):
    placed = (
        P("sub", None, "rhs"),
        P("sub", None),
        P("sub", None),
        P("sub", None, None),
        P("sub", None),
        P("sub"),
    )
    return jax.shard_map(
        body, mesh=mesh, in_specs=placed, out_specs=P("sub", None, "rhs"), check_vma=False
    )
```

```python
import functools
import jax
import jax.numpy as jnp
from jax import lax
from jax.experimental import pallas as pl
from jax.experimental.pallas import tpu as pltpu
from jax.sharding import PartitionSpec as P

EPS = 1e-06
W = 252
WP = 256
NS = 4
NB = 8
R = 128
NSUB = 64
SHIFT = 1.0
ROWS = NB * W
GROUP = 32
F32 = jnp.float32
BF16 = jnp.bfloat16
CHUNK = 8
SPLIT = 2
OWN = 1024
FROM = 896
ANY = pl.BlockSpec(memory_space=pl.ANY)
VM = pl.BlockSpec(memory_space=pltpu.VMEM)
SM = pl.BlockSpec(memory_space=pltpu.SMEM)


def call(kernel, outs, ins, scratch=(), limit=24, cost=None):
    return pl.pallas_call(
        kernel,
        out_shape=[pltpu.VMEM(s, d) if keep else jax.ShapeDtypeStruct(s, d) for s, d, *keep in outs],
        in_specs=ins,
        out_specs=[VM] * len(outs),
        scratch_shapes=list(scratch),
        compiler_params=pltpu.CompilerParams(vmem_limit_bytes=limit << 20),
        cost_estimate=cost,
    )


def start_kernel(counts, right, v0_ref, v0b_ref):
    for s in range(NS):
        alive = jnp.where(counts[0] > s, 1.0, 0.0)
        v0_ref[s, :W, :] = right[pl.ds(s, W, stride=NS), :] * alive
        v0_ref[s, W:, :] = jnp.zeros((WP - W, R), F32)
        v0b_ref[s] = v0_ref[s].astype(BF16)


def coupling_kernel(blocks, groups, first, flat, *rest):
    if first:
        inverse, c_ref, inverse_ref, raw, x, lo, hi, sems = rest
    else:
        _, c_ref, raw, x, lo, hi, sems = rest
    lanes = GROUP * W
    count = groups[1] - groups[0]
    step = CHUNK * lanes
    chunks = count // CHUNK
    copies = [
        pltpu.make_async_copy(
            flat.at[:, pl.ds(groups[0] * lanes + c * step, step)],
            raw.at[:, pl.ds(c * step, step)],
            sems.at[c],
        )
        for c in range(chunks)
    ]
    if first:
        copies.append(pltpu.make_async_copy(inverse.at[0], inverse_ref, sems.at[chunks]))
    for copy in copies:
        copy.start()
    lane = lax.broadcasted_iota(jnp.int32, (8, 128), 1)

    def pair(i, carry):
        for h in range(2):
            at = pl.multiple_of((2 * i + h) * lanes, 128)
            x[4 * h : 4 * h + 4, :] = raw[:, pl.ds(at, lanes)].astype(F32)
        base = pl.multiple_of(2 * i * (GROUP * NS), 8)
        for s in range(GROUP):
            def rolled(t):
                piece = x[:, 128 * t : 128 * t + 128]
                return pltpu.roll(piece, 4 * s, 1) if s else piece

            middle = rolled(2 * s)
            if s == 0:
                left, right = middle, rolled(1)
            else:
                early = lane < 4 * s
                left = jnp.where(early, rolled(2 * s - 1), middle)
                right = jnp.where(early, middle, rolled(2 * s + 1)) if s < GROUP - 1 else middle
            for h in range(2):
                at = base + (h * GROUP + s) * NS
                lo[pl.ds(at, NS), :] = left[4 * h : 4 * h + 4]
                hi[pl.ds(at, NS), :] = right[4 * h : 4 * h + 4]
        return carry

    for c in range(chunks):
        copies[c].wait()
        lax.fori_loop(c * CHUNK // 2, (c + 1) * CHUNK // 2, pair, 0)
    keep = lax.broadcasted_iota(jnp.int32, (WP, 128), 1) < W - 128
    pad = jnp.zeros((WP - W, 128), F32)
    skip = (blocks[0] * W - groups[0] * GROUP) * NS
    number = blocks[1] - blocks[0]

    def place(k, carry):
        for p in range(NS):
            row = skip + k * (W * NS) + p
            left = lo[pl.ds(row, W, stride=NS), :]
            right = hi[pl.ds(row, W, stride=NS), :]
            right = jnp.where(keep, jnp.concatenate([right, pad], axis=0), 0.0)
            c_ref[p * number + k, :, :128] = jnp.concatenate([left, pad], axis=0).astype(BF16)
            c_ref[p * number + k, :, 128:] = right.astype(BF16)
        return carry

    lax.fori_loop(0, number, place, 0)
    if first:
        copies[chunks].wait()


def own_kernel(inverse, own, part_ref, ext):
    for s in range(NS):
        ext[s * W : (s + 1) * W, :] = own[s, :W, :]
    ext[NS * W :, :] = jnp.zeros((OWN - NS * W, R), F32)
    part_ref[...] = jnp.dot(inverse[:, :OWN], ext[...].astype(BF16), preferred_element_type=F32)


def places(place, margin):
    here = place[0]
    low = jnp.clip(margin[0, 0] - NS * jnp.maximum(here - 1, 0), 0, NS - 1)
    high = jnp.clip(margin[0, 1] - NS * jnp.minimum(here + 1, NSUB - 1), 0, NS - 1)
    return here % 2 == 0, here == 0, here == NSUB - 1, low, high


def spilled(inverse, part, ext, block, index):
    begin = block * W // 16 * 16
    end = -(-(block + 1) * W // 16) * 16
    end = min(end, 6 * W)
    rows = jnp.dot(inverse[begin:end, FROM:], ext, preferred_element_type=F32)
    rows = rows[block * W - begin : (block + 1) * W - begin] + part[block * W : (block + 1) * W, :]
    mark = jnp.ones((WP - W, R), F32) * index.astype(F32)
    return jnp.concatenate([rows, mark], axis=0)


def margin_kernel(place, margin, inverse, part, own, inner, outer, in_ref, ext_ref, ext):
    even, first, last, low, high = places(place, margin)
    odd = jnp.logical_not(even)
    ext[: NS * W - FROM, :] = jnp.zeros((NS * W - FROM, R), F32)
    some = inner.shape[0] > 1

    def put(when, block, source, index):
        @pl.when(when)
        def _():
            ext[block * W - FROM : (block + 1) * W - FROM, :] = source[index].astype(F32)[:W]

    put(first, NS, own, low)
    put(jnp.logical_and(even, jnp.logical_not(first)), NS, outer, low if some else 0)
    put(odd, NS, inner, low if some else 0)
    put(last, NS + 1, own, high)
    put(jnp.logical_and(odd, jnp.logical_not(last)), NS + 1, outer, high if some else 0)
    put(even, NS + 1, inner, high if some else 0)
    ext_ref[...] = ext[...].astype(BF16)

    @pl.when(even)
    def _():
        in_ref[0] = spilled(inverse, part, ext_ref[...], NS + 1, high).astype(BF16)

    @pl.when(odd)
    def _():
        in_ref[0] = spilled(inverse, part, ext_ref[...], NS, low).astype(BF16)


def solve_kernel(place, margin, inverse, part, ext, out_ref, out2_ref, res):
    even, first, last, low, high = places(place, margin)
    mine = NS * W
    res[...] = part[:mine, :] + jnp.dot(inverse[:mine, FROM:], ext[...], preferred_element_type=F32)
    pad = jnp.zeros((WP - W, R), F32)
    for s in range(NS):
        out_ref[s] = jnp.concatenate([res[s * W : (s + 1) * W, :], pad], axis=0)
    keep = lax.broadcasted_iota(jnp.int32, (WP, R), 0) < W

    def spill(when, ends, block, index):
        @pl.when(when)
        def _():
            rows = spilled(inverse, part, ext[...], block, index)
            out2_ref[0] = rows.astype(BF16)

            @pl.when(ends)
            def _():
                out_ref[index] += jnp.where(keep, rows, 0.0)

    spill(even, first, NS, low)
    spill(jnp.logical_not(even), last, NS + 1, high)


def opened(block):
    x = block.astype(F32)
    rows = lax.broadcasted_iota(jnp.int32, x.shape, 0)
    return jnp.where(rows < W, x, 0.0), x[W : W + 1, :]


def inner_kernel(out, spill_in, spill_out, part_ref, sent_ref):
    values, index = opened(spill_in[0])
    for s in range(NS):
        part = out[s] + jnp.where(index == s, values, 0.0)
        part_ref[s] = part
        sent_ref[s] = part.astype(BF16)
    sent_ref[NS] = spill_out[0]


def outer_kernel(place, counts, part, got, spill_in, spill_out, *rest):
    p_ref, own_ref, outer_ref, marks_ref = rest[-4:]
    here = place[0]
    ends = jnp.logical_or(here == 0, here == NSUB - 1)
    got_values, got_index = opened(got[NS])
    got_index = jnp.where(ends, -1.0, got_index)
    values, index = opened(spill_out[0])
    for s in range(NS):
        alive = jnp.where(counts[0] > s, 1.0, 0.0)
        p = (part[s] + jnp.where(got_index == s, got_values, 0.0)) * alive
        p_ref[s] = p
        own_ref[s] = p.astype(BF16)
        outer_ref[s] = (got[s].astype(F32) + jnp.where(index == s, values, 0.0)).astype(BF16)
    marks_ref[...] = jnp.concatenate([spill_in[0][WP - 8 :].astype(F32)[4:5]] * 4 + [got_index] * 4, axis=0)


def system_kernel(first, place, counts, neighbours, ca, cb, p, own, outer, inner, marks, v0, *rest):
    if first:
        w_ref, win_ref, wout_ref, sums_ref, u = rest
    else:
        w, sums_ref, u = rest
    here = place[0]
    odd = here % 2 == 1
    for s in range(NS):
        u[s] = outer[s]
        u[NS + s] = own[s]
        u[2 * NS + s] = inner[s]
    zero = jnp.zeros((1, R), F32)
    sums = [zero] * 3
    for s in range(NS):
        acc = jnp.zeros((WP, R), F32)
        for k in range(NB):
            slot = jnp.clip(neighbours[s, k] - NS * (here - 1), 0, 3 * NS - 1)
            slot = jnp.where(odd, slot + 2 * NS * (1 - slot // NS), slot)
            matrix = ca[s * SPLIT + k] if k < SPLIT else cb[s * (NB - SPLIT) + k - SPLIT]
            acc += jnp.dot(matrix, u[slot], preferred_element_type=F32)
        alive = jnp.where(counts[0] > s, 1.0, 0.0)
        image = (p[s] + acc) * alive
        start = v0[s]
        if first:
            image = image - SHIFT * start
            w_ref[s] = image
            terms = (start * start, start * image, image * image)
        else:
            terms = (start * image, w[s] * image, image * image)
        sums = [t + jnp.sum(x, axis=0, keepdims=True) for t, x in zip(sums, terms)]
    if first:
        for ref, index in ((win_ref, marks[0:1, :]), (wout_ref, marks[4:5, :])):
            chosen = jnp.zeros((WP, R), F32)
            for s in range(NS):
                chosen = chosen + jnp.where(index == s, w_ref[s], 0.0)
            ref[0] = chosen.astype(BF16)
    sums_ref[...] = jnp.concatenate(sums + [zero] * 5, axis=0)


def finish_kernel(gathered, p0, q, out):
    total = jnp.sum(gathered[...], axis=0)
    s00, s01, s11, s02, s12, s22 = (total[i : i + 1, :] for i in range(6))
    c = SHIFT
    bb = s00 + EPS
    beta = jnp.sqrt(bb)
    h11 = (s01 + c * s00) / bb
    a = c - h11
    n2 = (s11 + 2 * a * s01 + a * a * s00) / bb
    h21s = jnp.maximum(n2, 0.0) + EPS
    h21 = jnp.sqrt(h21s)
    full = bb * h21s
    v0i = s01 + c * s00
    h12 = (s02 + a * v0i) / (bb * h21)
    cross = (s01 + a * s00) / (bb * h21)
    b2i = (s12 + a * s02 + a * (s11 + c * s01) + a * a * v0i) / full
    h22 = b2i - h12 * cross
    ii = (s22 + 2 * a * (s12 + c * s02) + a * a * (s11 + 2 * c * s01 + c * c * s00)) / full
    rest = (
        ii + h12 * h12 * (s00 / bb) + h22 * h22 * (n2 / h21s)
        - 2 * h12 * h12 - 2 * h22 * b2i + 2 * h12 * h22 * cross
    )
    h32s = jnp.maximum(rest, 0.0) + EPS
    g00 = h11 * h11 + h21s
    g01 = h11 * h12 + h21 * h22
    g11 = h12 * h12 + h22 * h22 + h32s
    det = g00 * g11 - g01 * g01
    y1 = beta * (g11 * h11 - g01 * h12) / det
    y2 = beta * (g00 * h12 - g01 * h11) / det
    two = y2 / (beta * h21)
    one = y1 / beta + a * two
    for s in range(NS):
        out[pl.ds(s, W, stride=NS), :] = one * p0[s, :W, :] + two * q[s, :W, :]


def to_inner(x):
    return lax.ppermute(x, "sub", [(i, i ^ 1) for i in range(NSUB)])


def to_outer(x):
    return lax.ppermute(x, "sub", [(i, (((i + 1) ^ 1) - 1) % NSUB) for i in range(NSUB)])


def body(right_side, coupling, neighbours, inverse, margin, counts):
    here = lax.axis_index("sub").astype(jnp.int32).reshape(1)
    flat_right = right_side.transpose(1, 0, 2).reshape(W * NS, R)
    block, one = (NS, WP, R), (1, WP, R)
    v0, v0b = call(start_kernel, [(block, F32), (block, BF16)], [SM, VM])(counts, flat_right)
    outer, inner = to_outer(v0b), to_inner(v0b)

    coupling = pltpu.with_memory_space_constraint(coupling, pltpu.HBM)
    inverse = pltpu.with_memory_space_constraint(inverse, pltpu.HBM)

    def matrices(first, more):
        lanes = GROUP * W
        blocks = (0, SPLIT) if first else (SPLIT, NB)
        begin = blocks[0] * W // GROUP
        end = -(-blocks[1] * W // GROUP)
        count = -(-(end - begin) // CHUNK) * CHUNK
        groups = (begin, begin + count) if first else (end - count, end)
        outs = [((NS * (blocks[1] - blocks[0]), WP, WP), BF16, True)]
        if first:
            outs.append(((6 * W, 6 * W), BF16, True))
        return call(
            functools.partial(coupling_kernel, blocks, groups, first),
            outs,
            [ANY, ANY],
            [
                pltpu.VMEM((NS, count * lanes), BF16),
                pltpu.VMEM((2 * NS, lanes), F32),
                pltpu.VMEM((count * GROUP * NS, 128), F32),
                pltpu.VMEM((count * GROUP * NS, 128), F32),
                pltpu.SemaphoreType.DMA((count // CHUNK + 1,)),
            ],
            limit=24,
            cost=pl.CostEstimate(flops=1 << 20, bytes_accessed=12 << 20, transcendentals=0),
        )(coupling, more)

    first_part, held = matrices(True, inverse)
    held = pltpu.with_memory_space_constraint(held, pltpu.VMEM)
    first_part = pltpu.with_memory_space_constraint(first_part, pltpu.VMEM)

    def solve(own, inner, outer):
        (part,) = call(
            own_kernel, [((6 * W, R), F32, True)], [VM, VM], [pltpu.VMEM((OWN, R), F32)],
            cost=pl.CostEstimate(flops=1 << 30, bytes_accessed=4 << 20, transcendentals=0),
        )(held, own)
        depth = 6 * W - FROM
        spill_in, ext = call(
            margin_kernel,
            [(one, BF16), ((depth, R), BF16)],
            [SM, SM] + [VM] * 5,
            [pltpu.VMEM((depth, R), F32)],
        )(here, margin, held, part, own, inner, outer)
        got_in = to_inner(spill_in)
        out, spill_out = call(
            solve_kernel,
            [(block, F32), (one, BF16)],
            [SM, SM] + [VM] * 3,
            [pltpu.VMEM((NS * W, R), F32)],
            cost=pl.CostEstimate(flops=1 << 30, bytes_accessed=4 << 20, transcendentals=0),
        )(here, margin, held, part, ext)
        return out, got_in, spill_out

    def joined(out, got_in, spill_out, meanwhile=None):
        part, sent = call(inner_kernel, [(block, F32), ((NS + 1, WP, R), BF16)], [VM] * 3)(
            out, got_in, spill_out
        )
        got = to_outer(sent)
        done = meanwhile(sent) if meanwhile else []
        p, own, outer, marks = call(
            outer_kernel,
            [(block, F32), (block, BF16), (block, BF16), ((8, R), F32)],
            [SM, SM] + [VM] * 4 + [ANY] * len(done),
        )(here, counts, part, got, got_in, spill_out, *done)
        return done, p, own, outer, to_inner(own), marks

    def system(first, halves, p, own, outer, inner, marks, *more):
        outs = [(block, F32), (one, BF16), (one, BF16)] if first else []
        return call(
            functools.partial(system_kernel, first),
            outs + [((8, R), F32)],
            [SM, SM, SM] + [VM] * (7 + len(more)),
            [pltpu.VMEM((3 * NS, WP, R), BF16)],
        )(here, counts, neighbours, *halves, p, own, outer, inner, marks, *more)

    def second(sent):
        (made,) = matrices(False, sent)
        return [pltpu.with_memory_space_constraint(made, pltpu.VMEM)]

    (second_part,), p0, *rest = joined(*solve(v0, inner, outer), second)
    halves = first_part, second_part
    w, w_in, w_out, sums_one = system(True, halves, p0, *rest, v0)
    _, q, *rest = joined(*solve(w, to_inner(w_in), to_outer(w_out)))
    (sums_two,) = system(False, halves, q, *rest, v0, w)
    sums = jnp.concatenate([sums_one[:3], sums_two[:3]], axis=0)
    sums = sums + to_inner(sums)
    gathered = lax.all_to_all(
        jnp.broadcast_to(sums[None], (NSUB // 2, 6, R)), "sub", 0, 0,
        axis_index_groups=[list(range(c, NSUB, 2)) for c in range(2)],
    )
    (flat,) = call(finish_kernel, [((W * NS, R), F32)], [VM] * 3)(gathered, p0, q)
    return flat.reshape(W, NS, R).transpose(1, 0, 2)


def solution(mesh):
    placed = (
        P("sub", None, "rhs"),
        P("sub", None),
        P("sub", None),
        P("sub", None, None),
        P("sub", None),
        P("sub"),
    )
    return jax.shard_map(
        body, mesh=mesh, in_specs=placed, out_specs=P("sub", None, "rhs"), check_vma=False
    )
```

```python
import functools
import jax
import jax.numpy as jnp
from jax import lax
from jax.experimental import pallas as pl
from jax.experimental.pallas import tpu as pltpu
from jax.sharding import PartitionSpec as P

EPS = 1e-06
W = 252
WP = 256
NS = 4
NB = 8
R = 128
NSUB = 64
SHIFT = 1.0
ROWS = NB * W
GROUP = 32
F32 = jnp.float32
BF16 = jnp.bfloat16
CHUNK = 8
SPLIT = 2
OWN = 1024
FROM = 896
ANY = pl.BlockSpec(memory_space=pl.ANY)
VM = pl.BlockSpec(memory_space=pltpu.VMEM)
SM = pl.BlockSpec(memory_space=pltpu.SMEM)


def call(kernel, outs, ins, scratch=(), limit=24, cost=None):
    return pl.pallas_call(
        kernel,
        out_shape=[pltpu.VMEM(s, d) if keep else jax.ShapeDtypeStruct(s, d) for s, d, *keep in outs],
        in_specs=ins,
        out_specs=[VM] * len(outs),
        scratch_shapes=list(scratch),
        compiler_params=pltpu.CompilerParams(vmem_limit_bytes=limit << 20),
        cost_estimate=cost,
    )


def start_kernel(counts, right, v0_ref, v0b_ref):
    for s in range(NS):
        alive = jnp.where(counts[0] > s, 1.0, 0.0)
        v0_ref[s, :W, :] = right[pl.ds(s, W, stride=NS), :] * alive
        v0_ref[s, W:, :] = jnp.zeros((WP - W, R), F32)
        v0b_ref[s] = v0_ref[s].astype(BF16)


def coupling_kernel(blocks, groups, first, flat, *rest):
    if first:
        inverse, c_ref, inverse_ref, raw, x, lo, hi, sems = rest
    else:
        _, c_ref, raw, x, lo, hi, sems = rest
    lanes = GROUP * W
    count = groups[1] - groups[0]
    step = CHUNK * lanes
    chunks = count // CHUNK
    copies = [
        pltpu.make_async_copy(
            flat.at[:, pl.ds(groups[0] * lanes + c * step, step)],
            raw.at[:, pl.ds(c * step, step)],
            sems.at[c],
        )
        for c in range(chunks)
    ]
    if first:
        copies.append(pltpu.make_async_copy(inverse.at[0], inverse_ref, sems.at[chunks]))
    for copy in copies:
        copy.start()
    lane = lax.broadcasted_iota(jnp.int32, (8, 128), 1)

    def pair(i, carry):
        for h in range(2):
            at = pl.multiple_of((2 * i + h) * lanes, 128)
            x[4 * h : 4 * h + 4, :] = raw[:, pl.ds(at, lanes)].astype(F32)
        base = pl.multiple_of(2 * i * (GROUP * NS), 8)
        for s in range(GROUP):
            def rolled(t):
                piece = x[:, 128 * t : 128 * t + 128]
                return pltpu.roll(piece, 4 * s, 1) if s else piece

            middle = rolled(2 * s)
            if s == 0:
                left, right = middle, rolled(1)
            else:
                early = lane < 4 * s
                left = jnp.where(early, rolled(2 * s - 1), middle)
                right = jnp.where(early, middle, rolled(2 * s + 1)) if s < GROUP - 1 else middle
            for h in range(2):
                at = base + (h * GROUP + s) * NS
                lo[pl.ds(at, NS), :] = left[4 * h : 4 * h + 4]
                hi[pl.ds(at, NS), :] = right[4 * h : 4 * h + 4]
        return carry

    for c in range(chunks):
        copies[c].wait()
        lax.fori_loop(c * CHUNK // 2, (c + 1) * CHUNK // 2, pair, 0)
    keep = lax.broadcasted_iota(jnp.int32, (WP, 128), 1) < W - 128
    pad = jnp.zeros((WP - W, 128), F32)
    skip = (blocks[0] * W - groups[0] * GROUP) * NS
    number = blocks[1] - blocks[0]

    def place(k, carry):
        for p in range(NS):
            row = skip + k * (W * NS) + p
            left = lo[pl.ds(row, W, stride=NS), :]
            right = hi[pl.ds(row, W, stride=NS), :]
            right = jnp.where(keep, jnp.concatenate([right, pad], axis=0), 0.0)
            c_ref[p * number + k, :, :128] = jnp.concatenate([left, pad], axis=0).astype(BF16)
            c_ref[p * number + k, :, 128:] = right.astype(BF16)
        return carry

    lax.fori_loop(0, number, place, 0)
    if first:
        copies[chunks].wait()


def own_kernel(inverse, own, part_ref, ext):
    for s in range(NS):
        ext[s * W : (s + 1) * W, :] = own[s, :W, :]
    ext[NS * W :, :] = jnp.zeros((OWN - NS * W, R), F32)
    part_ref[...] = jnp.dot(inverse[:, :OWN], ext[...].astype(BF16), preferred_element_type=F32)


def places(place, margin):
    here = place[0]
    low = jnp.clip(margin[0, 0] - NS * jnp.maximum(here - 1, 0), 0, NS - 1)
    high = jnp.clip(margin[0, 1] - NS * jnp.minimum(here + 1, NSUB - 1), 0, NS - 1)
    return here % 2 == 0, here == 0, here == NSUB - 1, low, high


def spilled(inverse, part, ext, block, index):
    begin = block * W // 16 * 16
    end = -(-(block + 1) * W // 16) * 16
    end = min(end, 6 * W)
    rows = jnp.dot(inverse[begin:end, FROM:], ext, preferred_element_type=F32)
    rows = rows[block * W - begin : (block + 1) * W - begin] + part[block * W : (block + 1) * W, :]
    mark = jnp.ones((WP - W, R), F32) * index.astype(F32)
    return jnp.concatenate([rows, mark], axis=0)


def margin_kernel(place, margin, inverse, part, own, inner, outer, in_ref, ext_ref, ext):
    even, first, last, low, high = places(place, margin)
    odd = jnp.logical_not(even)
    ext[: NS * W - FROM, :] = jnp.zeros((NS * W - FROM, R), F32)
    some = inner.shape[0] > 1

    def put(when, block, source, index):
        @pl.when(when)
        def _():
            ext[block * W - FROM : (block + 1) * W - FROM, :] = source[index].astype(F32)[:W]

    put(first, NS, own, low)
    put(jnp.logical_and(even, jnp.logical_not(first)), NS, outer, low if some else 0)
    put(odd, NS, inner, low if some else 0)
    put(last, NS + 1, own, high)
    put(jnp.logical_and(odd, jnp.logical_not(last)), NS + 1, outer, high if some else 0)
    put(even, NS + 1, inner, high if some else 0)
    ext_ref[...] = ext[...].astype(BF16)

    @pl.when(even)
    def _():
        in_ref[0] = spilled(inverse, part, ext_ref[...], NS + 1, high).astype(BF16)

    @pl.when(odd)
    def _():
        in_ref[0] = spilled(inverse, part, ext_ref[...], NS, low).astype(BF16)


def solve_kernel(place, margin, inverse, part, ext, out_ref, out2_ref, res):
    even, first, last, low, high = places(place, margin)
    mine = NS * W
    res[...] = part[:mine, :] + jnp.dot(inverse[:mine, FROM:], ext[...], preferred_element_type=F32)
    pad = jnp.zeros((WP - W, R), F32)
    for s in range(NS):
        out_ref[s] = jnp.concatenate([res[s * W : (s + 1) * W, :], pad], axis=0)
    keep = lax.broadcasted_iota(jnp.int32, (WP, R), 0) < W

    def spill(when, ends, block, index):
        @pl.when(when)
        def _():
            rows = spilled(inverse, part, ext[...], block, index)
            out2_ref[0] = rows.astype(BF16)

            @pl.when(ends)
            def _():
                out_ref[index] += jnp.where(keep, rows, 0.0)

    spill(even, first, NS, low)
    spill(jnp.logical_not(even), last, NS + 1, high)


def opened(block):
    x = block.astype(F32)
    rows = lax.broadcasted_iota(jnp.int32, x.shape, 0)
    return jnp.where(rows < W, x, 0.0), x[W : W + 1, :]


def inner_kernel(out, spill_in, spill_out, part_ref, sent_ref, near_ref):
    values, index = opened(spill_in[0])
    for s in range(NS):
        part = out[s] + jnp.where(index == s, values, 0.0)
        part_ref[s] = part
        sent_ref[s] = part.astype(BF16)
        near_ref[s] = part.astype(BF16)
    sent_ref[NS] = spill_out[0]


def system_kernel(
    first, place, counts, neighbours, ca, cb, part, got, near, far, spill_in, spill_out, v0, *rest
):
    if first:
        p_ref, w_ref, win_ref, wout_ref, sums_ref, u = rest
    else:
        w, p_ref, sums_ref, u = rest
    here = place[0]
    odd = here % 2 == 1
    ends = jnp.logical_or(here == 0, here == NSUB - 1)
    got_values, got_index = opened(got[NS])
    got_index = jnp.where(ends, -1.0, got_index)
    far_values, far_index = opened(far[0])
    far_index = jnp.where(jnp.logical_or(here == 1, here == NSUB - 2), -1.0, far_index)
    values, index = opened(spill_out[0])
    for s in range(NS):
        alive = jnp.where(counts[0] > s, 1.0, 0.0)
        p = (part[s] + jnp.where(got_index == s, got_values, 0.0)) * alive
        p_ref[s] = p
        u[s] = (got[s].astype(F32) + jnp.where(index == s, values, 0.0)).astype(BF16)
        u[NS + s] = p.astype(BF16)
        u[2 * NS + s] = (near[s].astype(F32) + jnp.where(far_index == s, far_values, 0.0)).astype(BF16)
    sums_ref[...] = jnp.zeros((8, R), F32)
    if first:
        w_ref[...] = jnp.zeros((NS, WP, R), F32)

    def one(s):
        acc = p_ref[s]
        for k in range(NB):
            slot = jnp.clip(neighbours[s, k] - NS * (here - 1), 0, 3 * NS - 1)
            slot = jnp.where(odd, slot + 2 * NS * (1 - slot // NS), slot)
            matrix = ca[s * SPLIT + k] if k < SPLIT else cb[s * (NB - SPLIT) + k - SPLIT]
            acc += jnp.dot(matrix, u[slot], preferred_element_type=F32)
        image = acc
        start = v0[s]
        if first:
            image = image - SHIFT * start
            w_ref[s] = image
            terms = (start * start, start * image, image * image)
        else:
            terms = (start * image, w[s] * image, image * image)
        sums = [jnp.sum(x, axis=0, keepdims=True) for x in terms]
        sums_ref[...] += jnp.concatenate(sums + [jnp.zeros((5, R), F32)], axis=0)

    for s in range(NS):
        pl.when(counts[0] > s)(functools.partial(one, s))
    if first:
        wanted = opened(spill_in[0])[1]
        for ref, index in ((win_ref, wanted), (wout_ref, got_index)):
            chosen = jnp.zeros((WP, R), F32)
            for s in range(NS):
                chosen = chosen + jnp.where(index == s, w_ref[s], 0.0)
            ref[0] = chosen.astype(BF16)


def finish_kernel(gathered, p0, q, out):
    total = jnp.sum(gathered[...], axis=0)
    s00, s01, s11, s02, s12, s22 = (total[i : i + 1, :] for i in range(6))
    c = SHIFT
    bb = s00 + EPS
    beta = jnp.sqrt(bb)
    h11 = (s01 + c * s00) / bb
    a = c - h11
    n2 = (s11 + 2 * a * s01 + a * a * s00) / bb
    h21s = jnp.maximum(n2, 0.0) + EPS
    h21 = jnp.sqrt(h21s)
    full = bb * h21s
    v0i = s01 + c * s00
    h12 = (s02 + a * v0i) / (bb * h21)
    cross = (s01 + a * s00) / (bb * h21)
    b2i = (s12 + a * s02 + a * (s11 + c * s01) + a * a * v0i) / full
    h22 = b2i - h12 * cross
    ii = (s22 + 2 * a * (s12 + c * s02) + a * a * (s11 + 2 * c * s01 + c * c * s00)) / full
    rest = (
        ii + h12 * h12 * (s00 / bb) + h22 * h22 * (n2 / h21s)
        - 2 * h12 * h12 - 2 * h22 * b2i + 2 * h12 * h22 * cross
    )
    h32s = jnp.maximum(rest, 0.0) + EPS
    g00 = h11 * h11 + h21s
    g01 = h11 * h12 + h21 * h22
    g11 = h12 * h12 + h22 * h22 + h32s
    det = g00 * g11 - g01 * g01
    y1 = beta * (g11 * h11 - g01 * h12) / det
    y2 = beta * (g00 * h12 - g01 * h11) / det
    two = y2 / (beta * h21)
    one = y1 / beta + a * two
    for s in range(NS):
        out[pl.ds(s, W, stride=NS), :] = one * p0[s, :W, :] + two * q[s, :W, :]


def to_inner(x):
    return lax.ppermute(x, "sub", [(i, i ^ 1) for i in range(NSUB)])


def to_outer(x):
    ends = (0, NSUB - 1)
    return lax.ppermute(x, "sub", [(i, i if i in ends else ((i + 1) ^ 1) - 1) for i in range(NSUB)])


def to_far(x):
    return lax.ppermute(x, "sub", [(i, (i + (2 if i % 2 else -2)) % NSUB) for i in range(NSUB)])


def body(right_side, coupling, neighbours, inverse, margin, counts):
    here = lax.axis_index("sub").astype(jnp.int32).reshape(1)
    flat_right = right_side.transpose(1, 0, 2).reshape(W * NS, R)
    block, one = (NS, WP, R), (1, WP, R)
    v0, v0b = call(start_kernel, [(block, F32), (block, BF16)], [SM, VM])(counts, flat_right)
    outer, inner = to_outer(v0b), to_inner(v0b)

    coupling = pltpu.with_memory_space_constraint(coupling, pltpu.HBM)
    inverse = pltpu.with_memory_space_constraint(inverse, pltpu.HBM)

    def matrices(first, more):
        lanes = GROUP * W
        blocks = (0, SPLIT) if first else (SPLIT, NB)
        begin = blocks[0] * W // GROUP
        end = -(-blocks[1] * W // GROUP)
        count = -(-(end - begin) // CHUNK) * CHUNK
        groups = (begin, begin + count) if first else (end - count, end)
        outs = [((NS * (blocks[1] - blocks[0]), WP, WP), BF16, True)]
        if first:
            outs.append(((6 * W, 6 * W), BF16, True))
        return call(
            functools.partial(coupling_kernel, blocks, groups, first),
            outs,
            [ANY, ANY],
            [
                pltpu.VMEM((NS, count * lanes), BF16),
                pltpu.VMEM((2 * NS, lanes), F32),
                pltpu.VMEM((count * GROUP * NS, 128), F32),
                pltpu.VMEM((count * GROUP * NS, 128), F32),
                pltpu.SemaphoreType.DMA((count // CHUNK + 1,)),
            ],
            limit=24,
            cost=pl.CostEstimate(flops=1 << 20, bytes_accessed=12 << 20, transcendentals=0),
        )(coupling, more)

    first_part, held = matrices(True, inverse)
    held = pltpu.with_memory_space_constraint(held, pltpu.VMEM)
    first_part = pltpu.with_memory_space_constraint(first_part, pltpu.VMEM)

    def solve(own, inner, outer):
        (part,) = call(
            own_kernel, [((6 * W, R), F32, True)], [VM, VM], [pltpu.VMEM((OWN, R), F32)],
            cost=pl.CostEstimate(flops=1 << 30, bytes_accessed=4 << 20, transcendentals=0),
        )(held, own)
        depth = 6 * W - FROM
        spill_in, ext = call(
            margin_kernel,
            [(one, BF16), ((depth, R), BF16)],
            [SM, SM] + [VM] * 5,
            [pltpu.VMEM((depth, R), F32)],
        )(here, margin, held, part, own, inner, outer)
        got_in = to_inner(spill_in)
        out, spill_out = call(
            solve_kernel,
            [(block, F32), (one, BF16)],
            [SM, SM] + [VM] * 3,
            [pltpu.VMEM((NS * W, R), F32)],
            cost=pl.CostEstimate(flops=1 << 30, bytes_accessed=4 << 20, transcendentals=0),
        )(here, margin, held, part, ext)
        return out, got_in, spill_out

    def system(first, out, got_in, spill_out, *more):
        part, sent, near = call(
            inner_kernel, [(block, F32), ((NS + 1, WP, R), BF16), (block, BF16)], [VM] * 3
        )(out, got_in, spill_out)
        got, near, far = to_outer(sent), to_inner(near), to_far(spill_out)
        if first:
            (made,) = matrices(False, sent)
            matrix_parts.append(pltpu.with_memory_space_constraint(made, pltpu.VMEM))
        outs = [(block, F32)] + ([(block, F32), (one, BF16), (one, BF16)] if first else [])
        return call(
            functools.partial(system_kernel, first),
            outs + [((8, R), F32)],
            [SM, SM, SM] + [VM] * (8 + len(more)),
            [pltpu.VMEM((3 * NS, WP, R), BF16)],
        )(here, counts, neighbours, *matrix_parts, part, got, near, far, got_in, spill_out, *more)

    matrix_parts = [first_part]
    p0, w, w_in, w_out, sums_one = system(True, *solve(v0, inner, outer), v0)
    q, sums_two = system(False, *solve(w, to_inner(w_in), to_outer(w_out)), v0, w)
    sums = jnp.concatenate([sums_one[:3], sums_two[:3]], axis=0)
    sums = sums + to_inner(sums)
    gathered = lax.all_to_all(
        jnp.broadcast_to(sums[None], (NSUB // 2, 6, R)), "sub", 0, 0,
        axis_index_groups=[list(range(c, NSUB, 2)) for c in range(2)],
    )
    (flat,) = call(finish_kernel, [((W * NS, R), F32)], [VM] * 3)(gathered, p0, q)
    return flat.reshape(W, NS, R).transpose(1, 0, 2)


def solution(mesh):
    placed = (
        P("sub", None, "rhs"),
        P("sub", None),
        P("sub", None),
        P("sub", None, None),
        P("sub", None),
        P("sub"),
    )
    return jax.shard_map(
        body, mesh=mesh, in_specs=placed, out_specs=P("sub", None, "rhs"), check_vma=False
    )
```

```python
import functools
import jax
import jax.numpy as jnp
from jax import lax
from jax.experimental import pallas as pl
from jax.experimental.pallas import tpu as pltpu
from jax.sharding import PartitionSpec as P

EPS = 1e-06
W = 252
WP = 256
NS = 4
NB = 8
R = 128
NSUB = 64
SHIFT = 1.0
ROWS = NB * W
GROUP = 32
F32 = jnp.float32
BF16 = jnp.bfloat16
CHUNK = 8
SPLIT = 2
OWN = 1024
FROM = 896
ANY = pl.BlockSpec(memory_space=pl.ANY)
VM = pl.BlockSpec(memory_space=pltpu.VMEM)
SM = pl.BlockSpec(memory_space=pltpu.SMEM)


def call(kernel, outs, ins, scratch=(), limit=24, cost=None):
    return pl.pallas_call(
        kernel,
        out_shape=[pltpu.VMEM(s, d) if keep else jax.ShapeDtypeStruct(s, d) for s, d, *keep in outs],
        in_specs=ins,
        out_specs=[VM] * len(outs),
        scratch_shapes=list(scratch),
        compiler_params=pltpu.CompilerParams(vmem_limit_bytes=limit << 20),
        cost_estimate=cost,
    )


def start_kernel(counts, right, v0_ref, v0b_ref):
    for s in range(NS):
        alive = jnp.where(counts[0] > s, 1.0, 0.0)
        v0_ref[s, :W, :] = right[pl.ds(s, W, stride=NS), :] * alive
        v0_ref[s, W:, :] = jnp.zeros((WP - W, R), F32)
        v0b_ref[s] = v0_ref[s].astype(BF16)


def coupling_kernel(blocks, groups, first, flat, *rest):
    if first:
        inverse, c_ref, inverse_ref, raw, x, lo, hi, sems = rest
    else:
        _, c_ref, raw, x, lo, hi, sems = rest
    lanes = GROUP * W
    count = groups[1] - groups[0]
    step = CHUNK * lanes
    chunks = count // CHUNK
    copies = [
        pltpu.make_async_copy(
            flat.at[:, pl.ds(groups[0] * lanes + c * step, step)],
            raw.at[:, pl.ds(c * step, step)],
            sems.at[c],
        )
        for c in range(chunks)
    ]
    if first:
        copies.append(pltpu.make_async_copy(inverse.at[0], inverse_ref, sems.at[chunks]))
    for copy in copies:
        copy.start()
    lane = lax.broadcasted_iota(jnp.int32, (8, 128), 1)

    def pair(i, carry):
        for h in range(2):
            at = pl.multiple_of((2 * i + h) * lanes, 128)
            x[4 * h : 4 * h + 4, :] = raw[:, pl.ds(at, lanes)].astype(F32)
        base = pl.multiple_of(2 * i * (GROUP * NS), 8)
        for s in range(GROUP):
            def rolled(t):
                piece = x[:, 128 * t : 128 * t + 128]
                return pltpu.roll(piece, 4 * s, 1) if s else piece

            middle = rolled(2 * s)
            if s == 0:
                left, right = middle, rolled(1)
            else:
                early = lane < 4 * s
                left = jnp.where(early, rolled(2 * s - 1), middle)
                right = jnp.where(early, middle, rolled(2 * s + 1)) if s < GROUP - 1 else middle
            for h in range(2):
                at = base + (h * GROUP + s) * NS
                lo[pl.ds(at, NS), :] = left[4 * h : 4 * h + 4]
                hi[pl.ds(at, NS), :] = right[4 * h : 4 * h + 4]
        return carry

    for c in range(chunks):
        copies[c].wait()
        lax.fori_loop(c * CHUNK // 2, (c + 1) * CHUNK // 2, pair, 0)
    keep = lax.broadcasted_iota(jnp.int32, (WP, 128), 1) < W - 128
    pad = jnp.zeros((WP - W, 128), F32)
    skip = (blocks[0] * W - groups[0] * GROUP) * NS
    number = blocks[1] - blocks[0]

    def place(k, carry):
        for p in range(NS):
            row = skip + k * (W * NS) + p
            left = lo[pl.ds(row, W, stride=NS), :]
            right = hi[pl.ds(row, W, stride=NS), :]
            right = jnp.where(keep, jnp.concatenate([right, pad], axis=0), 0.0)
            c_ref[p * number + k, :, :128] = jnp.concatenate([left, pad], axis=0).astype(BF16)
            c_ref[p * number + k, :, 128:] = right.astype(BF16)
        return carry

    lax.fori_loop(0, number, place, 0)
    if first:
        copies[chunks].wait()


def own_kernel(inverse, own, part_ref, ext):
    for s in range(NS):
        ext[s * W : (s + 1) * W, :] = own[s, :W, :]
    ext[NS * W :, :] = jnp.zeros((OWN - NS * W, R), F32)
    part_ref[...] = jnp.dot(inverse[:, :OWN], ext[...].astype(BF16), preferred_element_type=F32)


def places(place, margin):
    here = place[0]
    low = jnp.clip(margin[0, 0] - NS * jnp.maximum(here - 1, 0), 0, NS - 1)
    high = jnp.clip(margin[0, 1] - NS * jnp.minimum(here + 1, NSUB - 1), 0, NS - 1)
    return here % 2 == 0, here == 0, here == NSUB - 1, low, high


def spilled(inverse, part, ext, block, index):
    begin = block * W // 16 * 16
    end = -(-(block + 1) * W // 16) * 16
    end = min(end, 6 * W)
    rows = jnp.dot(inverse[begin:end, FROM:], ext, preferred_element_type=F32)
    rows = rows[block * W - begin : (block + 1) * W - begin] + part[block * W : (block + 1) * W, :]
    mark = jnp.ones((WP - W, R), F32) * index.astype(F32)
    return jnp.concatenate([rows, mark], axis=0)


def margin_kernel(place, margin, inverse, part, own, inner, outer, in_ref, ext_ref, ext):
    even, first, last, low, high = places(place, margin)
    odd = jnp.logical_not(even)
    ext[: NS * W - FROM, :] = jnp.zeros((NS * W - FROM, R), F32)
    some = inner.shape[0] > 1

    def put(when, block, source, index):
        @pl.when(when)
        def _():
            ext[block * W - FROM : (block + 1) * W - FROM, :] = source[index].astype(F32)[:W]

    put(first, NS, own, low)
    put(jnp.logical_and(even, jnp.logical_not(first)), NS, outer, low if some else 0)
    put(odd, NS, inner, low if some else 0)
    put(last, NS + 1, own, high)
    put(jnp.logical_and(odd, jnp.logical_not(last)), NS + 1, outer, high if some else 0)
    put(even, NS + 1, inner, high if some else 0)
    ext_ref[...] = ext[...].astype(BF16)

    @pl.when(even)
    def _():
        in_ref[0] = spilled(inverse, part, ext_ref[...], NS + 1, high).astype(BF16)

    @pl.when(odd)
    def _():
        in_ref[0] = spilled(inverse, part, ext_ref[...], NS, low).astype(BF16)


def solve_kernel(place, margin, inverse, part, ext, out_ref, out2_ref, res):
    even, first, last, low, high = places(place, margin)
    mine = NS * W
    res[...] = part[:mine, :] + jnp.dot(inverse[:mine, FROM:], ext[...], preferred_element_type=F32)
    pad = jnp.zeros((WP - W, R), F32)
    for s in range(NS):
        out_ref[s] = jnp.concatenate([res[s * W : (s + 1) * W, :], pad], axis=0)
    keep = lax.broadcasted_iota(jnp.int32, (WP, R), 0) < W

    def spill(when, ends, block, index):
        @pl.when(when)
        def _():
            rows = spilled(inverse, part, ext[...], block, index)
            out2_ref[0] = rows.astype(BF16)

            @pl.when(ends)
            def _():
                out_ref[index] += jnp.where(keep, rows, 0.0)

    spill(even, first, NS, low)
    spill(jnp.logical_not(even), last, NS + 1, high)


def opened(block):
    x = block.astype(F32)
    rows = lax.broadcasted_iota(jnp.int32, x.shape, 0)
    return jnp.where(rows < W, x, 0.0), x[W : W + 1, :]


def inner_kernel(out, spill_in, spill_out, part_ref, sent_ref, near_ref):
    values, index = opened(spill_in[0])
    for s in range(NS):
        part = out[s] + jnp.where(index == s, values, 0.0)
        part_ref[s] = part
        sent_ref[s] = part.astype(BF16)
        near_ref[s] = part.astype(BF16)
    sent_ref[NS] = spill_out[0]


def system_kernel(
    first, place, counts, neighbours, ca, cb, part, got, near, far, spill_in, spill_out, v0, *rest
):
    if first:
        p_ref, w_ref, win_ref, wout_ref, sums_ref, u = rest
    else:
        w, p_ref, sums_ref, u = rest
    here = place[0]
    odd = here % 2 == 1
    ends = jnp.logical_or(here == 0, here == NSUB - 1)
    got_values, got_index = opened(got[NS])
    got_index = jnp.where(ends, -1.0, got_index)
    far_values, far_index = opened(far[0])
    far_index = jnp.where(jnp.logical_or(here == 1, here == NSUB - 2), -1.0, far_index)
    values, index = opened(spill_out[0])
    for s in range(NS):
        alive = jnp.where(counts[0] > s, 1.0, 0.0)
        p = (part[s] + jnp.where(got_index == s, got_values, 0.0)) * alive
        p_ref[s] = p
        u[s] = (got[s].astype(F32) + jnp.where(index == s, values, 0.0)).astype(BF16)
        u[NS + s] = p.astype(BF16)
        u[2 * NS + s] = (near[s].astype(F32) + jnp.where(far_index == s, far_values, 0.0)).astype(BF16)
    sums_ref[...] = jnp.zeros((8, R), F32)
    if first:
        w_ref[...] = jnp.zeros((NS, WP, R), F32)

    def one(s):
        acc = p_ref[s]
        for k in range(NB):
            slot = jnp.clip(neighbours[s, k] - NS * (here - 1), 0, 3 * NS - 1)
            slot = jnp.where(odd, slot + 2 * NS * (1 - slot // NS), slot)
            matrix = ca[s * SPLIT + k] if k < SPLIT else cb[s * (NB - SPLIT) + k - SPLIT]
            acc += jnp.dot(matrix, u[slot], preferred_element_type=F32)
        image = acc
        start = v0[s]
        if first:
            image = image - SHIFT * start
            w_ref[s] = image
            terms = (start * start, start * image, image * image)
        else:
            terms = (start * image, w[s] * image, image * image)
        sums = [jnp.sum(x, axis=0, keepdims=True) for x in terms]
        sums_ref[...] += jnp.concatenate(sums + [jnp.zeros((5, R), F32)], axis=0)

    for s in range(NS):
        pl.when(counts[0] > s)(functools.partial(one, s))
    if first:
        wanted = opened(spill_in[0])[1]
        for ref, index in ((win_ref, wanted), (wout_ref, got_index)):
            chosen = jnp.zeros((WP, R), F32)
            for s in range(NS):
                chosen = chosen + jnp.where(index == s, w_ref[s], 0.0)
            ref[0] = chosen.astype(BF16)


def finish_kernel(gathered, p0, q, out):
    total = jnp.sum(gathered[...], axis=0)
    s00, s01, s11, s02, s12, s22 = (total[i : i + 1, :] for i in range(6))
    c = SHIFT
    bb = s00 + EPS
    beta = jnp.sqrt(bb)
    h11 = (s01 + c * s00) / bb
    a = c - h11
    n2 = (s11 + 2 * a * s01 + a * a * s00) / bb
    h21s = jnp.maximum(n2, 0.0) + EPS
    h21 = jnp.sqrt(h21s)
    full = bb * h21s
    v0i = s01 + c * s00
    h12 = (s02 + a * v0i) / (bb * h21)
    cross = (s01 + a * s00) / (bb * h21)
    b2i = (s12 + a * s02 + a * (s11 + c * s01) + a * a * v0i) / full
    h22 = b2i - h12 * cross
    ii = (s22 + 2 * a * (s12 + c * s02) + a * a * (s11 + 2 * c * s01 + c * c * s00)) / full
    rest = (
        ii + h12 * h12 * (s00 / bb) + h22 * h22 * (n2 / h21s)
        - 2 * h12 * h12 - 2 * h22 * b2i + 2 * h12 * h22 * cross
    )
    h32s = jnp.maximum(rest, 0.0) + EPS
    g00 = h11 * h11 + h21s
    g01 = h11 * h12 + h21 * h22
    g11 = h12 * h12 + h22 * h22 + h32s
    det = g00 * g11 - g01 * g01
    y1 = beta * (g11 * h11 - g01 * h12) / det
    y2 = beta * (g00 * h12 - g01 * h11) / det
    two = y2 / (beta * h21)
    one = y1 / beta + a * two
    for s in range(NS):
        out[pl.ds(s, W, stride=NS), :] = one * p0[s, :W, :] + two * q[s, :W, :]


def permuted(x, target):
    parts = lax.axis_size("rhs")
    pairs = [(i, j) for i in range(NSUB) for j in range(parts)]
    return lax.ppermute(
        x, ("sub", "rhs"), [(i * parts + j, t[0] * parts + t[1]) for i, j in pairs for t in [target(i, j)]]
    )


def to_inner(x):
    return permuted(x, lambda i, j: (i ^ 1, j))


def to_outer(x):
    return permuted(x, lambda i, j: (i, j ^ 1) if i in (0, NSUB - 1) else (((i + 1) ^ 1) - 1, j))


def to_far(x):
    def target(i, j):
        if i in (0, NSUB - 1):
            return i ^ 1, j
        return i + (2 if i % 2 else -2), j

    return permuted(x, target)


def body(right_side, coupling, neighbours, inverse, margin, counts):
    here = lax.axis_index("sub").astype(jnp.int32).reshape(1)
    flat_right = right_side.transpose(1, 0, 2).reshape(W * NS, R)
    block, one = (NS, WP, R), (1, WP, R)
    v0, v0b = call(start_kernel, [(block, F32), (block, BF16)], [SM, VM])(counts, flat_right)
    outer, inner = to_outer(v0b), to_inner(v0b)

    coupling = pltpu.with_memory_space_constraint(coupling, pltpu.HBM)
    inverse = pltpu.with_memory_space_constraint(inverse, pltpu.HBM)

    def matrices(first, more):
        lanes = GROUP * W
        blocks = (0, SPLIT) if first else (SPLIT, NB)
        begin = blocks[0] * W // GROUP
        end = -(-blocks[1] * W // GROUP)
        count = -(-(end - begin) // CHUNK) * CHUNK
        groups = (begin, begin + count) if first else (end - count, end)
        outs = [((NS * (blocks[1] - blocks[0]), WP, WP), BF16, True)]
        if first:
            outs.append(((6 * W, 6 * W), BF16, True))
        return call(
            functools.partial(coupling_kernel, blocks, groups, first),
            outs,
            [ANY, ANY],
            [
                pltpu.VMEM((NS, count * lanes), BF16),
                pltpu.VMEM((2 * NS, lanes), F32),
                pltpu.VMEM((count * GROUP * NS, 128), F32),
                pltpu.VMEM((count * GROUP * NS, 128), F32),
                pltpu.SemaphoreType.DMA((count // CHUNK + 1,)),
            ],
            limit=24,
            cost=pl.CostEstimate(flops=1 << 20, bytes_accessed=12 << 20, transcendentals=0),
        )(coupling, more)

    first_part, held = matrices(True, inverse)
    held = pltpu.with_memory_space_constraint(held, pltpu.VMEM)
    first_part = pltpu.with_memory_space_constraint(first_part, pltpu.VMEM)

    def solve(own, inner, outer):
        (part,) = call(
            own_kernel, [((6 * W, R), F32, True)], [VM, VM], [pltpu.VMEM((OWN, R), F32)],
            cost=pl.CostEstimate(flops=1 << 30, bytes_accessed=4 << 20, transcendentals=0),
        )(held, own)
        depth = 6 * W - FROM
        spill_in, ext = call(
            margin_kernel,
            [(one, BF16), ((depth, R), BF16)],
            [SM, SM] + [VM] * 5,
            [pltpu.VMEM((depth, R), F32)],
        )(here, margin, held, part, own, inner, outer)
        got_in = to_inner(spill_in)
        out, spill_out = call(
            solve_kernel,
            [(block, F32), (one, BF16)],
            [SM, SM] + [VM] * 3,
            [pltpu.VMEM((NS * W, R), F32)],
            cost=pl.CostEstimate(flops=1 << 30, bytes_accessed=4 << 20, transcendentals=0),
        )(here, margin, held, part, ext)
        return out, got_in, spill_out

    def system(first, out, got_in, spill_out, *more):
        part, sent, near = call(
            inner_kernel, [(block, F32), ((NS + 1, WP, R), BF16), (block, BF16)], [VM] * 3
        )(out, got_in, spill_out)
        got, near, far = to_outer(sent), to_inner(near), to_far(spill_out)
        if first:
            (made,) = matrices(False, sent)
            matrix_parts.append(pltpu.with_memory_space_constraint(made, pltpu.VMEM))
        outs = [(block, F32)] + ([(block, F32), (one, BF16), (one, BF16)] if first else [])
        return call(
            functools.partial(system_kernel, first),
            outs + [((8, R), F32)],
            [SM, SM, SM] + [VM] * (8 + len(more)),
            [pltpu.VMEM((3 * NS, WP, R), BF16)],
        )(here, counts, neighbours, *matrix_parts, part, got, near, far, got_in, spill_out, *more)

    matrix_parts = [first_part]
    p0, w, w_in, w_out, sums_one = system(True, *solve(v0, inner, outer), v0)
    q, sums_two = system(False, *solve(w, to_inner(w_in), to_outer(w_out)), v0, w)
    sums = jnp.concatenate([sums_one[:3], sums_two[:3]], axis=0)
    sums = sums + to_inner(sums)
    gathered = lax.all_to_all(
        jnp.broadcast_to(sums[None], (NSUB // 2, 6, R)), "sub", 0, 0,
        axis_index_groups=[list(range(c, NSUB, 2)) for c in range(2)],
    )
    (flat,) = call(finish_kernel, [((W * NS, R), F32)], [VM] * 3)(gathered, p0, q)
    return flat.reshape(W, NS, R).transpose(1, 0, 2)


def solution(mesh):
    placed = (
        P("sub", None, "rhs"),
        P("sub", None),
        P("sub", None),
        P("sub", None, None),
        P("sub", None),
        P("sub"),
    )
    return jax.shard_map(
        body, mesh=mesh, in_specs=placed, out_specs=P("sub", None, "rhs"), check_vma=False
    )
```

```python
import functools
import jax
import jax.numpy as jnp
from jax import lax
from jax.experimental import pallas as pl
from jax.experimental.pallas import tpu as pltpu
from jax.sharding import PartitionSpec as P

EPS = 1e-06
W = 252
WP = 256
NS = 4
NB = 8
R = 128
NSUB = 64
SHIFT = 1.0
ROWS = NB * W
GROUP = 32
F32 = jnp.float32
BF16 = jnp.bfloat16
CHUNK = 8
SPLIT = 4
OWN = 1024
FROM = 896
ANY = pl.BlockSpec(memory_space=pl.ANY)
VM = pl.BlockSpec(memory_space=pltpu.VMEM)
SM = pl.BlockSpec(memory_space=pltpu.SMEM)


def call(kernel, outs, ins, scratch=(), limit=24, cost=None):
    return pl.pallas_call(
        kernel,
        out_shape=[pltpu.VMEM(s, d) if keep else jax.ShapeDtypeStruct(s, d) for s, d, *keep in outs],
        in_specs=ins,
        out_specs=[VM] * len(outs),
        scratch_shapes=list(scratch),
        compiler_params=pltpu.CompilerParams(vmem_limit_bytes=limit << 20),
        cost_estimate=cost,
    )


def start_kernel(counts, right, v0_ref, v0b_ref):
    for s in range(NS):
        alive = jnp.where(counts[0] > s, 1.0, 0.0)
        v0_ref[s, :W, :] = right[pl.ds(s, W, stride=NS), :] * alive
        v0_ref[s, W:, :] = jnp.zeros((WP - W, R), F32)
        v0b_ref[s] = v0_ref[s].astype(BF16)


def coupling_kernel(blocks, groups, first, flat, *rest):
    if first:
        inverse, c_ref, inverse_ref, raw, x, lo, hi, sems = rest
    else:
        _, c_ref, raw, x, lo, hi, sems = rest
    lanes = GROUP * W
    count = groups[1] - groups[0]
    step = CHUNK * lanes
    chunks = count // CHUNK
    copies = [
        pltpu.make_async_copy(
            flat.at[:, pl.ds(groups[0] * lanes + c * step, step)],
            raw.at[:, pl.ds(c * step, step)],
            sems.at[c],
        )
        for c in range(chunks)
    ]
    if first:
        copies.append(pltpu.make_async_copy(inverse.at[0], inverse_ref, sems.at[chunks]))
    for copy in copies:
        copy.start()
    lane = lax.broadcasted_iota(jnp.int32, (4 * NS, 128), 1)

    def four(i, carry):
        for h in range(4):
            at = pl.multiple_of((4 * i + h) * lanes, 128)
            x[NS * h : NS * h + NS, :] = raw[:, pl.ds(at, lanes)]
        base = pl.multiple_of(4 * i * (GROUP * NS), 8)
        for s in range(GROUP):
            def rolled(t):
                piece = x[:, 128 * t : 128 * t + 128]
                return pltpu.roll(piece, 4 * s, 1) if s else piece

            middle = rolled(2 * s)
            if s == 0:
                left, right = middle, rolled(1)
            else:
                early = lane < 4 * s
                left = jnp.where(early, rolled(2 * s - 1), middle)
                right = jnp.where(early, middle, rolled(2 * s + 1)) if s < GROUP - 1 else middle
            left, right = left.astype(F32), right.astype(F32)
            for h in range(4):
                at = base + (h * GROUP + s) * NS
                lo[pl.ds(at, NS), :] = left[NS * h : NS * h + NS]
                hi[pl.ds(at, NS), :] = right[NS * h : NS * h + NS]
        return carry

    for c in range(chunks):
        copies[c].wait()
        lax.fori_loop(c * CHUNK // 4, (c + 1) * CHUNK // 4, four, 0)
    keep = lax.broadcasted_iota(jnp.int32, (WP, 128), 1) < W - 128
    pad = jnp.zeros((WP - W, 128), F32)
    skip = (blocks[0] * W - groups[0] * GROUP) * NS
    number = blocks[1] - blocks[0]

    def place(k, carry):
        for p in range(NS):
            row = skip + k * (W * NS) + p
            left = lo[pl.ds(row, W, stride=NS), :]
            right = hi[pl.ds(row, W, stride=NS), :]
            right = jnp.where(keep, jnp.concatenate([right, pad], axis=0), 0.0)
            c_ref[p * number + k, :, :128] = jnp.concatenate([left, pad], axis=0).astype(BF16)
            c_ref[p * number + k, :, 128:] = right.astype(BF16)
        return carry

    lax.fori_loop(0, number, place, 0)
    if first:
        copies[chunks].wait()


def own_kernel(inverse, own, part_ref, ext):
    for s in range(NS):
        ext[s * W : (s + 1) * W, :] = own[s, :W, :]
    ext[NS * W :, :] = jnp.zeros((OWN - NS * W, R), F32)
    part_ref[...] = jnp.dot(inverse[:, :OWN], ext[...].astype(BF16), preferred_element_type=F32)


def places(place, margin):
    here = place[0]
    low = jnp.clip(margin[0, 0] - NS * jnp.maximum(here - 1, 0), 0, NS - 1)
    high = jnp.clip(margin[0, 1] - NS * jnp.minimum(here + 1, NSUB - 1), 0, NS - 1)
    return here % 2 == 0, here == 0, here == NSUB - 1, low, high


def spilled(inverse, part, ext, block, index):
    begin = block * W // 16 * 16
    end = -(-(block + 1) * W // 16) * 16
    end = min(end, 6 * W)
    rows = jnp.dot(inverse[begin:end, FROM:], ext, preferred_element_type=F32)
    rows = rows[block * W - begin : (block + 1) * W - begin] + part[block * W : (block + 1) * W, :]
    mark = jnp.ones((WP - W, R), F32) * index.astype(F32)
    return jnp.concatenate([rows, mark], axis=0)


def margin_kernel(place, margin, inverse, part, own, inner, outer, in_ref, ext_ref, ext):
    even, first, last, low, high = places(place, margin)
    odd = jnp.logical_not(even)
    ext[: NS * W - FROM, :] = jnp.zeros((NS * W - FROM, R), F32)
    some = inner.shape[0] > 1

    def put(when, block, source, index):
        @pl.when(when)
        def _():
            ext[block * W - FROM : (block + 1) * W - FROM, :] = source[index].astype(F32)[:W]

    put(first, NS, own, low)
    put(jnp.logical_and(even, jnp.logical_not(first)), NS, outer, low if some else 0)
    put(odd, NS, inner, low if some else 0)
    put(last, NS + 1, own, high)
    put(jnp.logical_and(odd, jnp.logical_not(last)), NS + 1, outer, high if some else 0)
    put(even, NS + 1, inner, high if some else 0)
    ext_ref[...] = ext[...].astype(BF16)

    @pl.when(even)
    def _():
        in_ref[0] = spilled(inverse, part, ext_ref[...], NS + 1, high).astype(BF16)

    @pl.when(odd)
    def _():
        in_ref[0] = spilled(inverse, part, ext_ref[...], NS, low).astype(BF16)


def solve_kernel(place, margin, inverse, part, ext, out_ref, out2_ref, res):
    even, first, last, low, high = places(place, margin)
    mine = NS * W
    res[...] = part[:mine, :] + jnp.dot(inverse[:mine, FROM:], ext[...], preferred_element_type=F32)
    pad = jnp.zeros((WP - W, R), F32)
    for s in range(NS):
        out_ref[s] = jnp.concatenate([res[s * W : (s + 1) * W, :], pad], axis=0)
    keep = lax.broadcasted_iota(jnp.int32, (WP, R), 0) < W

    def spill(when, ends, block, index):
        @pl.when(when)
        def _():
            rows = spilled(inverse, part, ext[...], block, index)
            out2_ref[0] = rows.astype(BF16)

            @pl.when(ends)
            def _():
                out_ref[index] += jnp.where(keep, rows, 0.0)

    spill(even, first, NS, low)
    spill(jnp.logical_not(even), last, NS + 1, high)


def opened(block):
    x = block.astype(F32)
    rows = lax.broadcasted_iota(jnp.int32, x.shape, 0)
    return jnp.where(rows < W, x, 0.0), x[W : W + 1, :]


def inner_kernel(out, spill_in, spill_out, part_ref, sent_ref, near_ref):
    values, index = opened(spill_in[0])
    for s in range(NS):
        part = out[s] + jnp.where(index == s, values, 0.0)
        part_ref[s] = part
        sent_ref[s] = part.astype(BF16)
        near_ref[s] = part.astype(BF16)
    sent_ref[NS] = spill_out[0]


def system_kernel(
    first, place, counts, neighbours, ca, cb, part, got, near, far, spill_in, spill_out, v0, *rest
):
    if first:
        p_ref, w_ref, win_ref, wout_ref, sums_ref, u = rest
    else:
        w, p_ref, sums_ref, u = rest
    here = place[0]
    odd = here % 2 == 1
    ends = jnp.logical_or(here == 0, here == NSUB - 1)
    got_values, got_index = opened(got[NS])
    got_index = jnp.where(ends, -1.0, got_index)
    far_values, far_index = opened(far[0])
    far_index = jnp.where(jnp.logical_or(here == 1, here == NSUB - 2), -1.0, far_index)
    values, index = opened(spill_out[0])
    for s in range(NS):
        alive = jnp.where(counts[0] > s, 1.0, 0.0)
        p = (part[s] + jnp.where(got_index == s, got_values, 0.0)) * alive
        p_ref[s] = p
        u[s] = (got[s].astype(F32) + jnp.where(index == s, values, 0.0)).astype(BF16)
        u[NS + s] = p.astype(BF16)
        u[2 * NS + s] = (near[s].astype(F32) + jnp.where(far_index == s, far_values, 0.0)).astype(BF16)
    sums_ref[...] = jnp.zeros((8, R), F32)
    if first:
        w_ref[...] = jnp.zeros((NS, WP, R), F32)

    def one(s):
        acc = p_ref[s]
        for k in range(NB):
            slot = jnp.clip(neighbours[s, k] - NS * (here - 1), 0, 3 * NS - 1)
            slot = jnp.where(odd, slot + 2 * NS * (1 - slot // NS), slot)
            matrix = ca[s * SPLIT + k] if k < SPLIT else cb[s * (NB - SPLIT) + k - SPLIT]
            acc += jnp.dot(matrix, u[slot], preferred_element_type=F32)
        image = acc
        start = v0[s]
        if first:
            image = image - SHIFT * start
            w_ref[s] = image
            terms = (start * start, start * image, image * image)
        else:
            terms = (start * image, w[s] * image, image * image)
        sums = [jnp.sum(x, axis=0, keepdims=True) for x in terms]
        sums_ref[...] += jnp.concatenate(sums + [jnp.zeros((5, R), F32)], axis=0)

    for s in range(NS):
        pl.when(counts[0] > s)(functools.partial(one, s))
    if first:
        wanted = opened(spill_in[0])[1]
        for ref, index in ((win_ref, wanted), (wout_ref, got_index)):
            chosen = jnp.zeros((WP, R), F32)
            for s in range(NS):
                chosen = chosen + jnp.where(index == s, w_ref[s], 0.0)
            ref[0] = chosen.astype(BF16)


def finish_kernel(gathered, p0, q, out):
    total = jnp.sum(gathered[...], axis=0)
    s00, s01, s11, s02, s12, s22 = (total[i : i + 1, :] for i in range(6))
    c = SHIFT
    bb = s00 + EPS
    beta = jnp.sqrt(bb)
    h11 = (s01 + c * s00) / bb
    a = c - h11
    n2 = (s11 + 2 * a * s01 + a * a * s00) / bb
    h21s = jnp.maximum(n2, 0.0) + EPS
    h21 = jnp.sqrt(h21s)
    full = bb * h21s
    v0i = s01 + c * s00
    h12 = (s02 + a * v0i) / (bb * h21)
    cross = (s01 + a * s00) / (bb * h21)
    b2i = (s12 + a * s02 + a * (s11 + c * s01) + a * a * v0i) / full
    h22 = b2i - h12 * cross
    ii = (s22 + 2 * a * (s12 + c * s02) + a * a * (s11 + 2 * c * s01 + c * c * s00)) / full
    rest = (
        ii + h12 * h12 * (s00 / bb) + h22 * h22 * (n2 / h21s)
        - 2 * h12 * h12 - 2 * h22 * b2i + 2 * h12 * h22 * cross
    )
    h32s = jnp.maximum(rest, 0.0) + EPS
    g00 = h11 * h11 + h21s
    g01 = h11 * h12 + h21 * h22
    g11 = h12 * h12 + h22 * h22 + h32s
    det = g00 * g11 - g01 * g01
    y1 = beta * (g11 * h11 - g01 * h12) / det
    y2 = beta * (g00 * h12 - g01 * h11) / det
    two = y2 / (beta * h21)
    one = y1 / beta + a * two
    for s in range(NS):
        out[pl.ds(s, W, stride=NS), :] = one * p0[s, :W, :] + two * q[s, :W, :]


def permuted(x, target):
    parts = lax.axis_size("rhs")
    pairs = [(i, j) for i in range(NSUB) for j in range(parts)]
    return lax.ppermute(
        x, ("sub", "rhs"), [(i * parts + j, t[0] * parts + t[1]) for i, j in pairs for t in [target(i, j)]]
    )


def to_inner(x):
    return permuted(x, lambda i, j: (i ^ 1, j))


def to_outer(x):
    return permuted(x, lambda i, j: (i, j ^ 1) if i in (0, NSUB - 1) else (((i + 1) ^ 1) - 1, j))


def to_far(x):
    def target(i, j):
        if i in (0, NSUB - 1):
            return i ^ 1, j
        return i + (2 if i % 2 else -2), j

    return permuted(x, target)


def body(right_side, coupling, neighbours, inverse, margin, counts):
    here = lax.axis_index("sub").astype(jnp.int32).reshape(1)
    flat_right = right_side.transpose(1, 0, 2).reshape(W * NS, R)
    block, one = (NS, WP, R), (1, WP, R)
    v0, v0b = call(start_kernel, [(block, F32), (block, BF16)], [SM, VM])(counts, flat_right)
    outer, inner = to_outer(v0b), to_inner(v0b)

    coupling = pltpu.with_memory_space_constraint(coupling, pltpu.HBM)
    inverse = pltpu.with_memory_space_constraint(inverse, pltpu.HBM)

    def matrices(first, more):
        lanes = GROUP * W
        blocks = (0, SPLIT) if first else (SPLIT, NB)
        begin = blocks[0] * W // GROUP
        end = -(-blocks[1] * W // GROUP)
        count = -(-(end - begin) // CHUNK) * CHUNK
        groups = (begin, begin + count) if first else (end - count, end)
        outs = [((NS * (blocks[1] - blocks[0]), WP, WP), BF16, True)]
        if first:
            outs.append(((6 * W, 6 * W), BF16, True))
        return call(
            functools.partial(coupling_kernel, blocks, groups, first),
            outs,
            [ANY, ANY],
            [
                pltpu.VMEM((NS, count * lanes), BF16),
                pltpu.VMEM((4 * NS, lanes), BF16),
                pltpu.VMEM((count * GROUP * NS, 128), F32),
                pltpu.VMEM((count * GROUP * NS, 128), F32),
                pltpu.SemaphoreType.DMA((count // CHUNK + 1,)),
            ],
            limit=24,
            cost=pl.CostEstimate(flops=1 << 20, bytes_accessed=12 << 20, transcendentals=0),
        )(coupling, more)

    first_part, held = matrices(True, inverse)
    held = pltpu.with_memory_space_constraint(held, pltpu.VMEM)
    first_part = pltpu.with_memory_space_constraint(first_part, pltpu.VMEM)

    def solve(own, inner, outer):
        (part,) = call(
            own_kernel, [((6 * W, R), F32, True)], [VM, VM], [pltpu.VMEM((OWN, R), F32)],
            cost=pl.CostEstimate(flops=1 << 30, bytes_accessed=4 << 20, transcendentals=0),
        )(held, own)
        depth = 6 * W - FROM
        spill_in, ext = call(
            margin_kernel,
            [(one, BF16), ((depth, R), BF16)],
            [SM, SM] + [VM] * 5,
            [pltpu.VMEM((depth, R), F32)],
        )(here, margin, held, part, own, inner, outer)
        got_in = to_inner(spill_in)
        out, spill_out = call(
            solve_kernel,
            [(block, F32), (one, BF16)],
            [SM, SM] + [VM] * 3,
            [pltpu.VMEM((NS * W, R), F32)],
            cost=pl.CostEstimate(flops=1 << 30, bytes_accessed=4 << 20, transcendentals=0),
        )(here, margin, held, part, ext)
        return out, got_in, spill_out

    def system(first, out, got_in, spill_out, *more):
        part, sent, near = call(
            inner_kernel, [(block, F32), ((NS + 1, WP, R), BF16), (block, BF16)], [VM] * 3
        )(out, got_in, spill_out)
        got, near, far = to_outer(sent), to_inner(near), to_far(spill_out)
        if first:
            (made,) = matrices(False, sent)
            matrix_parts.append(pltpu.with_memory_space_constraint(made, pltpu.VMEM))
        outs = [(block, F32)] + ([(block, F32), (one, BF16), (one, BF16)] if first else [])
        return call(
            functools.partial(system_kernel, first),
            outs + [((8, R), F32)],
            [SM, SM, SM] + [VM] * (8 + len(more)),
            [pltpu.VMEM((3 * NS, WP, R), BF16)],
        )(here, counts, neighbours, *matrix_parts, part, got, near, far, got_in, spill_out, *more)

    matrix_parts = [first_part]
    p0, w, w_in, w_out, sums_one = system(True, *solve(v0, inner, outer), v0)
    q, sums_two = system(False, *solve(w, to_inner(w_in), to_outer(w_out)), v0, w)
    sums = jnp.concatenate([sums_one[:3], sums_two[:3]], axis=0)
    sums = sums + to_inner(sums)
    gathered = lax.all_to_all(
        jnp.broadcast_to(sums[None], (NSUB // 2, 6, R)), "sub", 0, 0,
        axis_index_groups=[list(range(c, NSUB, 2)) for c in range(2)],
    )
    (flat,) = call(finish_kernel, [((W * NS, R), F32)], [VM] * 3)(gathered, p0, q)
    return flat.reshape(W, NS, R).transpose(1, 0, 2)


def solution(mesh):
    placed = (
        P("sub", None, "rhs"),
        P("sub", None),
        P("sub", None),
        P("sub", None, None),
        P("sub", None),
        P("sub"),
    )
    return jax.shard_map(
        body, mesh=mesh, in_specs=placed, out_specs=P("sub", None, "rhs"), check_vma=False
    )
```

```python
import functools
import jax
import jax.numpy as jnp
from jax import lax
from jax.experimental import pallas as pl
from jax.experimental.pallas import tpu as pltpu
from jax.sharding import PartitionSpec as P

EPS = 1e-06
W = 252
WP = 256
NS = 4
NB = 8
R = 128
NSUB = 64
SHIFT = 1.0
ROWS = NB * W
GROUP = 32
F32 = jnp.float32
BF16 = jnp.bfloat16
CHUNK = 8
SPLIT = 4
EVEN, FIRST, LAST, LOW, HIGH, COUNT, ENDS, NEXT, OUT, SLOTS = range(10)
TABLE = SLOTS + NS * NB
OWN = 1024
FROM = 896
ANY = pl.BlockSpec(memory_space=pl.ANY)
VM = pl.BlockSpec(memory_space=pltpu.VMEM)
SM = pl.BlockSpec(memory_space=pltpu.SMEM)


def call(kernel, outs, ins, scratch=(), limit=24, cost=None):
    return pl.pallas_call(
        kernel,
        out_shape=[keep[0](s, d) if keep else jax.ShapeDtypeStruct(s, d) for s, d, *keep in outs],
        in_specs=ins,
        out_specs=[SM if keep == [pltpu.SMEM] else VM for _, _, *keep in outs],
        scratch_shapes=list(scratch),
        compiler_params=pltpu.CompilerParams(vmem_limit_bytes=limit << 20),
        cost_estimate=cost,
    )


def start_kernel(counts, right, v0_ref, v0b_ref):
    for s in range(NS):
        alive = jnp.where(counts[0] > s, 1.0, 0.0)
        v0_ref[s, :W, :] = right[pl.ds(s, W, stride=NS), :] * alive
        v0_ref[s, W:, :] = jnp.zeros((WP - W, R), F32)
        v0b_ref[s] = v0_ref[s].astype(BF16)


def fill_table(table, place, counts, margin, neighbours):
    here = place[0]
    even = here % 2 == 0
    first, last = here == 0, here == NSUB - 1
    low = jnp.clip(margin[0, 0] - NS * jnp.maximum(here - 1, 0), 0, NS - 1)
    high = jnp.clip(margin[0, 1] - NS * jnp.minimum(here + 1, NSUB - 1), 0, NS - 1)
    table[EVEN] = jnp.where(even, 1, 0)
    table[FIRST] = jnp.where(first, 1, 0)
    table[LAST] = jnp.where(last, 1, 0)
    table[LOW] = low
    table[HIGH] = high
    table[COUNT] = counts[0]
    table[ENDS] = jnp.where(jnp.logical_or(first, last), 1, 0)
    table[NEXT] = jnp.where(jnp.logical_or(here == 1, here == NSUB - 2), 1, 0)
    table[OUT] = jnp.where(even, low, high)
    for s in range(NS):
        for k in range(NB):
            slot = jnp.clip(neighbours[s, k] - NS * (here - 1), 0, 3 * NS - 1)
            table[SLOTS + s * NB + k] = jnp.where(even, slot, slot + 2 * NS * (1 - slot // NS))


def coupling_kernel(blocks, groups, first, flat, *rest):
    if first:
        inverse, place, counts, margin, neighbours, c_ref, inverse_ref, table, raw, x, lo, hi, sems = rest
    else:
        _, c_ref, raw, x, lo, hi, sems = rest
    lanes = GROUP * W
    count = groups[1] - groups[0]
    step = CHUNK * lanes
    chunks = count // CHUNK
    copies = [
        pltpu.make_async_copy(
            flat.at[:, pl.ds(groups[0] * lanes + c * step, step)],
            raw.at[:, pl.ds(c * step, step)],
            sems.at[c],
        )
        for c in range(chunks)
    ]
    if first:
        copies.append(pltpu.make_async_copy(inverse.at[0], inverse_ref, sems.at[chunks]))
    for copy in copies:
        copy.start()
    if first:
        fill_table(table, place, counts, margin, neighbours)
    lane = lax.broadcasted_iota(jnp.int32, (4 * NS, 128), 1)

    def four(i, carry):
        for h in range(4):
            at = pl.multiple_of((4 * i + h) * lanes, 128)
            x[NS * h : NS * h + NS, :] = raw[:, pl.ds(at, lanes)]
        base = pl.multiple_of(4 * i * (GROUP * NS), 8)
        for s in range(GROUP):
            def rolled(t):
                piece = x[:, 128 * t : 128 * t + 128]
                return pltpu.roll(piece, 4 * s, 1) if s else piece

            middle = rolled(2 * s)
            if s == 0:
                left, right = middle, rolled(1)
            else:
                early = lane < 4 * s
                left = jnp.where(early, rolled(2 * s - 1), middle)
                right = jnp.where(early, middle, rolled(2 * s + 1)) if s < GROUP - 1 else middle
            left, right = left.astype(F32), right.astype(F32)
            for h in range(4):
                at = base + (h * GROUP + s) * NS
                lo[pl.ds(at, NS), :] = left[NS * h : NS * h + NS]
                hi[pl.ds(at, NS), :] = right[NS * h : NS * h + NS]
        return carry

    for c in range(chunks):
        copies[c].wait()
        lax.fori_loop(c * CHUNK // 4, (c + 1) * CHUNK // 4, four, 0)
    keep = lax.broadcasted_iota(jnp.int32, (WP, 128), 1) < W - 128
    pad = jnp.zeros((WP - W, 128), F32)
    skip = (blocks[0] * W - groups[0] * GROUP) * NS
    number = blocks[1] - blocks[0]

    def place(k, carry):
        for p in range(NS):
            row = skip + k * (W * NS) + p
            left = lo[pl.ds(row, W, stride=NS), :]
            right = hi[pl.ds(row, W, stride=NS), :]
            right = jnp.where(keep, jnp.concatenate([right, pad], axis=0), 0.0)
            c_ref[p * number + k, :, :128] = jnp.concatenate([left, pad], axis=0).astype(BF16)
            c_ref[p * number + k, :, 128:] = right.astype(BF16)
        return carry

    lax.fori_loop(0, number, place, 0)
    if first:
        copies[chunks].wait()


def own_kernel(inverse, own, part_ref, ext):
    for s in range(NS):
        ext[s * W : (s + 1) * W, :] = own[s, :W, :]
    ext[NS * W :, :] = jnp.zeros((OWN - NS * W, R), F32)
    part_ref[...] = jnp.dot(inverse[:, :OWN], ext[...].astype(BF16), preferred_element_type=F32)


def places(table):
    return table[EVEN] == 1, table[FIRST] == 1, table[LAST] == 1, table[LOW], table[HIGH]


def spilled(inverse, part, ext, block, index):
    begin = block * W // 16 * 16
    end = -(-(block + 1) * W // 16) * 16
    end = min(end, 6 * W)
    rows = jnp.dot(inverse[begin:end, FROM:], ext, preferred_element_type=F32)
    rows = rows[block * W - begin : (block + 1) * W - begin] + part[block * W : (block + 1) * W, :]
    mark = jnp.ones((WP - W, R), F32) * index.astype(F32)
    return jnp.concatenate([rows, mark], axis=0)


def margin_kernel(table, inverse, part, own, inner, outer, in_ref, ext_ref, ext):
    even, first, last, low, high = places(table)
    odd = jnp.logical_not(even)
    ext[: NS * W - FROM, :] = jnp.zeros((NS * W - FROM, R), F32)
    some = inner.shape[0] > 1

    def put(when, block, source, index):
        @pl.when(when)
        def _():
            ext[block * W - FROM : (block + 1) * W - FROM, :] = source[index].astype(F32)[:W]

    put(first, NS, own, low)
    put(jnp.logical_and(even, jnp.logical_not(first)), NS, outer, low if some else 0)
    put(odd, NS, inner, low if some else 0)
    put(last, NS + 1, own, high)
    put(jnp.logical_and(odd, jnp.logical_not(last)), NS + 1, outer, high if some else 0)
    put(even, NS + 1, inner, high if some else 0)
    ext_ref[...] = ext[...].astype(BF16)

    @pl.when(even)
    def _():
        in_ref[0] = spilled(inverse, part, ext_ref[...], NS + 1, high).astype(BF16)

    @pl.when(odd)
    def _():
        in_ref[0] = spilled(inverse, part, ext_ref[...], NS, low).astype(BF16)


def solve_kernel(table, inverse, part, ext, out_ref, out2_ref, res):
    even, first, last, low, high = places(table)
    mine = NS * W
    res[...] = part[:mine, :] + jnp.dot(inverse[:mine, FROM:], ext[...], preferred_element_type=F32)
    pad = jnp.zeros((WP - W, R), F32)
    for s in range(NS):
        out_ref[s] = jnp.concatenate([res[s * W : (s + 1) * W, :], pad], axis=0)
    keep = lax.broadcasted_iota(jnp.int32, (WP, R), 0) < W

    def spill(when, ends, block, index):
        @pl.when(when)
        def _():
            rows = spilled(inverse, part, ext[...], block, index)
            out2_ref[0] = rows.astype(BF16)

            @pl.when(ends)
            def _():
                out_ref[index] += jnp.where(keep, rows, 0.0)

    spill(even, first, NS, low)
    spill(jnp.logical_not(even), last, NS + 1, high)


def opened(block):
    x = block.astype(F32)
    rows = lax.broadcasted_iota(jnp.int32, x.shape, 0)
    return jnp.where(rows < W, x, 0.0), x[W : W + 1, :]


def inner_kernel(out, spill_in, spill_out, part_ref, sent_ref, near_ref):
    values, index = opened(spill_in[0])
    for s in range(NS):
        part = out[s] + jnp.where(index == s, values, 0.0)
        part_ref[s] = part
        sent_ref[s] = part.astype(BF16)
        near_ref[s] = part.astype(BF16)
    sent_ref[NS] = spill_out[0]


def system_kernel(
    first, table, ca, cb, part, got, near, far, spill_out, v0, *rest
):
    if first:
        p_ref, w_ref, wout_ref, sums_ref, u = rest
    else:
        w, p_ref, sums_ref, u = rest
    got_values, got_index = opened(got[NS])
    got_index = jnp.where(table[ENDS] == 1, -1.0, got_index)
    far_values, far_index = opened(far[0])
    far_index = jnp.where(table[NEXT] == 1, -1.0, far_index)
    count = table[COUNT]
    for s in range(NS):
        alive = jnp.where(count > s, 1.0, 0.0)
        p = (part[s] + jnp.where(got_index == s, got_values, 0.0)) * alive
        p_ref[s] = p
        u[s] = got[s]
        u[NS + s] = p.astype(BF16)
        u[2 * NS + s] = (near[s].astype(F32) + jnp.where(far_index == s, far_values, 0.0)).astype(BF16)
    index = table[OUT]
    u[index] = (got[index].astype(F32) + opened(spill_out[0])[0]).astype(BF16)
    sums_ref[...] = jnp.zeros((8, R), F32)
    if first:
        w_ref[...] = jnp.zeros((NS, WP, R), F32)

    def one(s):
        acc = p_ref[s]
        for k in range(NB):
            slot = table[SLOTS + s * NB + k]
            matrix = ca[s * SPLIT + k] if k < SPLIT else cb[s * (NB - SPLIT) + k - SPLIT]
            acc += jnp.dot(matrix, u[slot], preferred_element_type=F32)
        image = acc
        start = v0[s]
        if first:
            image = image - SHIFT * start
            w_ref[s] = image
            terms = (start * start, start * image, image * image)
        else:
            terms = (start * image, w[s] * image, image * image)
        sums = [jnp.sum(x, axis=0, keepdims=True) for x in terms]
        sums_ref[...] += jnp.concatenate(sums + [jnp.zeros((5, R), F32)], axis=0)

    for s in range(NS):
        pl.when(count > s)(functools.partial(one, s))
    if first:
        picked(wout_ref, w_ref, got_index)


def picked(ref, w, index):
    chosen = jnp.zeros((WP, R), F32)
    for s in range(NS):
        chosen = chosen + jnp.where(index == s, w[s], 0.0)
    ref[0] = chosen.astype(BF16)


def pick_kernel(w, spill_in, win_ref):
    picked(win_ref, w, opened(spill_in[0])[1])


def finish_kernel(gathered, p0, q, out):
    total = jnp.sum(gathered[...], axis=0)
    s00, s01, s11, s02, s12, s22 = (total[i : i + 1, :] for i in range(6))
    c = SHIFT
    bb = s00 + EPS
    beta = jnp.sqrt(bb)
    h11 = (s01 + c * s00) / bb
    a = c - h11
    n2 = (s11 + 2 * a * s01 + a * a * s00) / bb
    h21s = jnp.maximum(n2, 0.0) + EPS
    h21 = jnp.sqrt(h21s)
    full = bb * h21s
    v0i = s01 + c * s00
    h12 = (s02 + a * v0i) / (bb * h21)
    cross = (s01 + a * s00) / (bb * h21)
    b2i = (s12 + a * s02 + a * (s11 + c * s01) + a * a * v0i) / full
    h22 = b2i - h12 * cross
    ii = (s22 + 2 * a * (s12 + c * s02) + a * a * (s11 + 2 * c * s01 + c * c * s00)) / full
    rest = (
        ii + h12 * h12 * (s00 / bb) + h22 * h22 * (n2 / h21s)
        - 2 * h12 * h12 - 2 * h22 * b2i + 2 * h12 * h22 * cross
    )
    h32s = jnp.maximum(rest, 0.0) + EPS
    g00 = h11 * h11 + h21s
    g01 = h11 * h12 + h21 * h22
    g11 = h12 * h12 + h22 * h22 + h32s
    det = g00 * g11 - g01 * g01
    y1 = beta * (g11 * h11 - g01 * h12) / det
    y2 = beta * (g00 * h12 - g01 * h11) / det
    two = y2 / (beta * h21)
    one = y1 / beta + a * two
    for s in range(NS):
        out[pl.ds(s, W, stride=NS), :] = one * p0[s, :W, :] + two * q[s, :W, :]


def permuted(x, target):
    parts = lax.axis_size("rhs")
    pairs = [(i, j) for i in range(NSUB) for j in range(parts)]
    return lax.ppermute(
        x, ("sub", "rhs"), [(i * parts + j, t[0] * parts + t[1]) for i, j in pairs for t in [target(i, j)]]
    )


def to_inner(x):
    return permuted(x, lambda i, j: (i ^ 1, j))


def to_outer(x):
    return permuted(x, lambda i, j: (i, j ^ 1) if i in (0, NSUB - 1) else (((i + 1) ^ 1) - 1, j))


def to_far(x):
    def target(i, j):
        if i in (0, NSUB - 1):
            return i ^ 1, j
        return i + (2 if i % 2 else -2), j

    return permuted(x, target)


def body(right_side, coupling, neighbours, inverse, margin, counts):
    here = lax.axis_index("sub").astype(jnp.int32).reshape(1)
    flat_right = right_side.transpose(1, 0, 2).reshape(W * NS, R)
    block, one = (NS, WP, R), (1, WP, R)
    v0, v0b = call(start_kernel, [(block, F32), (block, BF16)], [SM, VM])(counts, flat_right)
    outer, inner = to_outer(v0b), to_inner(v0b)

    coupling = pltpu.with_memory_space_constraint(coupling, pltpu.HBM)
    inverse, margin, neighbours = (
        pltpu.with_memory_space_constraint(a, pltpu.HBM) for a in (inverse, margin, neighbours)
    )

    def matrices(first, *more):
        lanes = GROUP * W
        blocks = (0, SPLIT) if first else (SPLIT, NB)
        begin = blocks[0] * W // GROUP
        end = -(-blocks[1] * W // GROUP)
        count = -(-(end - begin) // CHUNK) * CHUNK
        groups = (begin, begin + count) if first else (end - count, end)
        outs = [((NS * (blocks[1] - blocks[0]), WP, WP), BF16, pltpu.VMEM)]
        if first:
            outs += [((6 * W, 6 * W), BF16, pltpu.VMEM), ((TABLE,), jnp.int32, pltpu.SMEM)]
        return call(
            functools.partial(coupling_kernel, blocks, groups, first),
            outs,
            [ANY, ANY] + [SM] * (len(more) - 1),
            [
                pltpu.VMEM((NS, count * lanes), BF16),
                pltpu.VMEM((4 * NS, lanes), BF16),
                pltpu.VMEM((count * GROUP * NS, 128), F32),
                pltpu.VMEM((count * GROUP * NS, 128), F32),
                pltpu.SemaphoreType.DMA((count // CHUNK + 1,)),
            ],
            limit=24,
            cost=pl.CostEstimate(flops=1 << 20, bytes_accessed=12 << 20, transcendentals=0),
        )(coupling, *more)

    first_part, held, table = matrices(True, inverse, here, counts, margin, neighbours)
    table = pltpu.with_memory_space_constraint(table, pltpu.SMEM)
    held = pltpu.with_memory_space_constraint(held, pltpu.VMEM)
    first_part = pltpu.with_memory_space_constraint(first_part, pltpu.VMEM)

    def solve(own, inner, outer):
        (part,) = call(
            own_kernel, [((6 * W, R), F32, pltpu.VMEM)], [VM, VM], [pltpu.VMEM((OWN, R), F32)],
            cost=pl.CostEstimate(flops=1 << 30, bytes_accessed=4 << 20, transcendentals=0),
        )(held, own)
        depth = 6 * W - FROM
        spill_in, ext = call(
            margin_kernel,
            [(one, BF16), ((depth, R), BF16)],
            [SM] + [VM] * 5,
            [pltpu.VMEM((depth, R), F32)],
        )(table, held, part, own, inner, outer)
        got_in = to_inner(spill_in)
        out, spill_out = call(
            solve_kernel,
            [(block, F32), (one, BF16)],
            [SM] + [VM] * 3,
            [pltpu.VMEM((NS * W, R), F32)],
            cost=pl.CostEstimate(flops=1 << 30, bytes_accessed=4 << 20, transcendentals=0),
        )(table, held, part, ext)
        return out, got_in, spill_out

    def system(first, out, got_in, spill_out, *more):
        part, sent, near = call(
            inner_kernel, [(block, F32), ((NS + 1, WP, R), BF16), (block, BF16)], [VM] * 3
        )(out, got_in, spill_out)
        got, near, far = to_outer(sent), to_inner(near), to_far(spill_out)
        if first:
            (made,) = matrices(False, sent)
            matrix_parts.append(pltpu.with_memory_space_constraint(made, pltpu.VMEM))
        outs = [(block, F32)] + ([(block, F32), (one, BF16)] if first else [])
        return call(
            functools.partial(system_kernel, first),
            outs + [((8, R), F32)],
            [SM] + [VM] * (7 + len(more)),
            [pltpu.VMEM((3 * NS, WP, R), BF16)],
        )(table, *matrix_parts, part, got, near, far, spill_out, *more)

    matrix_parts = [first_part]
    out, got_in, spill_out = solve(v0, inner, outer)
    p0, w, w_out, sums_one = system(True, out, got_in, spill_out, v0)
    outer = to_outer(w_out)
    (w_in,) = call(pick_kernel, [(one, BF16)], [VM] * 2)(w, got_in)
    q, sums_two = system(False, *solve(w, to_inner(w_in), outer), v0, w)
    sums = jnp.concatenate([sums_one[:3], sums_two[:3]], axis=0)
    sums = sums + to_inner(sums)
    gathered = lax.all_to_all(
        jnp.broadcast_to(sums[None], (NSUB // 2, 6, R)), "sub", 0, 0,
        axis_index_groups=[list(range(c, NSUB, 2)) for c in range(2)],
    )
    (flat,) = call(finish_kernel, [((W * NS, R), F32)], [VM] * 3)(gathered, p0, q)
    return flat.reshape(W, NS, R).transpose(1, 0, 2)


def solution(mesh):
    placed = (
        P("sub", None, "rhs"),
        P("sub", None),
        P("sub", None),
        P("sub", None, None),
        P("sub", None),
        P("sub"),
    )
    return jax.shard_map(
        body, mesh=mesh, in_specs=placed, out_specs=P("sub", None, "rhs"), check_vma=False
    )
```

```python
import functools
import jax
import jax.numpy as jnp
from jax import lax
from jax.experimental import pallas as pl
from jax.experimental.pallas import tpu as pltpu
from jax.sharding import PartitionSpec as P

EPS = 1e-06
W = 252
WP = 256
NS = 4
NB = 8
R = 128
NSUB = 64
SHIFT = 1.0
ROWS = NB * W
GROUP = 32
F32 = jnp.float32
BF16 = jnp.bfloat16
CHUNK = 8
SPLIT = 4
EVEN, FIRST, LAST, LOW, HIGH, COUNT, ENDS, NEXT, OUT, SLOTS = range(10)
TABLE = SLOTS + NS * NB
OWN = 1024
FROM = 896
ANY = pl.BlockSpec(memory_space=pl.ANY)
PARTS = ((0, 64), (64, 64), (128, 64), (192, 60))
VM = pl.BlockSpec(memory_space=pltpu.VMEM)
SM = pl.BlockSpec(memory_space=pltpu.SMEM)


def call(kernel, outs, ins, scratch=(), limit=24, cost=None):
    return pl.pallas_call(
        kernel,
        out_shape=[keep[0](s, d) if keep else jax.ShapeDtypeStruct(s, d) for s, d, *keep in outs],
        in_specs=ins,
        out_specs=[{pltpu.SMEM: SM, pltpu.HBM: ANY}.get(keep[0], VM) if keep else VM for _, _, *keep in outs],
        scratch_shapes=list(scratch),
        compiler_params=pltpu.CompilerParams(vmem_limit_bytes=limit << 20),
        cost_estimate=cost,
    )


def start_kernel(counts, right, v0_ref, v0b_ref, rows, sems):
    copies = []
    for begin, size in PARTS:
        part = pl.ds(begin * NS, size * NS)
        copies.append(pltpu.make_async_copy(right.at[part, :], rows.at[part, :], sems.at[len(copies)]))
        copies[-1].start()
    for (begin, size), copy in zip(PARTS, copies):
        copy.wait()
        for s in range(NS):
            alive = jnp.where(counts[0] > s, 1.0, 0.0)
            block = rows[pl.ds(begin * NS + s, size, stride=NS), :] * alive
            if begin + size == W:
                block = jnp.concatenate([block, jnp.zeros((WP - W, R), F32)], axis=0)
            v0_ref[s, begin : begin + block.shape[0], :] = block
            v0b_ref[s, begin : begin + block.shape[0], :] = block.astype(BF16)


def fill_table(table, place, counts, margin, neighbours):
    here = place[0]
    even = here % 2 == 0
    first, last = here == 0, here == NSUB - 1
    low = jnp.clip(margin[0, 0] - NS * jnp.maximum(here - 1, 0), 0, NS - 1)
    high = jnp.clip(margin[0, 1] - NS * jnp.minimum(here + 1, NSUB - 1), 0, NS - 1)
    table[EVEN] = jnp.where(even, 1, 0)
    table[FIRST] = jnp.where(first, 1, 0)
    table[LAST] = jnp.where(last, 1, 0)
    table[LOW] = low
    table[HIGH] = high
    table[COUNT] = counts[0]
    table[ENDS] = jnp.where(jnp.logical_or(first, last), 1, 0)
    table[NEXT] = jnp.where(jnp.logical_or(here == 1, here == NSUB - 2), 1, 0)
    table[OUT] = jnp.where(even, low, high)
    for s in range(NS):
        for k in range(NB):
            slot = jnp.clip(neighbours[s, k] - NS * (here - 1), 0, 3 * NS - 1)
            table[SLOTS + s * NB + k] = jnp.where(even, slot, slot + 2 * NS * (1 - slot // NS))


def coupling_kernel(blocks, groups, first, flat, *rest):
    if first:
        inverse, place, counts, margin, neighbours, c_ref, inverse_ref, table, raw, x, lo, hi, sems = rest
    else:
        _, c_ref, raw, x, lo, hi, sems = rest
    lanes = GROUP * W
    count = groups[1] - groups[0]
    step = CHUNK * lanes
    chunks = count // CHUNK
    copies = [
        pltpu.make_async_copy(
            flat.at[:, pl.ds(groups[0] * lanes + c * step, step)],
            raw.at[:, pl.ds(c * step, step)],
            sems.at[c],
        )
        for c in range(chunks)
    ]
    if first:
        copies.append(pltpu.make_async_copy(inverse.at[0], inverse_ref, sems.at[chunks]))
    for copy in copies:
        copy.start()
    if first:
        fill_table(table, place, counts, margin, neighbours)
    lane = lax.broadcasted_iota(jnp.int32, (4 * NS, 128), 1)

    def four(i, carry):
        for h in range(4):
            at = pl.multiple_of((4 * i + h) * lanes, 128)
            x[NS * h : NS * h + NS, :] = raw[:, pl.ds(at, lanes)]
        base = pl.multiple_of(4 * i * (GROUP * NS), 8)
        for s in range(GROUP):
            def rolled(t):
                piece = x[:, 128 * t : 128 * t + 128]
                return pltpu.roll(piece, 4 * s, 1) if s else piece

            middle = rolled(2 * s)
            if s == 0:
                left, right = middle, rolled(1)
            else:
                early = lane < 4 * s
                left = jnp.where(early, rolled(2 * s - 1), middle)
                right = jnp.where(early, middle, rolled(2 * s + 1)) if s < GROUP - 1 else middle
            left, right = left.astype(F32), right.astype(F32)
            for h in range(4):
                at = base + (h * GROUP + s) * NS
                lo[pl.ds(at, NS), :] = left[NS * h : NS * h + NS]
                hi[pl.ds(at, NS), :] = right[NS * h : NS * h + NS]
        return carry

    for c in range(chunks):
        copies[c].wait()
        lax.fori_loop(c * CHUNK // 4, (c + 1) * CHUNK // 4, four, 0)
    keep = lax.broadcasted_iota(jnp.int32, (WP, 128), 1) < W - 128
    pad = jnp.zeros((WP - W, 128), F32)
    skip = (blocks[0] * W - groups[0] * GROUP) * NS
    number = blocks[1] - blocks[0]

    def place(k, carry):
        for p in range(NS):
            row = skip + k * (W * NS) + p
            left = lo[pl.ds(row, W, stride=NS), :]
            right = hi[pl.ds(row, W, stride=NS), :]
            right = jnp.where(keep, jnp.concatenate([right, pad], axis=0), 0.0)
            c_ref[p * number + k, :, :128] = jnp.concatenate([left, pad], axis=0).astype(BF16)
            c_ref[p * number + k, :, 128:] = right.astype(BF16)
        return carry

    lax.fori_loop(0, number, place, 0)
    if first:
        copies[chunks].wait()


def own_kernel(inverse, own, part_ref, ext):
    for s in range(NS):
        ext[s * W : (s + 1) * W, :] = own[s, :W, :]
    ext[NS * W :, :] = jnp.zeros((OWN - NS * W, R), F32)
    part_ref[...] = jnp.dot(inverse[:, :OWN], ext[...].astype(BF16), preferred_element_type=F32)


def places(table):
    return table[EVEN] == 1, table[FIRST] == 1, table[LAST] == 1, table[LOW], table[HIGH]


def spilled(inverse, part, ext, block, index):
    begin = block * W // 16 * 16
    end = -(-(block + 1) * W // 16) * 16
    end = min(end, 6 * W)
    rows = jnp.dot(inverse[begin:end, FROM:], ext, preferred_element_type=F32)
    rows = rows[block * W - begin : (block + 1) * W - begin] + part[block * W : (block + 1) * W, :]
    mark = jnp.ones((WP - W, R), F32) * index.astype(F32)
    return jnp.concatenate([rows, mark], axis=0)


def margin_kernel(table, inverse, part, own, inner, outer, in_ref, ext_ref, ext):
    even, first, last, low, high = places(table)
    odd = jnp.logical_not(even)
    ext[: NS * W - FROM, :] = jnp.zeros((NS * W - FROM, R), F32)
    some = inner.shape[0] > 1

    def put(when, block, source, index):
        @pl.when(when)
        def _():
            ext[block * W - FROM : (block + 1) * W - FROM, :] = source[index].astype(F32)[:W]

    put(first, NS, own, low)
    put(jnp.logical_and(even, jnp.logical_not(first)), NS, outer, low if some else 0)
    put(odd, NS, inner, low if some else 0)
    put(last, NS + 1, own, high)
    put(jnp.logical_and(odd, jnp.logical_not(last)), NS + 1, outer, high if some else 0)
    put(even, NS + 1, inner, high if some else 0)
    ext_ref[...] = ext[...].astype(BF16)

    @pl.when(even)
    def _():
        in_ref[0] = spilled(inverse, part, ext_ref[...], NS + 1, high).astype(BF16)

    @pl.when(odd)
    def _():
        in_ref[0] = spilled(inverse, part, ext_ref[...], NS, low).astype(BF16)


def solve_kernel(table, inverse, part, ext, out_ref, out2_ref, res):
    even, first, last, low, high = places(table)
    mine = NS * W
    res[...] = part[:mine, :] + jnp.dot(inverse[:mine, FROM:], ext[...], preferred_element_type=F32)
    pad = jnp.zeros((WP - W, R), F32)
    for s in range(NS):
        out_ref[s] = jnp.concatenate([res[s * W : (s + 1) * W, :], pad], axis=0)
    keep = lax.broadcasted_iota(jnp.int32, (WP, R), 0) < W

    def spill(when, ends, block, index):
        @pl.when(when)
        def _():
            rows = spilled(inverse, part, ext[...], block, index)
            out2_ref[0] = rows.astype(BF16)

            @pl.when(ends)
            def _():
                out_ref[index] += jnp.where(keep, rows, 0.0)

    spill(even, first, NS, low)
    spill(jnp.logical_not(even), last, NS + 1, high)


def opened(block):
    x = block.astype(F32)
    rows = lax.broadcasted_iota(jnp.int32, x.shape, 0)
    return jnp.where(rows < W, x, 0.0), x[W : W + 1, :]


def inner_kernel(out, spill_in, spill_out, part_ref, sent_ref, near_ref):
    values, index = opened(spill_in[0])
    for s in range(NS):
        part = out[s] + jnp.where(index == s, values, 0.0)
        part_ref[s] = part
        sent_ref[s] = part.astype(BF16)
        near_ref[s] = part.astype(BF16)
    sent_ref[NS] = spill_out[0]


def system_kernel(
    first, table, ca, cb, part, got, near, far, spill_out, v0, *rest
):
    if first:
        p_ref, w_ref, wout_ref, sums_ref, u = rest
    else:
        w, p_ref, sums_ref, u = rest
    got_values, got_index = opened(got[NS])
    got_index = jnp.where(table[ENDS] == 1, -1.0, got_index)
    far_values, far_index = opened(far[0])
    far_index = jnp.where(table[NEXT] == 1, -1.0, far_index)
    count = table[COUNT]
    for s in range(NS):
        alive = jnp.where(count > s, 1.0, 0.0)
        p = (part[s] + jnp.where(got_index == s, got_values, 0.0)) * alive
        p_ref[s] = p
        u[s] = got[s]
        u[NS + s] = p.astype(BF16)
        u[2 * NS + s] = (near[s].astype(F32) + jnp.where(far_index == s, far_values, 0.0)).astype(BF16)
    index = table[OUT]
    u[index] = (got[index].astype(F32) + opened(spill_out[0])[0]).astype(BF16)
    sums_ref[...] = jnp.zeros((8, R), F32)
    if first:
        w_ref[...] = jnp.zeros((NS, WP, R), F32)

    def one(s):
        acc = p_ref[s]
        for k in range(NB):
            slot = table[SLOTS + s * NB + k]
            matrix = ca[s * SPLIT + k] if k < SPLIT else cb[s * (NB - SPLIT) + k - SPLIT]
            acc += jnp.dot(matrix, u[slot], preferred_element_type=F32)
        image = acc
        start = v0[s]
        if first:
            image = image - SHIFT * start
            w_ref[s] = image
            terms = (start * start, start * image, image * image)
        else:
            terms = (start * image, w[s] * image, image * image)
        sums = [jnp.sum(x, axis=0, keepdims=True) for x in terms]
        sums_ref[...] += jnp.concatenate(sums + [jnp.zeros((5, R), F32)], axis=0)

    for s in range(NS):
        pl.when(count > s)(functools.partial(one, s))
    if first:
        picked(wout_ref, w_ref, got_index)


def picked(ref, w, index):
    chosen = jnp.zeros((WP, R), F32)
    for s in range(NS):
        chosen = chosen + jnp.where(index == s, w[s], 0.0)
    ref[0] = chosen.astype(BF16)


def pick_kernel(w, spill_in, win_ref):
    picked(win_ref, w, opened(spill_in[0])[1])


def finish_kernel(gathered, p0, q, out_ref, out, sems):
    total = jnp.sum(gathered[...], axis=0)
    s00, s01, s11, s02, s12, s22 = (total[i : i + 1, :] for i in range(6))
    c = SHIFT
    bb = s00 + EPS
    beta = jnp.sqrt(bb)
    h11 = (s01 + c * s00) / bb
    a = c - h11
    n2 = (s11 + 2 * a * s01 + a * a * s00) / bb
    h21s = jnp.maximum(n2, 0.0) + EPS
    h21 = jnp.sqrt(h21s)
    full = bb * h21s
    v0i = s01 + c * s00
    h12 = (s02 + a * v0i) / (bb * h21)
    cross = (s01 + a * s00) / (bb * h21)
    b2i = (s12 + a * s02 + a * (s11 + c * s01) + a * a * v0i) / full
    h22 = b2i - h12 * cross
    ii = (s22 + 2 * a * (s12 + c * s02) + a * a * (s11 + 2 * c * s01 + c * c * s00)) / full
    rest = (
        ii + h12 * h12 * (s00 / bb) + h22 * h22 * (n2 / h21s)
        - 2 * h12 * h12 - 2 * h22 * b2i + 2 * h12 * h22 * cross
    )
    h32s = jnp.maximum(rest, 0.0) + EPS
    g00 = h11 * h11 + h21s
    g01 = h11 * h12 + h21 * h22
    g11 = h12 * h12 + h22 * h22 + h32s
    det = g00 * g11 - g01 * g01
    y1 = beta * (g11 * h11 - g01 * h12) / det
    y2 = beta * (g00 * h12 - g01 * h11) / det
    two = y2 / (beta * h21)
    one = y1 / beta + a * two
    copies = []
    for begin, size in PARTS:
        for s in range(NS):
            p, r = p0[s, begin : begin + size, :], q[s, begin : begin + size, :]
            out[pl.ds(begin * NS + s, size, stride=NS), :] = one * p + two * r
        rows = pl.ds(begin * NS, size * NS)
        copies.append(pltpu.make_async_copy(out.at[rows, :], out_ref.at[rows, :], sems.at[len(copies)]))
        copies[-1].start()
    for copy in copies:
        copy.wait()


def permuted(x, target):
    parts = lax.axis_size("rhs")
    pairs = [(i, j) for i in range(NSUB) for j in range(parts)]
    return lax.ppermute(
        x, ("sub", "rhs"), [(i * parts + j, t[0] * parts + t[1]) for i, j in pairs for t in [target(i, j)]]
    )


def to_inner(x):
    return permuted(x, lambda i, j: (i ^ 1, j))


def to_outer(x):
    return permuted(x, lambda i, j: (i, j ^ 1) if i in (0, NSUB - 1) else (((i + 1) ^ 1) - 1, j))


def to_far(x):
    def target(i, j):
        if i in (0, NSUB - 1):
            return i ^ 1, j
        return i + (2 if i % 2 else -2), j

    return permuted(x, target)


def body(right_side, coupling, neighbours, inverse, margin, counts):
    here = lax.axis_index("sub").astype(jnp.int32).reshape(1)
    flat_right = right_side.transpose(1, 0, 2).reshape(W * NS, R)
    block, one = (NS, WP, R), (1, WP, R)
    flat_right = pltpu.with_memory_space_constraint(flat_right, pltpu.HBM)
    v0, v0b = call(
        start_kernel,
        [(block, F32), (block, BF16)],
        [SM, ANY],
        [pltpu.VMEM((W * NS, R), F32), pltpu.SemaphoreType.DMA((len(PARTS),))],
    )(counts, flat_right)
    outer, inner = to_outer(v0b), to_inner(v0b)

    coupling = pltpu.with_memory_space_constraint(coupling, pltpu.HBM)
    inverse, margin, neighbours = (
        pltpu.with_memory_space_constraint(a, pltpu.HBM) for a in (inverse, margin, neighbours)
    )

    def matrices(first, *more):
        lanes = GROUP * W
        blocks = (0, SPLIT) if first else (SPLIT, NB)
        begin = blocks[0] * W // GROUP
        end = -(-blocks[1] * W // GROUP)
        count = -(-(end - begin) // CHUNK) * CHUNK
        groups = (begin, begin + count) if first else (end - count, end)
        outs = [((NS * (blocks[1] - blocks[0]), WP, WP), BF16, pltpu.VMEM)]
        if first:
            outs += [((6 * W, 6 * W), BF16, pltpu.VMEM), ((TABLE,), jnp.int32, pltpu.SMEM)]
        return call(
            functools.partial(coupling_kernel, blocks, groups, first),
            outs,
            [ANY, ANY] + [SM] * (len(more) - 1),
            [
                pltpu.VMEM((NS, count * lanes), BF16),
                pltpu.VMEM((4 * NS, lanes), BF16),
                pltpu.VMEM((count * GROUP * NS, 128), F32),
                pltpu.VMEM((count * GROUP * NS, 128), F32),
                pltpu.SemaphoreType.DMA((count // CHUNK + 1,)),
            ],
            limit=24,
            cost=pl.CostEstimate(flops=1 << 20, bytes_accessed=12 << 20, transcendentals=0),
        )(coupling, *more)

    first_part, held, table = matrices(True, inverse, here, counts, margin, neighbours)
    table = pltpu.with_memory_space_constraint(table, pltpu.SMEM)
    held = pltpu.with_memory_space_constraint(held, pltpu.VMEM)
    first_part = pltpu.with_memory_space_constraint(first_part, pltpu.VMEM)

    def solve(own, inner, outer):
        (part,) = call(
            own_kernel, [((6 * W, R), F32, pltpu.VMEM)], [VM, VM], [pltpu.VMEM((OWN, R), F32)],
            cost=pl.CostEstimate(flops=1 << 30, bytes_accessed=4 << 20, transcendentals=0),
        )(held, own)
        depth = 6 * W - FROM
        spill_in, ext = call(
            margin_kernel,
            [(one, BF16), ((depth, R), BF16)],
            [SM] + [VM] * 5,
            [pltpu.VMEM((depth, R), F32)],
        )(table, held, part, own, inner, outer)
        got_in = to_inner(spill_in)
        out, spill_out = call(
            solve_kernel,
            [(block, F32), (one, BF16)],
            [SM] + [VM] * 3,
            [pltpu.VMEM((NS * W, R), F32)],
            cost=pl.CostEstimate(flops=1 << 30, bytes_accessed=4 << 20, transcendentals=0),
        )(table, held, part, ext)
        return out, got_in, spill_out

    def system(first, out, got_in, spill_out, *more):
        part, sent, near = call(
            inner_kernel, [(block, F32), ((NS + 1, WP, R), BF16), (block, BF16)], [VM] * 3
        )(out, got_in, spill_out)
        got, near, far = to_outer(sent), to_inner(near), to_far(spill_out)
        if first:
            (made,) = matrices(False, sent)
            matrix_parts.append(pltpu.with_memory_space_constraint(made, pltpu.VMEM))
        outs = [(block, F32)] + ([(block, F32), (one, BF16)] if first else [])
        return call(
            functools.partial(system_kernel, first),
            outs + [((8, R), F32)],
            [SM] + [VM] * (7 + len(more)),
            [pltpu.VMEM((3 * NS, WP, R), BF16)],
        )(table, *matrix_parts, part, got, near, far, spill_out, *more)

    matrix_parts = [first_part]
    out, got_in, spill_out = solve(v0, inner, outer)
    p0, w, w_out, sums_one = system(True, out, got_in, spill_out, v0)
    outer = to_outer(w_out)
    (w_in,) = call(pick_kernel, [(one, BF16)], [VM] * 2)(w, got_in)
    q, sums_two = system(False, *solve(w, to_inner(w_in), outer), v0, w)
    sums = jnp.concatenate([sums_one[:3], sums_two[:3]], axis=0)
    sums = sums + to_inner(sums)
    gathered = lax.all_to_all(
        jnp.broadcast_to(sums[None], (NSUB // 2, 6, R)), "sub", 0, 0,
        axis_index_groups=[list(range(c, NSUB, 2)) for c in range(2)],
    )
    (flat,) = call(
        finish_kernel,
        [((W * NS, R), F32, pltpu.HBM)],
        [VM] * 3,
        [pltpu.VMEM((W * NS, R), F32), pltpu.SemaphoreType.DMA((len(PARTS),))],
    )(gathered, p0, q)
    return flat.reshape(W, NS, R).transpose(1, 0, 2)


def solution(mesh):
    placed = (
        P("sub", None, "rhs"),
        P("sub", None),
        P("sub", None),
        P("sub", None, None),
        P("sub", None),
        P("sub"),
    )
    return jax.shard_map(
        body, mesh=mesh, in_specs=placed, out_specs=P("sub", None, "rhs"), check_vma=False
    )
```

```python
import functools
import jax
import jax.numpy as jnp
from jax import lax
from jax.experimental import pallas as pl
from jax.experimental.pallas import tpu as pltpu
from jax.sharding import PartitionSpec as P

EPS = 1e-06
W = 252
WP = 256
NS = 4
NB = 8
R = 128
NSUB = 64
SHIFT = 1.0
ROWS = NB * W
GROUP = 32
F32 = jnp.float32
BF16 = jnp.bfloat16
CHUNK = 8
SPLIT = 4
EVEN, FIRST, LAST, LOW, HIGH, COUNT, ENDS, NEXT, OUT, SLOTS = range(10)
TABLE = SLOTS + NS * NB
FAR_WEIGHT = 2450000000
OWN = 1024
FROM = 896
ANY = pl.BlockSpec(memory_space=pl.ANY)
PARTS = ((0, 64), (64, 64), (128, 64), (192, 60))
VM = pl.BlockSpec(memory_space=pltpu.VMEM)
SM = pl.BlockSpec(memory_space=pltpu.SMEM)


def call(kernel, outs, ins, scratch=(), limit=24, cost=None):
    return pl.pallas_call(
        kernel,
        out_shape=[keep[0](s, d) if keep else jax.ShapeDtypeStruct(s, d) for s, d, *keep in outs],
        in_specs=ins,
        out_specs=[{pltpu.SMEM: SM, pltpu.HBM: ANY}.get(keep[0], VM) if keep else VM for _, _, *keep in outs],
        scratch_shapes=list(scratch),
        compiler_params=pltpu.CompilerParams(vmem_limit_bytes=limit << 20),
        cost_estimate=cost,
    )


def start_kernel(counts, right, v0_ref, v0b_ref):
    for s in range(NS):
        alive = jnp.where(counts[0] > s, 1.0, 0.0)
        v0_ref[s, :W, :] = right[pl.ds(s, W, stride=NS), :] * alive
        v0_ref[s, W:, :] = jnp.zeros((WP - W, R), F32)
        v0b_ref[s] = v0_ref[s].astype(BF16)


def fill_table(table, place, counts, margin, neighbours):
    here = place[0]
    even = here % 2 == 0
    first, last = here == 0, here == NSUB - 1
    low = jnp.clip(margin[0, 0] - NS * jnp.maximum(here - 1, 0), 0, NS - 1)
    high = jnp.clip(margin[0, 1] - NS * jnp.minimum(here + 1, NSUB - 1), 0, NS - 1)
    table[EVEN] = jnp.where(even, 1, 0)
    table[FIRST] = jnp.where(first, 1, 0)
    table[LAST] = jnp.where(last, 1, 0)
    table[LOW] = low
    table[HIGH] = high
    table[COUNT] = counts[0]
    table[ENDS] = jnp.where(jnp.logical_or(first, last), 1, 0)
    table[NEXT] = jnp.where(jnp.logical_or(here == 1, here == NSUB - 2), 1, 0)
    table[OUT] = jnp.where(even, low, high)
    for s in range(NS):
        for k in range(NB):
            slot = jnp.clip(neighbours[s, k] - NS * (here - 1), 0, 3 * NS - 1)
            table[SLOTS + s * NB + k] = jnp.where(even, slot, slot + 2 * NS * (1 - slot // NS))


def coupling_kernel(blocks, groups, first, flat, *rest):
    if first:
        inverse, place, counts, margin, neighbours, c_ref, inverse_ref, table, raw, x, lo, hi, sems = rest
    else:
        _, c_ref, raw, x, lo, hi, sems = rest
    lanes = GROUP * W
    count = groups[1] - groups[0]
    step = CHUNK * lanes
    chunks = count // CHUNK
    copies = [
        pltpu.make_async_copy(
            flat.at[:, pl.ds(groups[0] * lanes + c * step, step)],
            raw.at[:, pl.ds(c * step, step)],
            sems.at[c],
        )
        for c in range(chunks)
    ]
    if first:
        copies.append(pltpu.make_async_copy(inverse.at[0], inverse_ref, sems.at[chunks]))
    for copy in copies:
        copy.start()
    if first:
        fill_table(table, place, counts, margin, neighbours)
    lane = lax.broadcasted_iota(jnp.int32, (4 * NS, 128), 1)

    def four(i, carry):
        for h in range(4):
            at = pl.multiple_of((4 * i + h) * lanes, 128)
            x[NS * h : NS * h + NS, :] = raw[:, pl.ds(at, lanes)]
        base = pl.multiple_of(4 * i * (GROUP * NS), 8)
        for s in range(GROUP):
            def rolled(t):
                piece = x[:, 128 * t : 128 * t + 128]
                return pltpu.roll(piece, 4 * s, 1) if s else piece

            middle = rolled(2 * s)
            if s == 0:
                left, right = middle, rolled(1)
            else:
                early = lane < 4 * s
                left = jnp.where(early, rolled(2 * s - 1), middle)
                right = jnp.where(early, middle, rolled(2 * s + 1)) if s < GROUP - 1 else middle
            left, right = left.astype(F32), right.astype(F32)
            for h in range(4):
                at = base + (h * GROUP + s) * NS
                lo[pl.ds(at, NS), :] = left[NS * h : NS * h + NS]
                hi[pl.ds(at, NS), :] = right[NS * h : NS * h + NS]
        return carry

    for c in range(chunks):
        copies[c].wait()
        lax.fori_loop(c * CHUNK // 4, (c + 1) * CHUNK // 4, four, 0)
    keep = lax.broadcasted_iota(jnp.int32, (WP, 128), 1) < W - 128
    pad = jnp.zeros((WP - W, 128), F32)
    skip = (blocks[0] * W - groups[0] * GROUP) * NS
    number = blocks[1] - blocks[0]

    def place(k, carry):
        for p in range(NS):
            row = skip + k * (W * NS) + p
            left = lo[pl.ds(row, W, stride=NS), :]
            right = hi[pl.ds(row, W, stride=NS), :]
            right = jnp.where(keep, jnp.concatenate([right, pad], axis=0), 0.0)
            c_ref[p * number + k, :, :128] = jnp.concatenate([left, pad], axis=0).astype(BF16)
            c_ref[p * number + k, :, 128:] = right.astype(BF16)
        return carry

    lax.fori_loop(0, number, place, 0)
    if first:
        copies[chunks].wait()


def own_kernel(inverse, own, part_ref, ext):
    for s in range(NS):
        ext[s * W : (s + 1) * W, :] = own[s, :W, :]
    ext[NS * W :, :] = jnp.zeros((OWN - NS * W, R), F32)
    part_ref[...] = jnp.dot(inverse[:, :OWN], ext[...].astype(BF16), preferred_element_type=F32)


def places(table):
    return table[EVEN] == 1, table[FIRST] == 1, table[LAST] == 1, table[LOW], table[HIGH]


def spilled(inverse, part, ext, block, index):
    begin = block * W // 16 * 16
    end = -(-(block + 1) * W // 16) * 16
    end = min(end, 6 * W)
    rows = jnp.dot(inverse[begin:end, FROM:], ext, preferred_element_type=F32)
    rows = rows[block * W - begin : (block + 1) * W - begin] + part[block * W : (block + 1) * W, :]
    mark = jnp.ones((WP - W, R), F32) * index.astype(F32)
    return jnp.concatenate([rows, mark], axis=0)


def margin_kernel(table, inverse, part, own, inner, outer, in_ref, ext_ref, ext):
    even, first, last, low, high = places(table)
    odd = jnp.logical_not(even)
    ext[: NS * W - FROM, :] = jnp.zeros((NS * W - FROM, R), F32)
    some = inner.shape[0] > 1

    def put(when, block, source, index):
        @pl.when(when)
        def _():
            ext[block * W - FROM : (block + 1) * W - FROM, :] = source[index].astype(F32)[:W]

    put(first, NS, own, low)
    put(jnp.logical_and(even, jnp.logical_not(first)), NS, outer, low if some else 0)
    put(odd, NS, inner, low if some else 0)
    put(last, NS + 1, own, high)
    put(jnp.logical_and(odd, jnp.logical_not(last)), NS + 1, outer, high if some else 0)
    put(even, NS + 1, inner, high if some else 0)
    ext_ref[...] = ext[...].astype(BF16)

    @pl.when(even)
    def _():
        in_ref[0] = spilled(inverse, part, ext_ref[...], NS + 1, high).astype(BF16)

    @pl.when(odd)
    def _():
        in_ref[0] = spilled(inverse, part, ext_ref[...], NS, low).astype(BF16)


def solve_kernel(table, inverse, part, ext, out_ref, out2_ref, res):
    even, first, last, low, high = places(table)
    mine = NS * W
    res[...] = part[:mine, :] + jnp.dot(inverse[:mine, FROM:], ext[...], preferred_element_type=F32)
    pad = jnp.zeros((WP - W, R), F32)
    for s in range(NS):
        out_ref[s] = jnp.concatenate([res[s * W : (s + 1) * W, :], pad], axis=0)
    keep = lax.broadcasted_iota(jnp.int32, (WP, R), 0) < W

    def spill(when, ends, block, index):
        @pl.when(when)
        def _():
            rows = spilled(inverse, part, ext[...], block, index)
            out2_ref[0] = rows.astype(BF16)

            @pl.when(ends)
            def _():
                out_ref[index] += jnp.where(keep, rows, 0.0)

    spill(even, first, NS, low)
    spill(jnp.logical_not(even), last, NS + 1, high)


def opened(block):
    x = block.astype(F32)
    rows = lax.broadcasted_iota(jnp.int32, x.shape, 0)
    return jnp.where(rows < W, x, 0.0), x[W : W + 1, :]


def inner_kernel(out, spill_in, spill_out, part_ref, sent_ref, near_ref):
    values, index = opened(spill_in[0])
    for s in range(NS):
        part = out[s] + jnp.where(index == s, values, 0.0)
        part_ref[s] = part
        sent_ref[s] = part.astype(BF16)
        near_ref[s] = part.astype(BF16)
    sent_ref[NS] = spill_out[0]


def far_kernel(table, far, values_ref, mark_ref):
    values, index = opened(far[0])
    values_ref[...] = values
    mark_ref[...] = jnp.zeros((8, R), F32) + jnp.where(table[NEXT] == 1, -1.0, index)


def system_kernel(
    first, table, ca, cb, part, got, near, far, mark, spill_out, v0, *rest
):
    if first:
        p_ref, w_ref, wout_ref, sums_ref, u = rest
    else:
        w, p_ref, sums_ref, u = rest
    got_values, got_index = opened(got[NS])
    got_index = jnp.where(table[ENDS] == 1, -1.0, got_index)
    far_values, far_index = far[...], mark[0:1, :]
    count = table[COUNT]
    for s in range(NS):
        alive = jnp.where(count > s, 1.0, 0.0)
        p = (part[s] + jnp.where(got_index == s, got_values, 0.0)) * alive
        p_ref[s] = p
        u[s] = got[s]
        u[NS + s] = p.astype(BF16)
        u[2 * NS + s] = (near[s].astype(F32) + jnp.where(far_index == s, far_values, 0.0)).astype(BF16)
    index = table[OUT]
    u[index] = (got[index].astype(F32) + opened(spill_out[0])[0]).astype(BF16)
    sums_ref[...] = jnp.zeros((8, R), F32)
    if first:
        w_ref[...] = jnp.zeros((NS, WP, R), F32)

    def one(s):
        acc = p_ref[s]
        for k in range(NB):
            slot = table[SLOTS + s * NB + k]
            matrix = ca[s * SPLIT + k] if k < SPLIT else cb[s * (NB - SPLIT) + k - SPLIT]
            acc += jnp.dot(matrix, u[slot], preferred_element_type=F32)
        image = acc
        start = v0[s]
        if first:
            image = image - SHIFT * start
            w_ref[s] = image
            terms = (start * start, start * image, image * image)
        else:
            terms = (start * image, w[s] * image, image * image)
        sums = [jnp.sum(x, axis=0, keepdims=True) for x in terms]
        sums_ref[...] += jnp.concatenate(sums + [jnp.zeros((5, R), F32)], axis=0)

    for s in range(NS):
        pl.when(count > s)(functools.partial(one, s))
    if first:
        picked(wout_ref, w_ref, got_index)


def picked(ref, w, index):
    chosen = jnp.zeros((WP, R), F32)
    for s in range(NS):
        chosen = chosen + jnp.where(index == s, w[s], 0.0)
    ref[0] = chosen.astype(BF16)


def pick_kernel(w, spill_in, win_ref):
    picked(win_ref, w, opened(spill_in[0])[1])


def finish_kernel(gathered, p0, q, out_ref, out, sems):
    total = jnp.sum(gathered[...], axis=0)
    s00, s01, s11, s02, s12, s22 = (total[i : i + 1, :] for i in range(6))
    c = SHIFT
    bb = s00 + EPS
    beta = jnp.sqrt(bb)
    h11 = (s01 + c * s00) / bb
    a = c - h11
    n2 = (s11 + 2 * a * s01 + a * a * s00) / bb
    h21s = jnp.maximum(n2, 0.0) + EPS
    h21 = jnp.sqrt(h21s)
    full = bb * h21s
    v0i = s01 + c * s00
    h12 = (s02 + a * v0i) / (bb * h21)
    cross = (s01 + a * s00) / (bb * h21)
    b2i = (s12 + a * s02 + a * (s11 + c * s01) + a * a * v0i) / full
    h22 = b2i - h12 * cross
    ii = (s22 + 2 * a * (s12 + c * s02) + a * a * (s11 + 2 * c * s01 + c * c * s00)) / full
    rest = (
        ii + h12 * h12 * (s00 / bb) + h22 * h22 * (n2 / h21s)
        - 2 * h12 * h12 - 2 * h22 * b2i + 2 * h12 * h22 * cross
    )
    h32s = jnp.maximum(rest, 0.0) + EPS
    g00 = h11 * h11 + h21s
    g01 = h11 * h12 + h21 * h22
    g11 = h12 * h12 + h22 * h22 + h32s
    det = g00 * g11 - g01 * g01
    y1 = beta * (g11 * h11 - g01 * h12) / det
    y2 = beta * (g00 * h12 - g01 * h11) / det
    two = y2 / (beta * h21)
    one = y1 / beta + a * two
    copies = []
    for begin, size in PARTS:
        for s in range(NS):
            p, r = p0[s, begin : begin + size, :], q[s, begin : begin + size, :]
            out[pl.ds(begin * NS + s, size, stride=NS), :] = one * p + two * r
        rows = pl.ds(begin * NS, size * NS)
        copies.append(pltpu.make_async_copy(out.at[rows, :], out_ref.at[rows, :], sems.at[len(copies)]))
        copies[-1].start()
    for copy in copies:
        copy.wait()


def permuted(x, target):
    parts = lax.axis_size("rhs")
    pairs = [(i, j) for i in range(NSUB) for j in range(parts)]
    return lax.ppermute(
        x, ("sub", "rhs"), [(i * parts + j, t[0] * parts + t[1]) for i, j in pairs for t in [target(i, j)]]
    )


def to_inner(x):
    return permuted(x, lambda i, j: (i ^ 1, j))


def to_outer(x):
    return permuted(x, lambda i, j: (i, j ^ 1) if i in (0, NSUB - 1) else (((i + 1) ^ 1) - 1, j))


def to_far(x):
    def target(i, j):
        if i in (0, NSUB - 1):
            return i ^ 1, j
        return i + (2 if i % 2 else -2), j

    return permuted(x, target)


def body(right_side, coupling, neighbours, inverse, margin, counts):
    here = lax.axis_index("sub").astype(jnp.int32).reshape(1)
    flat_right = right_side.transpose(1, 0, 2).reshape(W * NS, R)
    block, one = (NS, WP, R), (1, WP, R)
    v0, v0b = call(start_kernel, [(block, F32), (block, BF16)], [SM, VM])(counts, flat_right)
    outer, inner = to_outer(v0b), to_inner(v0b)

    coupling = pltpu.with_memory_space_constraint(coupling, pltpu.HBM)
    inverse, margin, neighbours = (
        pltpu.with_memory_space_constraint(a, pltpu.HBM) for a in (inverse, margin, neighbours)
    )

    def matrices(first, *more):
        lanes = GROUP * W
        blocks = (0, SPLIT) if first else (SPLIT, NB)
        begin = blocks[0] * W // GROUP
        end = -(-blocks[1] * W // GROUP)
        count = -(-(end - begin) // CHUNK) * CHUNK
        groups = (begin, begin + count) if first else (end - count, end)
        outs = [((NS * (blocks[1] - blocks[0]), WP, WP), BF16, pltpu.VMEM)]
        if first:
            outs += [((6 * W, 6 * W), BF16, pltpu.VMEM), ((TABLE,), jnp.int32, pltpu.SMEM)]
        return call(
            functools.partial(coupling_kernel, blocks, groups, first),
            outs,
            [ANY, ANY] + [SM] * (len(more) - 1),
            [
                pltpu.VMEM((NS, count * lanes), BF16),
                pltpu.VMEM((4 * NS, lanes), BF16),
                pltpu.VMEM((count * GROUP * NS, 128), F32),
                pltpu.VMEM((count * GROUP * NS, 128), F32),
                pltpu.SemaphoreType.DMA((count // CHUNK + 1,)),
            ],
            limit=24,
            cost=pl.CostEstimate(flops=1 << 20, bytes_accessed=12 << 20, transcendentals=0),
        )(coupling, *more)

    first_part, held, table = matrices(True, inverse, here, counts, margin, neighbours)
    table = pltpu.with_memory_space_constraint(table, pltpu.SMEM)
    held = pltpu.with_memory_space_constraint(held, pltpu.VMEM)
    first_part = pltpu.with_memory_space_constraint(first_part, pltpu.VMEM)

    def solve(own, inner, outer):
        (part,) = call(
            own_kernel, [((6 * W, R), F32, pltpu.VMEM)], [VM, VM], [pltpu.VMEM((OWN, R), F32)],
            cost=pl.CostEstimate(flops=1 << 30, bytes_accessed=4 << 20, transcendentals=0),
        )(held, own)
        depth = 6 * W - FROM
        spill_in, ext = call(
            margin_kernel,
            [(one, BF16), ((depth, R), BF16)],
            [SM] + [VM] * 5,
            [pltpu.VMEM((depth, R), F32)],
        )(table, held, part, own, inner, outer)
        got_in = to_inner(spill_in)
        out, spill_out = call(
            solve_kernel,
            [(block, F32), (one, BF16)],
            [SM] + [VM] * 3,
            [pltpu.VMEM((NS * W, R), F32)],
            cost=pl.CostEstimate(flops=1 << 30, bytes_accessed=4 << 20, transcendentals=0),
        )(table, held, part, ext)
        return out, got_in, spill_out

    def system(first, out, got_in, spill_out, *more):
        part, sent, near = call(
            inner_kernel, [(block, F32), ((NS + 1, WP, R), BF16), (block, BF16)], [VM] * 3
        )(out, got_in, spill_out)
        got, near, far = to_outer(sent), to_inner(near), to_far(spill_out)
        far, mark = call(
            far_kernel,
            [((WP, R), F32), ((8, R), F32)],
            [SM, VM],
            cost=pl.CostEstimate(flops=FAR_WEIGHT, bytes_accessed=1 << 18, transcendentals=0),
        )(table, far)
        if first:
            (made,) = matrices(False, sent)
            matrix_parts.append(pltpu.with_memory_space_constraint(made, pltpu.VMEM))
        outs = [(block, F32)] + ([(block, F32), (one, BF16)] if first else [])
        return call(
            functools.partial(system_kernel, first),
            outs + [((8, R), F32)],
            [SM] + [VM] * (8 + len(more)),
            [pltpu.VMEM((3 * NS, WP, R), BF16)],
        )(table, *matrix_parts, part, got, near, far, mark, spill_out, *more)

    matrix_parts = [first_part]
    out, got_in, spill_out = solve(v0, inner, outer)
    p0, w, w_out, sums_one = system(True, out, got_in, spill_out, v0)
    outer = to_outer(w_out)
    (w_in,) = call(pick_kernel, [(one, BF16)], [VM] * 2)(w, got_in)
    q, sums_two = system(False, *solve(w, to_inner(w_in), outer), v0, w)
    sums = jnp.concatenate([sums_one[:3], sums_two[:3]], axis=0)
    sums = sums + to_inner(sums)
    gathered = lax.all_to_all(
        jnp.broadcast_to(sums[None], (NSUB // 2, 6, R)), "sub", 0, 0,
        axis_index_groups=[list(range(c, NSUB, 2)) for c in range(2)],
    )
    (flat,) = call(
        finish_kernel,
        [((W * NS, R), F32, pltpu.HBM)],
        [VM] * 3,
        [pltpu.VMEM((W * NS, R), F32), pltpu.SemaphoreType.DMA((len(PARTS),))],
    )(gathered, p0, q)
    return flat.reshape(W, NS, R).transpose(1, 0, 2)


def solution(mesh):
    placed = (
        P("sub", None, "rhs"),
        P("sub", None),
        P("sub", None),
        P("sub", None, None),
        P("sub", None),
        P("sub"),
    )
    return jax.shard_map(
        body, mesh=mesh, in_specs=placed, out_specs=P("sub", None, "rhs"), check_vma=False
    )
```

```python
import functools
import jax
import jax.numpy as jnp
from jax import lax
from jax.experimental import pallas as pl
from jax.experimental.pallas import tpu as pltpu
from jax.sharding import PartitionSpec as P

EPS = 1e-06
W = 252
WP = 256
NS = 4
NB = 8
R = 128
NSUB = 64
SHIFT = 1.0
ROWS = NB * W
GROUP = 32
F32 = jnp.float32
BF16 = jnp.bfloat16
CHUNK = 8
SPLIT = 4
EVEN, FIRST, LAST, LOW, HIGH, COUNT, ENDS, NEXT, OUT, SLOTS = range(10)
TABLE = SLOTS + NS * NB
OWN = 1024
FROM = 896
ANY = pl.BlockSpec(memory_space=pl.ANY)
PARTS = ((0, 64), (64, 64), (128, 64), (192, 60))
VM = pl.BlockSpec(memory_space=pltpu.VMEM)
SM = pl.BlockSpec(memory_space=pltpu.SMEM)


def call(kernel, outs, ins, scratch=(), limit=24, cost=None):
    return pl.pallas_call(
        kernel,
        out_shape=[keep[0](s, d) if keep else jax.ShapeDtypeStruct(s, d) for s, d, *keep in outs],
        in_specs=ins,
        out_specs=[{pltpu.SMEM: SM, pltpu.HBM: ANY}.get(keep[0], VM) if keep else VM for _, _, *keep in outs],
        scratch_shapes=list(scratch),
        compiler_params=pltpu.CompilerParams(vmem_limit_bytes=limit << 20),
        cost_estimate=cost,
    )


def start_kernel(counts, right, v0_ref, v0b_ref):
    for s in range(NS):
        alive = jnp.where(counts[0] > s, 1.0, 0.0)
        v0_ref[s, :W, :] = right[pl.ds(s, W, stride=NS), :] * alive
        v0_ref[s, W:, :] = jnp.zeros((WP - W, R), F32)
        v0b_ref[s] = v0_ref[s].astype(BF16)


def fill_table(table, place, counts, margin, neighbours):
    here = place[0]
    even = here % 2 == 0
    first, last = here == 0, here == NSUB - 1
    low = jnp.clip(margin[0, 0] - NS * jnp.maximum(here - 1, 0), 0, NS - 1)
    high = jnp.clip(margin[0, 1] - NS * jnp.minimum(here + 1, NSUB - 1), 0, NS - 1)
    table[EVEN] = jnp.where(even, 1, 0)
    table[FIRST] = jnp.where(first, 1, 0)
    table[LAST] = jnp.where(last, 1, 0)
    table[LOW] = low
    table[HIGH] = high
    table[COUNT] = counts[0]
    table[ENDS] = jnp.where(jnp.logical_or(first, last), 1, 0)
    table[NEXT] = jnp.where(jnp.logical_or(here == 1, here == NSUB - 2), 1, 0)
    table[OUT] = jnp.where(even, low, high)
    for s in range(NS):
        for k in range(NB):
            slot = jnp.clip(neighbours[s, k] - NS * (here - 1), 0, 3 * NS - 1)
            table[SLOTS + s * NB + k] = jnp.where(even, slot, slot + 2 * NS * (1 - slot // NS))


def coupling_kernel(blocks, groups, first, flat, *rest):
    if first:
        inverse, place, counts, margin, neighbours, c_ref, inverse_ref, table, raw, x, lo, hi, sems = rest
    else:
        _, c_ref, raw, x, lo, hi, sems = rest
    lanes = GROUP * W
    count = groups[1] - groups[0]
    step = CHUNK * lanes
    chunks = count // CHUNK
    copies = [
        pltpu.make_async_copy(
            flat.at[:, pl.ds(groups[0] * lanes + c * step, step)],
            raw.at[:, pl.ds(c * step, step)],
            sems.at[c],
        )
        for c in range(chunks)
    ]
    if first:
        copies.append(pltpu.make_async_copy(inverse.at[0], inverse_ref, sems.at[chunks]))
    for copy in copies:
        copy.start()
    if first:
        fill_table(table, place, counts, margin, neighbours)
    lane = lax.broadcasted_iota(jnp.int32, (4 * NS, 128), 1)

    def four(i, carry):
        for h in range(4):
            at = pl.multiple_of((4 * i + h) * lanes, 128)
            x[NS * h : NS * h + NS, :] = raw[:, pl.ds(at, lanes)]
        base = pl.multiple_of(4 * i * (GROUP * NS), 8)
        for s in range(GROUP):
            def rolled(t):
                piece = x[:, 128 * t : 128 * t + 128]
                return pltpu.roll(piece, 4 * s, 1) if s else piece

            middle = rolled(2 * s)
            if s == 0:
                left, right = middle, rolled(1)
            else:
                early = lane < 4 * s
                left = jnp.where(early, rolled(2 * s - 1), middle)
                right = jnp.where(early, middle, rolled(2 * s + 1)) if s < GROUP - 1 else middle
            left, right = left.astype(F32), right.astype(F32)
            for h in range(4):
                at = base + (h * GROUP + s) * NS
                lo[pl.ds(at, NS), :] = left[NS * h : NS * h + NS]
                hi[pl.ds(at, NS), :] = right[NS * h : NS * h + NS]
        return carry

    for c in range(chunks):
        copies[c].wait()
        lax.fori_loop(c * CHUNK // 4, (c + 1) * CHUNK // 4, four, 0)
    keep = lax.broadcasted_iota(jnp.int32, (WP, 128), 1) < W - 128
    pad = jnp.zeros((WP - W, 128), F32)
    skip = (blocks[0] * W - groups[0] * GROUP) * NS
    number = blocks[1] - blocks[0]

    def place(k, carry):
        for p in range(NS):
            row = skip + k * (W * NS) + p
            left = lo[pl.ds(row, W, stride=NS), :]
            right = hi[pl.ds(row, W, stride=NS), :]
            right = jnp.where(keep, jnp.concatenate([right, pad], axis=0), 0.0)
            c_ref[p * number + k, :, :128] = jnp.concatenate([left, pad], axis=0).astype(BF16)
            c_ref[p * number + k, :, 128:] = right.astype(BF16)
        return carry

    lax.fori_loop(0, number, place, 0)
    if first:
        copies[chunks].wait()


def own_kernel(inverse, own, part_ref, ext):
    for s in range(NS):
        ext[s * W : (s + 1) * W, :] = own[s, :W, :]
    ext[NS * W :, :] = jnp.zeros((OWN - NS * W, R), F32)
    part_ref[...] = jnp.dot(inverse[:, :OWN], ext[...].astype(BF16), preferred_element_type=F32)


def places(table):
    return table[EVEN] == 1, table[FIRST] == 1, table[LAST] == 1, table[LOW], table[HIGH]


def spilled(inverse, part, ext, block, index):
    begin = block * W // 16 * 16
    end = -(-(block + 1) * W // 16) * 16
    end = min(end, 6 * W)
    rows = jnp.dot(inverse[begin:end, FROM:], ext, preferred_element_type=F32)
    rows = rows[block * W - begin : (block + 1) * W - begin] + part[block * W : (block + 1) * W, :]
    mark = jnp.ones((WP - W, R), F32) * index.astype(F32)
    return jnp.concatenate([rows, mark], axis=0)


def margin_kernel(table, inverse, part, own, inner, outer, in_ref, ext_ref, ext):
    even, first, last, low, high = places(table)
    odd = jnp.logical_not(even)
    ext[: NS * W - FROM, :] = jnp.zeros((NS * W - FROM, R), F32)
    some = inner.shape[0] > 1

    def put(when, block, source, index):
        @pl.when(when)
        def _():
            ext[block * W - FROM : (block + 1) * W - FROM, :] = source[index].astype(F32)[:W]

    put(first, NS, own, low)
    put(jnp.logical_and(even, jnp.logical_not(first)), NS, outer, low if some else 0)
    put(odd, NS, inner, low if some else 0)
    put(last, NS + 1, own, high)
    put(jnp.logical_and(odd, jnp.logical_not(last)), NS + 1, outer, high if some else 0)
    put(even, NS + 1, inner, high if some else 0)
    ext_ref[...] = ext[...].astype(BF16)

    @pl.when(even)
    def _():
        in_ref[0] = spilled(inverse, part, ext_ref[...], NS + 1, high).astype(BF16)

    @pl.when(odd)
    def _():
        in_ref[0] = spilled(inverse, part, ext_ref[...], NS, low).astype(BF16)


def solve_kernel(table, inverse, part, ext, out_ref, out2_ref, res):
    even, first, last, low, high = places(table)
    mine = NS * W
    res[...] = part[:mine, :] + jnp.dot(inverse[:mine, FROM:], ext[...], preferred_element_type=F32)
    pad = jnp.zeros((WP - W, R), F32)
    for s in range(NS):
        out_ref[s] = jnp.concatenate([res[s * W : (s + 1) * W, :], pad], axis=0)
    keep = lax.broadcasted_iota(jnp.int32, (WP, R), 0) < W

    def spill(when, ends, block, index):
        @pl.when(when)
        def _():
            rows = spilled(inverse, part, ext[...], block, index)
            out2_ref[0] = rows.astype(BF16)

            @pl.when(ends)
            def _():
                out_ref[index] += jnp.where(keep, rows, 0.0)

    spill(even, first, NS, low)
    spill(jnp.logical_not(even), last, NS + 1, high)


def opened(block):
    x = block.astype(F32)
    rows = lax.broadcasted_iota(jnp.int32, x.shape, 0)
    return jnp.where(rows < W, x, 0.0), x[W : W + 1, :]


def inner_kernel(out, spill_in, spill_out, part_ref, sent_ref, near_ref):
    values, index = opened(spill_in[0])
    for s in range(NS):
        part = out[s] + jnp.where(index == s, values, 0.0)
        part_ref[s] = part
        sent_ref[s] = part.astype(BF16)
        near_ref[s] = part.astype(BF16)
    sent_ref[NS] = spill_out[0]


def system_kernel(
    first, table, ca, cb, part, got, near, far, spill_out, v0, *rest
):
    if first:
        p_ref, w_ref, wout_ref, sums_ref, u = rest
    else:
        w, p_ref, sums_ref, u = rest
    got_values, got_index = opened(got[NS])
    got_index = jnp.where(table[ENDS] == 1, -1.0, got_index)
    far_values, far_index = opened(far[0])
    far_index = jnp.where(table[NEXT] == 1, -1.0, far_index)
    count = table[COUNT]
    for s in range(NS):
        alive = jnp.where(count > s, 1.0, 0.0)
        p = (part[s] + jnp.where(got_index == s, got_values, 0.0)) * alive
        p_ref[s] = p
        u[s] = got[s]
        u[NS + s] = p.astype(BF16)
        u[2 * NS + s] = (near[s].astype(F32) + jnp.where(far_index == s, far_values, 0.0)).astype(BF16)
    index = table[OUT]
    u[index] = (got[index].astype(F32) + opened(spill_out[0])[0]).astype(BF16)
    sums_ref[...] = jnp.zeros((8, R), F32)
    if first:
        w_ref[...] = jnp.zeros((NS, WP, R), F32)

    def one(s):
        acc = p_ref[s]
        for k in range(NB):
            slot = table[SLOTS + s * NB + k]
            matrix = ca[s * SPLIT + k] if k < SPLIT else cb[s * (NB - SPLIT) + k - SPLIT]
            acc += jnp.dot(matrix, u[slot], preferred_element_type=F32)
        image = acc
        start = v0[s]
        if first:
            image = image - SHIFT * start
            w_ref[s] = image
            terms = (start * start, start * image, image * image)
        else:
            terms = (start * image, w[s] * image, image * image)
        sums = [jnp.sum(x, axis=0, keepdims=True) for x in terms]
        sums_ref[...] += jnp.concatenate(sums + [jnp.zeros((5, R), F32)], axis=0)

    for s in range(NS):
        pl.when(count > s)(functools.partial(one, s))
    if first:
        picked(wout_ref, w_ref, got_index)


def picked(ref, w, index):
    chosen = jnp.zeros((WP, R), F32)
    for s in range(NS):
        chosen = chosen + jnp.where(index == s, w[s], 0.0)
    ref[0] = chosen.astype(BF16)


def pick_kernel(w, spill_in, win_ref):
    picked(win_ref, w, opened(spill_in[0])[1])


def finish_kernel(gathered, p0, q, out_ref, out, sems):
    total = jnp.sum(gathered[...], axis=0)
    s00, s01, s11, s02, s12, s22 = (total[i : i + 1, :] for i in range(6))
    c = SHIFT
    bb = s00 + EPS
    beta = jnp.sqrt(bb)
    h11 = (s01 + c * s00) / bb
    a = c - h11
    n2 = (s11 + 2 * a * s01 + a * a * s00) / bb
    h21s = jnp.maximum(n2, 0.0) + EPS
    h21 = jnp.sqrt(h21s)
    full = bb * h21s
    v0i = s01 + c * s00
    h12 = (s02 + a * v0i) / (bb * h21)
    cross = (s01 + a * s00) / (bb * h21)
    b2i = (s12 + a * s02 + a * (s11 + c * s01) + a * a * v0i) / full
    h22 = b2i - h12 * cross
    ii = (s22 + 2 * a * (s12 + c * s02) + a * a * (s11 + 2 * c * s01 + c * c * s00)) / full
    rest = (
        ii + h12 * h12 * (s00 / bb) + h22 * h22 * (n2 / h21s)
        - 2 * h12 * h12 - 2 * h22 * b2i + 2 * h12 * h22 * cross
    )
    h32s = jnp.maximum(rest, 0.0) + EPS
    g00 = h11 * h11 + h21s
    g01 = h11 * h12 + h21 * h22
    g11 = h12 * h12 + h22 * h22 + h32s
    det = g00 * g11 - g01 * g01
    y1 = beta * (g11 * h11 - g01 * h12) / det
    y2 = beta * (g00 * h12 - g01 * h11) / det
    two = y2 / (beta * h21)
    one = y1 / beta + a * two
    copies = []
    for begin, size in PARTS:
        for s in range(NS):
            p, r = p0[s, begin : begin + size, :], q[s, begin : begin + size, :]
            out[pl.ds(begin * NS + s, size, stride=NS), :] = one * p + two * r
        rows = pl.ds(begin * NS, size * NS)
        copies.append(pltpu.make_async_copy(out.at[rows, :], out_ref.at[rows, :], sems.at[len(copies)]))
        copies[-1].start()
    for copy in copies:
        copy.wait()


def permuted(x, target):
    parts = lax.axis_size("rhs")
    pairs = [(i, j) for i in range(NSUB) for j in range(parts)]
    return lax.ppermute(
        x, ("sub", "rhs"), [(i * parts + j, t[0] * parts + t[1]) for i, j in pairs for t in [target(i, j)]]
    )


def to_inner(x):
    return permuted(x, lambda i, j: (i ^ 1, j))


def to_outer(x):
    return permuted(x, lambda i, j: (i, j ^ 1) if i in (0, NSUB - 1) else (((i + 1) ^ 1) - 1, j))


def to_far(x):
    def target(i, j):
        if i in (0, NSUB - 1):
            return i ^ 1, j
        return i + (2 if i % 2 else -2), j

    return permuted(x, target)


def body(right_side, coupling, neighbours, inverse, margin, counts):
    here = lax.axis_index("sub").astype(jnp.int32).reshape(1)
    flat_right = right_side.transpose(1, 0, 2).reshape(W * NS, R)
    block, one = (NS, WP, R), (1, WP, R)
    v0, v0b = call(start_kernel, [(block, F32), (block, BF16)], [SM, VM])(counts, flat_right)
    outer, inner = to_outer(v0b), to_inner(v0b)

    coupling = pltpu.with_memory_space_constraint(coupling, pltpu.HBM)
    inverse, margin, neighbours = (
        pltpu.with_memory_space_constraint(a, pltpu.HBM) for a in (inverse, margin, neighbours)
    )

    def matrices(first, *more):
        lanes = GROUP * W
        blocks = (0, SPLIT) if first else (SPLIT, NB)
        begin = blocks[0] * W // GROUP
        end = -(-blocks[1] * W // GROUP)
        count = -(-(end - begin) // CHUNK) * CHUNK
        groups = (begin, begin + count) if first else (end - count, end)
        outs = [((NS * (blocks[1] - blocks[0]), WP, WP), BF16, pltpu.VMEM)]
        if first:
            outs += [((6 * W, 6 * W), BF16, pltpu.VMEM), ((TABLE,), jnp.int32, pltpu.SMEM)]
        return call(
            functools.partial(coupling_kernel, blocks, groups, first),
            outs,
            [ANY, ANY] + [SM] * (len(more) - 1),
            [
                pltpu.VMEM((NS, count * lanes), BF16),
                pltpu.VMEM((4 * NS, lanes), BF16),
                pltpu.VMEM((count * GROUP * NS, 128), F32),
                pltpu.VMEM((count * GROUP * NS, 128), F32),
                pltpu.SemaphoreType.DMA((count // CHUNK + 1,)),
            ],
            limit=24,
            cost=pl.CostEstimate(flops=1 << 20, bytes_accessed=12 << 20, transcendentals=0),
        )(coupling, *more)

    first_part, held, table = matrices(True, inverse, here, counts, margin, neighbours)
    table = pltpu.with_memory_space_constraint(table, pltpu.SMEM)
    held = pltpu.with_memory_space_constraint(held, pltpu.VMEM)
    first_part = pltpu.with_memory_space_constraint(first_part, pltpu.VMEM)

    def solve(own, inner, outer):
        (part,) = call(
            own_kernel, [((6 * W, R), F32, pltpu.VMEM)], [VM, VM], [pltpu.VMEM((OWN, R), F32)],
            cost=pl.CostEstimate(flops=1 << 30, bytes_accessed=4 << 20, transcendentals=0),
        )(held, own)
        depth = 6 * W - FROM
        spill_in, ext = call(
            margin_kernel,
            [(one, BF16), ((depth, R), BF16)],
            [SM] + [VM] * 5,
            [pltpu.VMEM((depth, R), F32)],
        )(table, held, part, own, inner, outer)
        got_in = to_inner(spill_in)
        out, spill_out = call(
            solve_kernel,
            [(block, F32), (one, BF16)],
            [SM] + [VM] * 3,
            [pltpu.VMEM((NS * W, R), F32)],
            cost=pl.CostEstimate(flops=1 << 30, bytes_accessed=4 << 20, transcendentals=0),
        )(table, held, part, ext)
        return out, got_in, spill_out

    def system(first, out, got_in, spill_out, *more):
        part, sent, near = call(
            inner_kernel, [(block, F32), ((NS + 1, WP, R), BF16), (block, BF16)], [VM] * 3
        )(out, got_in, spill_out)
        got, near, far = to_outer(sent), to_inner(near), to_far(spill_out)
        if first:
            (made,) = matrices(False, sent)
            matrix_parts.append(pltpu.with_memory_space_constraint(made, pltpu.VMEM))
        outs = [(block, F32)] + ([(block, F32), (one, BF16)] if first else [])
        return call(
            functools.partial(system_kernel, first),
            outs + [((8, R), F32)],
            [SM] + [VM] * (7 + len(more)),
            [pltpu.VMEM((3 * NS, WP, R), BF16)],
        )(table, *matrix_parts, part, got, near, far, spill_out, *more)

    matrix_parts = [first_part]
    out, got_in, spill_out = solve(v0, inner, outer)
    p0, w, w_out, sums_one = system(True, out, got_in, spill_out, v0)
    outer = to_outer(w_out)
    (w_in,) = call(pick_kernel, [(one, BF16)], [VM] * 2)(w, got_in)
    q, sums_two = system(False, *solve(w, to_inner(w_in), outer), v0, w)
    sums = jnp.concatenate([sums_one[:3], sums_two[:3]], axis=0)
    sums = sums + to_inner(sums)
    gathered = lax.all_to_all(
        jnp.broadcast_to(sums[None], (NSUB // 2, 6, R)), "sub", 0, 0,
        axis_index_groups=[list(range(c, NSUB, 2)) for c in range(2)],
    )
    (flat,) = call(
        finish_kernel,
        [((W * NS, R), F32, pltpu.HBM)],
        [VM] * 3,
        [pltpu.VMEM((W * NS, R), F32), pltpu.SemaphoreType.DMA((len(PARTS),))],
    )(gathered, p0, q)
    return flat.reshape(W, NS, R).transpose(1, 0, 2)


def solution(mesh):
    placed = (
        P("sub", None, "rhs"),
        P("sub", None),
        P("sub", None),
        P("sub", None, None),
        P("sub", None),
        P("sub"),
    )
    return jax.shard_map(
        body, mesh=mesh, in_specs=placed, out_specs=P("sub", None, "rhs"), check_vma=False
    )
```

```python
import functools
import jax
import jax.numpy as jnp
from jax import lax
from jax.experimental import pallas as pl
from jax.experimental.pallas import tpu as pltpu
from jax.sharding import PartitionSpec as P

EPS = 1e-06
W = 252
WP = 256
NS = 4
NB = 8
R = 128
NSUB = 64
SHIFT = 1.0
ROWS = NB * W
GROUP = 32
F32 = jnp.float32
BF16 = jnp.bfloat16
CHUNK = 8
SPLIT = 4
EVEN, FIRST, LAST, LOW, HIGH, COUNT, ENDS, NEXT, OUT, SLOTS = range(10)
TABLE = SLOTS + NS * NB
OWN = 1024
FROM = 896
ANY = pl.BlockSpec(memory_space=pl.ANY)
PARTS = ((0, 64), (64, 64), (128, 64), (192, 60))
VM = pl.BlockSpec(memory_space=pltpu.VMEM)
SM = pl.BlockSpec(memory_space=pltpu.SMEM)


def call(kernel, outs, ins, scratch=(), limit=24, cost=None):
    return pl.pallas_call(
        kernel,
        out_shape=[keep[0](s, d) if keep else jax.ShapeDtypeStruct(s, d) for s, d, *keep in outs],
        in_specs=ins,
        out_specs=[{pltpu.SMEM: SM, pltpu.HBM: ANY}.get(keep[0], VM) if keep else VM for _, _, *keep in outs],
        scratch_shapes=list(scratch),
        compiler_params=pltpu.CompilerParams(vmem_limit_bytes=limit << 20),
        cost_estimate=cost,
    )


def start_kernel(counts, right, v0_ref, v0b_ref):
    for s in range(NS):
        alive = jnp.where(counts[0] > s, 1.0, 0.0)
        v0_ref[s, :W, :] = right[pl.ds(s, W, stride=NS), :] * alive
        v0_ref[s, W:, :] = jnp.zeros((WP - W, R), F32)
        v0b_ref[s] = v0_ref[s].astype(BF16)


def fill_table(table, place, counts, margin, neighbours):
    here = place[0]
    even = here % 2 == 0
    first, last = here == 0, here == NSUB - 1
    low = jnp.clip(margin[0, 0] - NS * jnp.maximum(here - 1, 0), 0, NS - 1)
    high = jnp.clip(margin[0, 1] - NS * jnp.minimum(here + 1, NSUB - 1), 0, NS - 1)
    table[EVEN] = jnp.where(even, 1, 0)
    table[FIRST] = jnp.where(first, 1, 0)
    table[LAST] = jnp.where(last, 1, 0)
    table[LOW] = low
    table[HIGH] = high
    table[COUNT] = counts[0]
    table[ENDS] = jnp.where(jnp.logical_or(first, last), 1, 0)
    table[NEXT] = jnp.where(jnp.logical_or(here == 1, here == NSUB - 2), 1, 0)
    table[OUT] = jnp.where(even, low, high)
    for s in range(NS):
        for k in range(NB):
            slot = jnp.clip(neighbours[s, k] - NS * (here - 1), 0, 3 * NS - 1)
            table[SLOTS + s * NB + k] = jnp.where(even, slot, slot + 2 * NS * (1 - slot // NS))


def coupling_kernel(blocks, groups, first, flat, *rest):
    if first:
        inverse, place, counts, margin, neighbours, c_ref, inverse_ref, table, raw, x, lo, hi, sems = rest
    else:
        _, c_ref, raw, x, lo, hi, sems = rest
    lanes = GROUP * W
    count = groups[1] - groups[0]
    step = CHUNK * lanes
    chunks = count // CHUNK
    copies = [
        pltpu.make_async_copy(
            flat.at[:, pl.ds(groups[0] * lanes + c * step, step)],
            raw.at[:, pl.ds(c * step, step)],
            sems.at[c],
        )
        for c in range(chunks)
    ]
    if first:
        copies.append(pltpu.make_async_copy(inverse.at[0], inverse_ref, sems.at[chunks]))
    for copy in copies:
        copy.start()
    if first:
        fill_table(table, place, counts, margin, neighbours)
    lane = lax.broadcasted_iota(jnp.int32, (4 * NS, 128), 1)

    def four(i, carry):
        for h in range(4):
            at = pl.multiple_of((4 * i + h) * lanes, 128)
            x[NS * h : NS * h + NS, :] = raw[:, pl.ds(at, lanes)]
        base = pl.multiple_of(4 * i * (GROUP * NS), 8)
        for s in range(GROUP):
            def rolled(t):
                piece = x[:, 128 * t : 128 * t + 128]
                return pltpu.roll(piece, 4 * s, 1) if s else piece

            middle = rolled(2 * s)
            if s == 0:
                left, right = middle, rolled(1)
            else:
                early = lane < 4 * s
                left = jnp.where(early, rolled(2 * s - 1), middle)
                right = jnp.where(early, middle, rolled(2 * s + 1)) if s < GROUP - 1 else middle
            left, right = left.astype(F32), right.astype(F32)
            for h in range(4):
                at = base + (h * GROUP + s) * NS
                lo[pl.ds(at, NS), :] = left[NS * h : NS * h + NS]
                hi[pl.ds(at, NS), :] = right[NS * h : NS * h + NS]
        return carry

    for c in range(chunks):
        copies[c].wait()
        lax.fori_loop(c * CHUNK // 4, (c + 1) * CHUNK // 4, four, 0)
    keep = lax.broadcasted_iota(jnp.int32, (WP, 128), 1) < W - 128
    pad = jnp.zeros((WP - W, 128), F32)
    skip = (blocks[0] * W - groups[0] * GROUP) * NS
    number = blocks[1] - blocks[0]

    def place(k, carry):
        for p in range(NS):
            row = skip + k * (W * NS) + p
            left = lo[pl.ds(row, W, stride=NS), :]
            right = hi[pl.ds(row, W, stride=NS), :]
            right = jnp.where(keep, jnp.concatenate([right, pad], axis=0), 0.0)
            c_ref[p * number + k, :, :128] = jnp.concatenate([left, pad], axis=0).astype(BF16)
            c_ref[p * number + k, :, 128:] = right.astype(BF16)
        return carry

    lax.fori_loop(0, number, place, 0)
    if first:
        copies[chunks].wait()


def own_kernel(inverse, own, part_ref, ext):
    for s in range(NS):
        ext[s * W : (s + 1) * W, :] = own[s, :W, :]
    ext[NS * W :, :] = jnp.zeros((OWN - NS * W, R), F32)
    part_ref[...] = jnp.dot(inverse[:, :OWN], ext[...].astype(BF16), preferred_element_type=F32)


def places(table):
    return table[EVEN] == 1, table[FIRST] == 1, table[LAST] == 1, table[LOW], table[HIGH]


def spilled(inverse, part, ext, block, index):
    begin = block * W // 16 * 16
    end = -(-(block + 1) * W // 16) * 16
    end = min(end, 6 * W)
    rows = jnp.dot(inverse[begin:end, FROM:], ext, preferred_element_type=F32)
    rows = rows[block * W - begin : (block + 1) * W - begin] + part[block * W : (block + 1) * W, :]
    mark = jnp.ones((WP - W, R), F32) * index.astype(F32)
    return jnp.concatenate([rows, mark], axis=0)


def margin_kernel(table, inverse, part, own, inner, outer, in_ref, ext_ref, ext):
    even, first, last, low, high = places(table)
    odd = jnp.logical_not(even)
    ext[: NS * W - FROM, :] = jnp.zeros((NS * W - FROM, R), F32)
    some = inner.shape[0] > 1

    def put(when, block, source, index):
        @pl.when(when)
        def _():
            ext[block * W - FROM : (block + 1) * W - FROM, :] = source[index].astype(F32)[:W]

    put(first, NS, own, low)
    put(jnp.logical_and(even, jnp.logical_not(first)), NS, outer, low if some else 0)
    put(odd, NS, inner, low if some else 0)
    put(last, NS + 1, own, high)
    put(jnp.logical_and(odd, jnp.logical_not(last)), NS + 1, outer, high if some else 0)
    put(even, NS + 1, inner, high if some else 0)
    ext_ref[...] = ext[...].astype(BF16)

    @pl.when(even)
    def _():
        in_ref[0] = spilled(inverse, part, ext_ref[...], NS + 1, high).astype(BF16)

    @pl.when(odd)
    def _():
        in_ref[0] = spilled(inverse, part, ext_ref[...], NS, low).astype(BF16)


def solve_kernel(table, inverse, part, ext, out_ref, out2_ref, res):
    even, first, last, low, high = places(table)
    mine = NS * W
    res[...] = part[:mine, :] + jnp.dot(inverse[:mine, FROM:], ext[...], preferred_element_type=F32)
    pad = jnp.zeros((WP - W, R), F32)
    for s in range(NS):
        out_ref[s] = jnp.concatenate([res[s * W : (s + 1) * W, :], pad], axis=0)
    keep = lax.broadcasted_iota(jnp.int32, (WP, R), 0) < W

    def spill(when, ends, block, index):
        @pl.when(when)
        def _():
            rows = spilled(inverse, part, ext[...], block, index)
            out2_ref[0] = rows.astype(BF16)

            @pl.when(ends)
            def _():
                out_ref[index] += jnp.where(keep, rows, 0.0)

    spill(even, first, NS, low)
    spill(jnp.logical_not(even), last, NS + 1, high)


def opened(block):
    x = block.astype(F32)
    rows = lax.broadcasted_iota(jnp.int32, x.shape, 0)
    return jnp.where(rows < W, x, 0.0), x[W : W + 1, :]


def inner_kernel(out, spill_in, spill_out, part_ref, sent_ref, near_ref):
    values, index = opened(spill_in[0])
    for s in range(NS):
        part = out[s] + jnp.where(index == s, values, 0.0)
        part_ref[s] = part
        sent_ref[s] = part.astype(BF16)
        near_ref[s] = part.astype(BF16)
    sent_ref[NS] = spill_out[0]


def system_kernel(
    first, table, ca, cb, part, got, near, far, spill_out, v0, *rest
):
    if first:
        p_ref, w_ref, wout_ref, sums_ref, u = rest
    else:
        w, p_ref, sums_ref, u = rest
    got_values, got_index = opened(got[NS])
    got_index = jnp.where(table[ENDS] == 1, -1.0, got_index)
    far_values, far_index = opened(far[0])
    far_index = jnp.where(table[NEXT] == 1, -1.0, far_index)
    count = table[COUNT]
    for s in range(NS):
        alive = jnp.where(count > s, 1.0, 0.0)
        p = (part[s] + jnp.where(got_index == s, got_values, 0.0)) * alive
        p_ref[s] = p
        u[s] = got[s]
        u[NS + s] = p.astype(BF16)
        u[2 * NS + s] = (near[s].astype(F32) + jnp.where(far_index == s, far_values, 0.0)).astype(BF16)
    index = table[OUT]
    u[index] = (got[index].astype(F32) + opened(spill_out[0])[0]).astype(BF16)
    sums_ref[...] = jnp.zeros((8, R), F32)
    if first:
        w_ref[...] = jnp.zeros((NS, WP, R), F32)

    def one(s):
        acc = p_ref[s]
        for k in range(NB):
            slot = table[SLOTS + s * NB + k]
            matrix = ca[s * SPLIT + k] if k < SPLIT else cb[s * (NB - SPLIT) + k - SPLIT]
            acc += jnp.dot(matrix, u[slot], preferred_element_type=F32)
        image = acc
        start = v0[s]
        if first:
            image = image - SHIFT * start
            w_ref[s] = image
            terms = (start * start, start * image, image * image)
        else:
            terms = (start * image, w[s] * image, image * image)
        sums = [jnp.sum(x, axis=0, keepdims=True) for x in terms]
        sums_ref[...] += jnp.concatenate(sums + [jnp.zeros((5, R), F32)], axis=0)

    for s in range(NS):
        pl.when(count > s)(functools.partial(one, s))
    if first:
        picked(wout_ref, w_ref, got_index)


def picked(ref, w, index):
    chosen = jnp.zeros((WP, R), F32)
    for s in range(NS):
        chosen = chosen + jnp.where(index == s, w[s], 0.0)
    ref[0] = chosen.astype(BF16)


def pick_kernel(w, spill_in, win_ref):
    picked(win_ref, w, opened(spill_in[0])[1])


def finish_kernel(table, gathered, other, p0, q, out_ref, out, sems):
    total = jnp.where(table[EVEN] == 1, jnp.sum(other[...], axis=0), jnp.sum(gathered[...], axis=0))
    s00, s01, s11, s02, s12, s22 = (total[i : i + 1, :] for i in range(6))
    c = SHIFT
    bb = s00 + EPS
    beta = jnp.sqrt(bb)
    h11 = (s01 + c * s00) / bb
    a = c - h11
    n2 = (s11 + 2 * a * s01 + a * a * s00) / bb
    h21s = jnp.maximum(n2, 0.0) + EPS
    h21 = jnp.sqrt(h21s)
    full = bb * h21s
    v0i = s01 + c * s00
    h12 = (s02 + a * v0i) / (bb * h21)
    cross = (s01 + a * s00) / (bb * h21)
    b2i = (s12 + a * s02 + a * (s11 + c * s01) + a * a * v0i) / full
    h22 = b2i - h12 * cross
    ii = (s22 + 2 * a * (s12 + c * s02) + a * a * (s11 + 2 * c * s01 + c * c * s00)) / full
    rest = (
        ii + h12 * h12 * (s00 / bb) + h22 * h22 * (n2 / h21s)
        - 2 * h12 * h12 - 2 * h22 * b2i + 2 * h12 * h22 * cross
    )
    h32s = jnp.maximum(rest, 0.0) + EPS
    g00 = h11 * h11 + h21s
    g01 = h11 * h12 + h21 * h22
    g11 = h12 * h12 + h22 * h22 + h32s
    det = g00 * g11 - g01 * g01
    y1 = beta * (g11 * h11 - g01 * h12) / det
    y2 = beta * (g00 * h12 - g01 * h11) / det
    two = y2 / (beta * h21)
    one = y1 / beta + a * two
    copies = []
    for begin, size in PARTS:
        for s in range(NS):
            p, r = p0[s, begin : begin + size, :], q[s, begin : begin + size, :]
            out[pl.ds(begin * NS + s, size, stride=NS), :] = one * p + two * r
        rows = pl.ds(begin * NS, size * NS)
        copies.append(pltpu.make_async_copy(out.at[rows, :], out_ref.at[rows, :], sems.at[len(copies)]))
        copies[-1].start()
    for copy in copies:
        copy.wait()


def permuted(x, target):
    parts = lax.axis_size("rhs")
    pairs = [(i, j) for i in range(NSUB) for j in range(parts)]
    return lax.ppermute(
        x, ("sub", "rhs"), [(i * parts + j, t[0] * parts + t[1]) for i, j in pairs for t in [target(i, j)]]
    )


def to_inner(x):
    return permuted(x, lambda i, j: (i ^ 1, j))


def to_outer(x):
    return permuted(x, lambda i, j: (i, j ^ 1) if i in (0, NSUB - 1) else (((i + 1) ^ 1) - 1, j))


def to_far(x):
    def target(i, j):
        if i in (0, NSUB - 1):
            return i ^ 1, j
        return i + (2 if i % 2 else -2), j

    return permuted(x, target)


def sum_groups(parts):
    odd = [[i * parts + j for i in range(1, NSUB, 2)] for j in range(parts)]
    near = NSUB // 2 // parts
    rows = 4
    width = near // rows
    even = [
        [
            (2 * (row * (NSUB // 2 // rows) + block * width + k)) * parts + j
            for j in range(parts)
            for row in range(rows)
            for k in range(width)
        ]
        for block in range(parts)
    ]
    return odd + even


def body(right_side, coupling, neighbours, inverse, margin, counts):
    here = lax.axis_index("sub").astype(jnp.int32).reshape(1)
    flat_right = right_side.transpose(1, 0, 2).reshape(W * NS, R)
    block, one = (NS, WP, R), (1, WP, R)
    v0, v0b = call(start_kernel, [(block, F32), (block, BF16)], [SM, VM])(counts, flat_right)
    outer, inner = to_outer(v0b), to_inner(v0b)

    coupling = pltpu.with_memory_space_constraint(coupling, pltpu.HBM)
    inverse, margin, neighbours = (
        pltpu.with_memory_space_constraint(a, pltpu.HBM) for a in (inverse, margin, neighbours)
    )

    def matrices(first, *more):
        lanes = GROUP * W
        blocks = (0, SPLIT) if first else (SPLIT, NB)
        begin = blocks[0] * W // GROUP
        end = -(-blocks[1] * W // GROUP)
        count = -(-(end - begin) // CHUNK) * CHUNK
        groups = (begin, begin + count) if first else (end - count, end)
        outs = [((NS * (blocks[1] - blocks[0]), WP, WP), BF16, pltpu.VMEM)]
        if first:
            outs += [((6 * W, 6 * W), BF16, pltpu.VMEM), ((TABLE,), jnp.int32, pltpu.SMEM)]
        return call(
            functools.partial(coupling_kernel, blocks, groups, first),
            outs,
            [ANY, ANY] + [SM] * (len(more) - 1),
            [
                pltpu.VMEM((NS, count * lanes), BF16),
                pltpu.VMEM((4 * NS, lanes), BF16),
                pltpu.VMEM((count * GROUP * NS, 128), F32),
                pltpu.VMEM((count * GROUP * NS, 128), F32),
                pltpu.SemaphoreType.DMA((count // CHUNK + 1,)),
            ],
            limit=24,
            cost=pl.CostEstimate(flops=1 << 20, bytes_accessed=12 << 20, transcendentals=0),
        )(coupling, *more)

    first_part, held, table = matrices(True, inverse, here, counts, margin, neighbours)
    table = pltpu.with_memory_space_constraint(table, pltpu.SMEM)
    held = pltpu.with_memory_space_constraint(held, pltpu.VMEM)
    first_part = pltpu.with_memory_space_constraint(first_part, pltpu.VMEM)

    def solve(own, inner, outer):
        (part,) = call(
            own_kernel, [((6 * W, R), F32, pltpu.VMEM)], [VM, VM], [pltpu.VMEM((OWN, R), F32)],
            cost=pl.CostEstimate(flops=1 << 30, bytes_accessed=4 << 20, transcendentals=0),
        )(held, own)
        depth = 6 * W - FROM
        spill_in, ext = call(
            margin_kernel,
            [(one, BF16), ((depth, R), BF16)],
            [SM] + [VM] * 5,
            [pltpu.VMEM((depth, R), F32)],
        )(table, held, part, own, inner, outer)
        got_in = to_inner(spill_in)
        out, spill_out = call(
            solve_kernel,
            [(block, F32), (one, BF16)],
            [SM] + [VM] * 3,
            [pltpu.VMEM((NS * W, R), F32)],
            cost=pl.CostEstimate(flops=1 << 30, bytes_accessed=4 << 20, transcendentals=0),
        )(table, held, part, ext)
        return out, got_in, spill_out

    def system(first, out, got_in, spill_out, *more):
        part, sent, near = call(
            inner_kernel, [(block, F32), ((NS + 1, WP, R), BF16), (block, BF16)], [VM] * 3
        )(out, got_in, spill_out)
        got, near, far = to_outer(sent), to_inner(near), to_far(spill_out)
        if first:
            (made,) = matrices(False, sent)
            matrix_parts.append(pltpu.with_memory_space_constraint(made, pltpu.VMEM))
        outs = [(block, F32)] + ([(block, F32), (one, BF16)] if first else [])
        return call(
            functools.partial(system_kernel, first),
            outs + [((8, R), F32)],
            [SM] + [VM] * (7 + len(more)),
            [pltpu.VMEM((3 * NS, WP, R), BF16)],
        )(table, *matrix_parts, part, got, near, far, spill_out, *more)

    matrix_parts = [first_part]
    out, got_in, spill_out = solve(v0, inner, outer)
    p0, w, w_out, sums_one = system(True, out, got_in, spill_out, v0)
    outer = to_outer(w_out)
    (w_in,) = call(pick_kernel, [(one, BF16)], [VM] * 2)(w, got_in)
    q, sums_two = system(False, *solve(w, to_inner(w_in), outer), v0, w)
    sums = jnp.concatenate([sums_one[:3], sums_two[:3]], axis=0)
    sums = sums + to_inner(sums)
    gathered = lax.all_to_all(
        jnp.broadcast_to(sums[None], (NSUB // 2, 6, R)), ("sub", "rhs"), 0, 0,
        axis_index_groups=sum_groups(lax.axis_size("rhs")),
    )
    other = to_inner(gathered)
    (flat,) = call(
        finish_kernel,
        [((W * NS, R), F32, pltpu.HBM)],
        [SM] + [VM] * 4,
        [pltpu.VMEM((W * NS, R), F32), pltpu.SemaphoreType.DMA((len(PARTS),))],
    )(table, gathered, other, p0, q)
    return flat.reshape(W, NS, R).transpose(1, 0, 2)


def solution(mesh):
    placed = (
        P("sub", None, "rhs"),
        P("sub", None),
        P("sub", None),
        P("sub", None, None),
        P("sub", None),
        P("sub"),
    )
    return jax.shard_map(
        body, mesh=mesh, in_specs=placed, out_specs=P("sub", None, "rhs"), check_vma=False
    )
```

```python
import functools
import jax
import jax.numpy as jnp
from jax import lax
from jax.experimental import pallas as pl
from jax.experimental.pallas import tpu as pltpu
from jax.sharding import PartitionSpec as P

EPS = 1e-06
W = 252
WP = 256
NS = 4
NB = 8
R = 128
NSUB = 64
SHIFT = 1.0
ROWS = NB * W
GROUP = 32
F32 = jnp.float32
BF16 = jnp.bfloat16
CHUNK = 8
SPLIT = 4
EVEN, FIRST, LAST, LOW, HIGH, COUNT, ENDS, NEXT, OUT, SLOTS = range(10)
TABLE = SLOTS + NS * NB
SPARE = 32
OWN = 1024
FROM = 896
ANY = pl.BlockSpec(memory_space=pl.ANY)
PARTS = ((0, 64), (64, 64), (128, 64), (192, 60))
VM = pl.BlockSpec(memory_space=pltpu.VMEM)
SM = pl.BlockSpec(memory_space=pltpu.SMEM)


def call(kernel, outs, ins, scratch=(), limit=24, cost=None):
    return pl.pallas_call(
        kernel,
        out_shape=[keep[0](s, d) if keep else jax.ShapeDtypeStruct(s, d) for s, d, *keep in outs],
        in_specs=ins,
        out_specs=[{pltpu.SMEM: SM, pltpu.HBM: ANY}.get(keep[0], VM) if keep else VM for _, _, *keep in outs],
        scratch_shapes=list(scratch),
        compiler_params=pltpu.CompilerParams(vmem_limit_bytes=limit << 20),
        cost_estimate=cost,
    )


def start_kernel(counts, right, v0_ref, v0b_ref):
    whole = W // 8 * 8
    tail = right[whole * NS :, :]
    for s in range(NS):
        alive = jnp.where(counts[0] > s, 1.0, 0.0)
        v0_ref[s, :whole, :] = right[pl.ds(s, whole, stride=NS), :] * alive
        last = [tail[NS * i + s : NS * i + s + 1, :] * alive for i in range(W - whole)]
        v0_ref[s, whole:, :] = jnp.concatenate(last + [jnp.zeros((WP - W, R), F32)], axis=0)
        v0b_ref[s] = v0_ref[s].astype(BF16)


def fill_table(table, place, counts, margin, neighbours):
    here = place[0]
    even = here % 2 == 0
    first, last = here == 0, here == NSUB - 1
    low = jnp.clip(margin[0, 0] - NS * jnp.maximum(here - 1, 0), 0, NS - 1)
    high = jnp.clip(margin[0, 1] - NS * jnp.minimum(here + 1, NSUB - 1), 0, NS - 1)
    table[EVEN] = jnp.where(even, 1, 0)
    table[FIRST] = jnp.where(first, 1, 0)
    table[LAST] = jnp.where(last, 1, 0)
    table[LOW] = low
    table[HIGH] = high
    table[COUNT] = counts[0]
    table[ENDS] = jnp.where(jnp.logical_or(first, last), 1, 0)
    table[NEXT] = jnp.where(jnp.logical_or(here == 1, here == NSUB - 2), 1, 0)
    table[OUT] = jnp.where(even, low, high)
    for s in range(NS):
        for k in range(NB):
            slot = jnp.clip(neighbours[s, k] - NS * (here - 1), 0, 3 * NS - 1)
            table[SLOTS + s * NB + k] = jnp.where(even, slot, slot + 2 * NS * (1 - slot // NS))


def coupling_kernel(blocks, groups, first, flat, *rest):
    if first:
        inverse, place, counts, margin, neighbours, c_ref, inverse_ref, table, raw, x, lo, hi, sems = rest
    else:
        _, c_ref, raw, x, lo, hi, sems = rest
    lanes = GROUP * W
    count = groups[1] - groups[0]
    step = CHUNK * lanes
    chunks = count // CHUNK
    copies = [
        pltpu.make_async_copy(
            flat.at[:, pl.ds(groups[0] * lanes + c * step, step)],
            raw.at[:, pl.ds(c * step, step)],
            sems.at[c],
        )
        for c in range(chunks)
    ]
    if first:
        copies.append(pltpu.make_async_copy(inverse.at[0], inverse_ref, sems.at[chunks]))
    for copy in copies:
        copy.start()
    if first:
        fill_table(table, place, counts, margin, neighbours)
    lane = lax.broadcasted_iota(jnp.int32, (4 * NS, 128), 1)

    def four(i, carry):
        for h in range(4):
            at = pl.multiple_of((4 * i + h) * lanes, 128)
            x[NS * h : NS * h + NS, :] = raw[:, pl.ds(at, lanes)]
        base = pl.multiple_of(4 * i * (GROUP * NS), 8)
        for s in range(GROUP):
            def rolled(t):
                piece = x[:, 128 * t : 128 * t + 128]
                return pltpu.roll(piece, 4 * s, 1) if s else piece

            middle = rolled(2 * s)
            if s == 0:
                left, right = middle, rolled(1)
            else:
                early = lane < 4 * s
                left = jnp.where(early, rolled(2 * s - 1), middle)
                right = jnp.where(early, middle, rolled(2 * s + 1)) if s < GROUP - 1 else middle
            left, right = left.astype(F32), right.astype(F32)
            for h in range(4):
                at = base + (h * GROUP + s) * NS
                lo[pl.ds(at, NS), :] = left[NS * h : NS * h + NS]
                hi[pl.ds(at, NS), :] = right[NS * h : NS * h + NS]
        return carry

    for c in range(chunks):
        copies[c].wait()
        lax.fori_loop(c * CHUNK // 4, (c + 1) * CHUNK // 4, four, 0)
    keep = lax.broadcasted_iota(jnp.int32, (WP, 128), 1) < W - 128
    pad = jnp.zeros((WP - W, 128), F32)
    skip = (blocks[0] * W - groups[0] * GROUP) * NS
    number = blocks[1] - blocks[0]

    def place(k, carry):
        for p in range(NS):
            row = skip + k * (W * NS) + p
            left = lo[pl.ds(row, W, stride=NS), :]
            right = hi[pl.ds(row, W, stride=NS), :]
            right = jnp.where(keep, jnp.concatenate([right, pad], axis=0), 0.0)
            c_ref[p * number + k, :, :128] = jnp.concatenate([left, pad], axis=0).astype(BF16)
            c_ref[p * number + k, :, 128:] = right.astype(BF16)
        return carry

    lax.fori_loop(0, number, place, 0)
    if first:
        copies[chunks].wait()


def own_kernel(inverse, own, part_ref, ext):
    for s in range(NS):
        ext[s * W : (s + 1) * W, :] = own[s, :W, :]
    ext[NS * W :, :] = jnp.zeros((OWN - NS * W, R), F32)
    part_ref[: 6 * W, :] = jnp.dot(inverse[:, :OWN], ext[...].astype(BF16), preferred_element_type=F32)


def places(table):
    return table[EVEN] == 1, table[FIRST] == 1, table[LAST] == 1, table[LOW], table[HIGH]


def spilled(inverse, part, ext, block, index):
    begin = block * W // 16 * 16
    end = -(-(block + 1) * W // 16) * 16
    end = min(end, 6 * W)
    rows = jnp.dot(inverse[begin:end, FROM:], ext, preferred_element_type=F32)
    rows = rows[block * W - begin : (block + 1) * W - begin] + part[block * W : (block + 1) * W, :]
    mark = jnp.ones((WP - W, R), F32) * index.astype(F32)
    return jnp.concatenate([rows, mark], axis=0)


def margin_kernel(table, inverse, part, own, inner, outer, in_ref, ext_ref, ext):
    even, first, last, low, high = places(table)
    odd = jnp.logical_not(even)
    ext[: NS * W - FROM, :] = jnp.zeros((NS * W - FROM, R), F32)
    some = inner.shape[0] > 1

    def put(when, block, source, index):
        @pl.when(when)
        def _():
            ext[block * W - FROM : (block + 1) * W - FROM, :] = source[index].astype(F32)[:W]

    put(first, NS, own, low)
    put(jnp.logical_and(even, jnp.logical_not(first)), NS, outer, low if some else 0)
    put(odd, NS, inner, low if some else 0)
    put(last, NS + 1, own, high)
    put(jnp.logical_and(odd, jnp.logical_not(last)), NS + 1, outer, high if some else 0)
    put(even, NS + 1, inner, high if some else 0)
    ext_ref[...] = ext[: 6 * W - FROM, :].astype(BF16)

    @pl.when(even)
    def _():
        in_ref[0] = spilled(inverse, part, ext_ref[...], NS + 1, high).astype(BF16)

    @pl.when(odd)
    def _():
        in_ref[0] = spilled(inverse, part, ext_ref[...], NS, low).astype(BF16)


def solve_kernel(table, inverse, part, ext, out_ref, out2_ref, res):
    even, first, last, low, high = places(table)
    mine = NS * W
    res[:mine, :] = part[:mine, :] + jnp.dot(inverse[:mine, FROM:], ext[...], preferred_element_type=F32)
    pad = jnp.zeros((WP - W, R), F32)
    for s in range(NS):
        out_ref[s] = jnp.concatenate([res[s * W : (s + 1) * W, :], pad], axis=0)
    keep = lax.broadcasted_iota(jnp.int32, (WP, R), 0) < W

    def spill(when, ends, block, index):
        @pl.when(when)
        def _():
            rows = spilled(inverse, part, ext[...], block, index)
            out2_ref[0] = rows.astype(BF16)

            @pl.when(ends)
            def _():
                out_ref[index] += jnp.where(keep, rows, 0.0)

    spill(even, first, NS, low)
    spill(jnp.logical_not(even), last, NS + 1, high)


def opened(block):
    x = block.astype(F32)
    rows = lax.broadcasted_iota(jnp.int32, x.shape, 0)
    return jnp.where(rows < W, x, 0.0), x[W : W + 1, :]


def inner_kernel(out, spill_in, spill_out, part_ref, sent_ref, near_ref):
    values, index = opened(spill_in[0])
    for s in range(NS):
        part = out[s] + jnp.where(index == s, values, 0.0)
        part_ref[s] = part
        sent_ref[s] = part.astype(BF16)
        near_ref[s] = part.astype(BF16)
    sent_ref[NS] = spill_out[0]


def system_kernel(
    first, table, ca, cb, part, got, near, far, spill_out, v0, *rest
):
    if first:
        p_ref, w_ref, wout_ref, sums_ref, u = rest
    else:
        w, p_ref, sums_ref, u = rest
    got_values, got_index = opened(got[NS])
    got_index = jnp.where(table[ENDS] == 1, -1.0, got_index)
    far_values, far_index = opened(far[0])
    far_index = jnp.where(table[NEXT] == 1, -1.0, far_index)
    count = table[COUNT]
    for s in range(NS):
        alive = jnp.where(count > s, 1.0, 0.0)
        p = (part[s] + jnp.where(got_index == s, got_values, 0.0)) * alive
        p_ref[s] = p
        u[s] = got[s]
        u[NS + s] = p.astype(BF16)
        u[2 * NS + s] = (near[s].astype(F32) + jnp.where(far_index == s, far_values, 0.0)).astype(BF16)
    index = table[OUT]
    u[index] = (got[index].astype(F32) + opened(spill_out[0])[0]).astype(BF16)
    sums_ref[...] = jnp.zeros((8, R), F32)
    if first:
        w_ref[...] = jnp.zeros((NS, WP, R), F32)

    def one(s):
        acc = p_ref[s]
        for k in range(NB):
            slot = table[SLOTS + s * NB + k]
            matrix = ca[s * SPLIT + k] if k < SPLIT else cb[s * (NB - SPLIT) + k - SPLIT]
            acc += jnp.dot(matrix, u[slot], preferred_element_type=F32)
        image = acc
        start = v0[s]
        if first:
            image = image - SHIFT * start
            w_ref[s] = image
            terms = (start * start, start * image, image * image)
        else:
            terms = (start * image, w[s] * image, image * image)
        sums = [jnp.sum(x, axis=0, keepdims=True) for x in terms]
        sums_ref[...] += jnp.concatenate(sums + [jnp.zeros((5, R), F32)], axis=0)

    for s in range(NS):
        pl.when(count > s)(functools.partial(one, s))
    if first:
        picked(wout_ref, w_ref, got_index)


def picked(ref, w, index):
    chosen = jnp.zeros((WP, R), F32)
    for s in range(NS):
        chosen = chosen + jnp.where(index == s, w[s], 0.0)
    ref[0] = chosen.astype(BF16)


def pick_kernel(w, spill_in, win_ref):
    picked(win_ref, w, opened(spill_in[0])[1])


def finish_kernel(gathered, p0, q, out_ref, out, sems):
    total = jnp.sum(gathered[...], axis=0)
    s00, s01, s11, s02, s12, s22 = (total[i : i + 1, :] for i in range(6))
    c = SHIFT
    bb = s00 + EPS
    beta = jnp.sqrt(bb)
    h11 = (s01 + c * s00) / bb
    a = c - h11
    n2 = (s11 + 2 * a * s01 + a * a * s00) / bb
    h21s = jnp.maximum(n2, 0.0) + EPS
    h21 = jnp.sqrt(h21s)
    full = bb * h21s
    v0i = s01 + c * s00
    h12 = (s02 + a * v0i) / (bb * h21)
    cross = (s01 + a * s00) / (bb * h21)
    b2i = (s12 + a * s02 + a * (s11 + c * s01) + a * a * v0i) / full
    h22 = b2i - h12 * cross
    ii = (s22 + 2 * a * (s12 + c * s02) + a * a * (s11 + 2 * c * s01 + c * c * s00)) / full
    rest = (
        ii + h12 * h12 * (s00 / bb) + h22 * h22 * (n2 / h21s)
        - 2 * h12 * h12 - 2 * h22 * b2i + 2 * h12 * h22 * cross
    )
    h32s = jnp.maximum(rest, 0.0) + EPS
    g00 = h11 * h11 + h21s
    g01 = h11 * h12 + h21 * h22
    g11 = h12 * h12 + h22 * h22 + h32s
    det = g00 * g11 - g01 * g01
    y1 = beta * (g11 * h11 - g01 * h12) / det
    y2 = beta * (g00 * h12 - g01 * h11) / det
    two = y2 / (beta * h21)
    one = y1 / beta + a * two
    copies = []
    for begin, size in PARTS:
        for s in range(NS):
            p, r = p0[s, begin : begin + size, :], q[s, begin : begin + size, :]
            out[pl.ds(begin * NS + s, size, stride=NS), :] = one * p + two * r
        rows = pl.ds(begin * NS, size * NS)
        copies.append(pltpu.make_async_copy(out.at[rows, :], out_ref.at[rows, :], sems.at[len(copies)]))
        copies[-1].start()
    for copy in copies:
        copy.wait()


def permuted(x, target):
    parts = lax.axis_size("rhs")
    pairs = [(i, j) for i in range(NSUB) for j in range(parts)]
    return lax.ppermute(
        x, ("sub", "rhs"), [(i * parts + j, t[0] * parts + t[1]) for i, j in pairs for t in [target(i, j)]]
    )


def to_inner(x):
    return permuted(x, lambda i, j: (i ^ 1, j))


def to_outer(x):
    return permuted(x, lambda i, j: (i, j ^ 1) if i in (0, NSUB - 1) else (((i + 1) ^ 1) - 1, j))


def to_far(x):
    def target(i, j):
        if i in (0, NSUB - 1):
            return i ^ 1, j
        return i + (2 if i % 2 else -2), j

    return permuted(x, target)


def body(right_side, coupling, neighbours, inverse, margin, counts):
    here = lax.axis_index("sub").astype(jnp.int32).reshape(1)
    flat_right = right_side.transpose(1, 0, 2).reshape(W * NS, R)
    block, one = (NS, WP, R), (1, WP, R)
    v0, v0b = call(start_kernel, [(block, F32), (block, BF16)], [SM, VM])(counts, flat_right)
    outer, inner = to_outer(v0b), to_inner(v0b)

    coupling = pltpu.with_memory_space_constraint(coupling, pltpu.HBM)
    inverse, margin, neighbours = (
        pltpu.with_memory_space_constraint(a, pltpu.HBM) for a in (inverse, margin, neighbours)
    )

    def matrices(first, *more):
        lanes = GROUP * W
        blocks = (0, SPLIT) if first else (SPLIT, NB)
        begin = blocks[0] * W // GROUP
        end = -(-blocks[1] * W // GROUP)
        count = -(-(end - begin) // CHUNK) * CHUNK
        groups = (begin, begin + count) if first else (end - count, end)
        outs = [((NS * (blocks[1] - blocks[0]), WP, WP), BF16, pltpu.VMEM)]
        if first:
            outs += [((6 * W, 6 * W), BF16, pltpu.VMEM), ((TABLE,), jnp.int32, pltpu.SMEM)]
        return call(
            functools.partial(coupling_kernel, blocks, groups, first),
            outs,
            [ANY, ANY] + [SM] * (len(more) - 1),
            [
                pltpu.VMEM((NS, count * lanes), BF16),
                pltpu.VMEM((4 * NS, lanes), BF16),
                pltpu.VMEM((count * GROUP * NS + SPARE, 128), F32),
                pltpu.VMEM((count * GROUP * NS + SPARE, 128), F32),
                pltpu.SemaphoreType.DMA((count // CHUNK + 1,)),
            ],
            limit=24,
            cost=pl.CostEstimate(flops=1 << 20, bytes_accessed=12 << 20, transcendentals=0),
        )(coupling, *more)

    first_part, held, table = matrices(True, inverse, here, counts, margin, neighbours)
    table = pltpu.with_memory_space_constraint(table, pltpu.SMEM)
    held = pltpu.with_memory_space_constraint(held, pltpu.VMEM)
    first_part = pltpu.with_memory_space_constraint(first_part, pltpu.VMEM)

    def solve(own, inner, outer):
        (part,) = call(
            own_kernel, [((6 * W + 8, R), F32, pltpu.VMEM)], [VM, VM], [pltpu.VMEM((OWN, R), F32)],
            cost=pl.CostEstimate(flops=1 << 30, bytes_accessed=4 << 20, transcendentals=0),
        )(held, own)
        depth = 6 * W - FROM
        spill_in, ext = call(
            margin_kernel,
            [(one, BF16), ((depth, R), BF16)],
            [SM] + [VM] * 5,
            [pltpu.VMEM((depth + 8, R), F32)],
        )(table, held, part, own, inner, outer)
        got_in = to_inner(spill_in)
        out, spill_out = call(
            solve_kernel,
            [(block, F32), (one, BF16)],
            [SM] + [VM] * 3,
            [pltpu.VMEM((NS * W + 8, R), F32)],
            cost=pl.CostEstimate(flops=1 << 30, bytes_accessed=4 << 20, transcendentals=0),
        )(table, held, part, ext)
        return out, got_in, spill_out

    def system(first, out, got_in, spill_out, *more):
        part, sent, near = call(
            inner_kernel, [(block, F32), ((NS + 1, WP, R), BF16), (block, BF16)], [VM] * 3
        )(out, got_in, spill_out)
        got, near, far = to_outer(sent), to_inner(near), to_far(spill_out)
        if first:
            (made,) = matrices(False, sent)
            matrix_parts.append(pltpu.with_memory_space_constraint(made, pltpu.VMEM))
        outs = [(block, F32)] + ([(block, F32), (one, BF16)] if first else [])
        return call(
            functools.partial(system_kernel, first),
            outs + [((8, R), F32)],
            [SM] + [VM] * (7 + len(more)),
            [pltpu.VMEM((3 * NS, WP, R), BF16)],
        )(table, *matrix_parts, part, got, near, far, spill_out, *more)

    matrix_parts = [first_part]
    out, got_in, spill_out = solve(v0, inner, outer)
    p0, w, w_out, sums_one = system(True, out, got_in, spill_out, v0)
    outer = to_outer(w_out)
    (w_in,) = call(pick_kernel, [(one, BF16)], [VM] * 2)(w, got_in)
    q, sums_two = system(False, *solve(w, to_inner(w_in), outer), v0, w)
    sums = jnp.concatenate([sums_one[:3], sums_two[:3]], axis=0)
    sums = sums + to_inner(sums)
    gathered = lax.all_to_all(
        jnp.broadcast_to(sums[None], (NSUB // 2, 6, R)), "sub", 0, 0,
        axis_index_groups=[list(range(c, NSUB, 2)) for c in range(2)],
    )
    (flat,) = call(
        finish_kernel,
        [((W * NS, R), F32, pltpu.HBM)],
        [VM] * 3,
        [pltpu.VMEM((W * NS + SPARE, R), F32), pltpu.SemaphoreType.DMA((len(PARTS),))],
    )(gathered, p0, q)
    return flat.reshape(W, NS, R).transpose(1, 0, 2)


def solution(mesh):
    placed = (
        P("sub", None, "rhs"),
        P("sub", None),
        P("sub", None),
        P("sub", None, None),
        P("sub", None),
        P("sub"),
    )
    return jax.shard_map(
        body, mesh=mesh, in_specs=placed, out_specs=P("sub", None, "rhs"), check_vma=False
    )
```

```python
import functools
import jax
import jax.numpy as jnp
from jax import lax
from jax.experimental import pallas as pl
from jax.experimental.pallas import tpu as pltpu
from jax.sharding import PartitionSpec as P

EPS = 1e-06
W = 252
WP = 256
NS = 4
NB = 8
R = 128
NSUB = 64
SHIFT = 1.0
ROWS = NB * W
GROUP = 32
F32 = jnp.float32
BF16 = jnp.bfloat16
CHUNK = 8
SPLIT = 4
EVEN, FIRST, LAST, LOW, HIGH, COUNT, ENDS, NEXT, OUT, SLOTS = range(10)
TABLE = SLOTS + NS * NB
SPARE = 32
OWN = 1024
FROM = 896
ANY = pl.BlockSpec(memory_space=pl.ANY)
PARTS = ((0, 64), (64, 64), (128, 64), (192, 60))
VM = pl.BlockSpec(memory_space=pltpu.VMEM)
SM = pl.BlockSpec(memory_space=pltpu.SMEM)


def call(kernel, outs, ins, scratch=(), limit=24, cost=None):
    return pl.pallas_call(
        kernel,
        out_shape=[keep[0](s, d) if keep else jax.ShapeDtypeStruct(s, d) for s, d, *keep in outs],
        in_specs=ins,
        out_specs=[{pltpu.SMEM: SM, pltpu.HBM: ANY}.get(keep[0], VM) if keep else VM for _, _, *keep in outs],
        scratch_shapes=list(scratch),
        compiler_params=pltpu.CompilerParams(vmem_limit_bytes=limit << 20),
        cost_estimate=cost,
    )


def start_kernel(counts, right, v0_ref, v0b_ref):
    whole = W // 8 * 8
    tail = right[whole * NS :, :]
    for s in range(NS):
        alive = jnp.where(counts[0] > s, 1.0, 0.0)
        v0_ref[s, :whole, :] = right[pl.ds(s, whole, stride=NS), :] * alive
        last = [tail[NS * i + s : NS * i + s + 1, :] * alive for i in range(W - whole)]
        v0_ref[s, whole:, :] = jnp.concatenate(last + [jnp.zeros((WP - W, R), F32)], axis=0)
        v0b_ref[s] = v0_ref[s].astype(BF16)


def fill_table(table, place, counts, margin, neighbours):
    here = place[0]
    even = here % 2 == 0
    first, last = here == 0, here == NSUB - 1
    low = jnp.clip(margin[0, 0] - NS * jnp.maximum(here - 1, 0), 0, NS - 1)
    high = jnp.clip(margin[0, 1] - NS * jnp.minimum(here + 1, NSUB - 1), 0, NS - 1)
    table[EVEN] = jnp.where(even, 1, 0)
    table[FIRST] = jnp.where(first, 1, 0)
    table[LAST] = jnp.where(last, 1, 0)
    table[LOW] = low
    table[HIGH] = high
    table[COUNT] = counts[0]
    table[ENDS] = jnp.where(jnp.logical_or(first, last), 1, 0)
    table[NEXT] = jnp.where(jnp.logical_or(here == 1, here == NSUB - 2), 1, 0)
    table[OUT] = jnp.where(even, low, high)
    for s in range(NS):
        for k in range(NB):
            slot = jnp.clip(neighbours[s, k] - NS * (here - 1), 0, 3 * NS - 1)
            table[SLOTS + s * NB + k] = jnp.where(even, slot, slot + 2 * NS * (1 - slot // NS))


def coupling_kernel(blocks, groups, first, flat, *rest):
    if first:
        inverse, place, counts, margin, neighbours, c_ref, inverse_ref, table, raw, x, lo, hi, sems = rest
    else:
        _, c_ref, raw, x, lo, hi, sems = rest
    lanes = GROUP * W
    count = groups[1] - groups[0]
    step = CHUNK * lanes
    chunks = count // CHUNK
    copies = [
        pltpu.make_async_copy(
            flat.at[:, pl.ds(groups[0] * lanes + c * step, step)],
            raw.at[:, pl.ds(c * step, step)],
            sems.at[c],
        )
        for c in range(chunks)
    ]
    if first:
        copies.append(pltpu.make_async_copy(inverse.at[0], inverse_ref, sems.at[chunks]))
    for copy in copies:
        copy.start()
    if first:
        fill_table(table, place, counts, margin, neighbours)
    lane = lax.broadcasted_iota(jnp.int32, (4 * NS, 128), 1)

    def four(i, carry):
        for h in range(4):
            at = pl.multiple_of((4 * i + h) * lanes, 128)
            x[NS * h : NS * h + NS, :] = raw[:, pl.ds(at, lanes)]
        base = pl.multiple_of(4 * i * (GROUP * NS), 8)
        for s in range(GROUP):
            def rolled(t):
                piece = x[:, 128 * t : 128 * t + 128]
                return pltpu.roll(piece, 4 * s, 1) if s else piece

            middle = rolled(2 * s)
            if s == 0:
                left, right = middle, rolled(1)
            else:
                early = lane < 4 * s
                left = jnp.where(early, rolled(2 * s - 1), middle)
                right = jnp.where(early, middle, rolled(2 * s + 1)) if s < GROUP - 1 else middle
            left, right = left.astype(F32), right.astype(F32)
            for h in range(4):
                at = base + (h * GROUP + s) * NS
                lo[pl.ds(at, NS), :] = left[NS * h : NS * h + NS]
                hi[pl.ds(at, NS), :] = right[NS * h : NS * h + NS]
        return carry

    for c in range(chunks):
        copies[c].wait()
        lax.fori_loop(c * CHUNK // 4, (c + 1) * CHUNK // 4, four, 0)
    keep = lax.broadcasted_iota(jnp.int32, (WP, 128), 1) < W - 128
    pad = jnp.zeros((WP - W, 128), F32)
    skip = (blocks[0] * W - groups[0] * GROUP) * NS
    number = blocks[1] - blocks[0]

    def place(k, carry):
        for p in range(NS):
            row = skip + k * (W * NS) + p
            left = lo[pl.ds(row, W, stride=NS), :]
            right = hi[pl.ds(row, W, stride=NS), :]
            right = jnp.where(keep, jnp.concatenate([right, pad], axis=0), 0.0)
            c_ref[p * number + k, :, :128] = jnp.concatenate([left, pad], axis=0).astype(BF16)
            c_ref[p * number + k, :, 128:] = right.astype(BF16)
        return carry

    lax.fori_loop(0, number, place, 0)
    if first:
        copies[chunks].wait()


def own_kernel(inverse, own, part_ref, ext):
    for s in range(NS):
        ext[s * W : (s + 1) * W, :] = own[s, :W, :]
    ext[NS * W :, :] = jnp.zeros((OWN - NS * W, R), F32)
    part_ref[: 6 * W, :] = jnp.dot(inverse[:, :OWN], ext[...].astype(BF16), preferred_element_type=F32)


def places(table):
    return table[EVEN] == 1, table[FIRST] == 1, table[LAST] == 1, table[LOW], table[HIGH]


def spilled(inverse, part, ext, block, index):
    begin = block * W // 16 * 16
    end = -(-(block + 1) * W // 16) * 16
    end = min(end, 6 * W)
    rows = jnp.dot(inverse[begin:end, FROM:], ext, preferred_element_type=F32)
    rows = rows[block * W - begin : (block + 1) * W - begin] + part[block * W : (block + 1) * W, :]
    mark = jnp.ones((WP - W, R), F32) * index.astype(F32)
    return jnp.concatenate([rows, mark], axis=0)


def margin_kernel(table, inverse, part, own, inner, outer, in_ref, ext_ref, ext):
    even, first, last, low, high = places(table)
    odd = jnp.logical_not(even)
    ext[: NS * W - FROM, :] = jnp.zeros((NS * W - FROM, R), F32)
    some = inner.shape[0] > 1

    def put(when, block, source, index):
        @pl.when(when)
        def _():
            ext[block * W - FROM : (block + 1) * W - FROM, :] = source[index].astype(F32)[:W]

    put(first, NS, own, low)
    put(jnp.logical_and(even, jnp.logical_not(first)), NS, outer, low if some else 0)
    put(odd, NS, inner, low if some else 0)
    put(last, NS + 1, own, high)
    put(jnp.logical_and(odd, jnp.logical_not(last)), NS + 1, outer, high if some else 0)
    put(even, NS + 1, inner, high if some else 0)
    ext_ref[...] = ext[: 6 * W - FROM, :].astype(BF16)

    @pl.when(even)
    def _():
        in_ref[0] = spilled(inverse, part, ext_ref[...], NS + 1, high).astype(BF16)

    @pl.when(odd)
    def _():
        in_ref[0] = spilled(inverse, part, ext_ref[...], NS, low).astype(BF16)


def solve_kernel(table, inverse, part, ext, out_ref, out2_ref, res):
    even, first, last, low, high = places(table)
    mine = NS * W
    res[:mine, :] = part[:mine, :] + jnp.dot(inverse[:mine, FROM:], ext[...], preferred_element_type=F32)
    pad = jnp.zeros((WP - W, R), F32)
    for s in range(NS):
        out_ref[s] = jnp.concatenate([res[s * W : (s + 1) * W, :], pad], axis=0)
    keep = lax.broadcasted_iota(jnp.int32, (WP, R), 0) < W

    def spill(when, ends, block, index):
        @pl.when(when)
        def _():
            rows = spilled(inverse, part, ext[...], block, index)
            out2_ref[0] = rows.astype(BF16)

            @pl.when(ends)
            def _():
                out_ref[index] += jnp.where(keep, rows, 0.0)

    spill(even, first, NS, low)
    spill(jnp.logical_not(even), last, NS + 1, high)


def opened(block):
    x = block.astype(F32)
    rows = lax.broadcasted_iota(jnp.int32, x.shape, 0)
    return jnp.where(rows < W, x, 0.0), x[W : W + 1, :]


def inner_kernel(out, spill_in, spill_out, part_ref, sent_ref, near_ref):
    values, index = opened(spill_in[0])
    for s in range(NS):
        part = out[s] + jnp.where(index == s, values, 0.0)
        part_ref[s] = part
        sent_ref[s] = part.astype(BF16)
        near_ref[s] = part.astype(BF16)
    sent_ref[NS] = spill_out[0]


def system_kernel(
    first, table, ca, cb, part, got, near, far, spill_out, v0, *rest
):
    if first:
        p_ref, w_ref, wout_ref, sums_ref, u = rest
    else:
        w, sums_one, p_ref, sums_ref, u = rest
    got_values, got_index = opened(got[NS])
    got_index = jnp.where(table[ENDS] == 1, -1.0, got_index)
    far_index = jnp.where(table[NEXT] == 1, -1.0, far[0, W : W + 1, :].astype(F32))
    inside = lax.broadcasted_iota(jnp.int32, (WP, R), 0) < W
    far_values = jnp.where(inside, far[0], jnp.zeros((), BF16))
    count = table[COUNT]
    for s in range(NS):
        alive = jnp.where(count > s, 1.0, 0.0)
        p = (part[s] + jnp.where(got_index == s, got_values, 0.0)) * alive
        p_ref[s] = p
        u[s] = got[s]
        u[NS + s] = p.astype(BF16)
        u[2 * NS + s] = near[s] + jnp.where(
            jnp.broadcast_to(far_index, (WP, R)) == s, far_values, jnp.zeros((), BF16)
        )
    index = table[OUT]
    u[index] = (got[index].astype(F32) + opened(spill_out[0])[0]).astype(BF16)
    if first:
        sums_ref[...] = jnp.zeros((6, R), F32)
    else:
        sums_ref[...] = sums_one[...]
    if first:
        w_ref[...] = jnp.zeros((NS, WP, R), F32)

    def one(s):
        acc = p_ref[s]
        for k in range(NB):
            slot = table[SLOTS + s * NB + k]
            matrix = ca[s * SPLIT + k] if k < SPLIT else cb[s * (NB - SPLIT) + k - SPLIT]
            acc += jnp.dot(matrix, u[slot], preferred_element_type=F32)
        image = acc
        start = v0[s]
        if first:
            image = image - SHIFT * start
            w_ref[s] = image
            terms = (start * start, start * image, image * image)
        else:
            terms = (start * image, w[s] * image, image * image)
        sums = [jnp.sum(x, axis=0, keepdims=True) for x in terms]
        rest_of_six = [jnp.zeros((3, R), F32)]
        sums_ref[...] += jnp.concatenate(sums + rest_of_six if first else rest_of_six + sums, axis=0)

    for s in range(NS):
        pl.when(count > s)(functools.partial(one, s))
    if first:
        picked(wout_ref, w_ref, got_index)


def picked(ref, w, index):
    chosen = jnp.zeros((WP, R), F32)
    for s in range(NS):
        chosen = chosen + jnp.where(index == s, w[s], 0.0)
    ref[0] = chosen.astype(BF16)


def pick_kernel(w, spill_in, win_ref):
    picked(win_ref, w, opened(spill_in[0])[1])


def finish_kernel(gathered, p0, q, out_ref, out, sems):
    total = jnp.sum(gathered[...], axis=0)
    s00, s01, s11, s02, s12, s22 = (total[i : i + 1, :] for i in range(6))
    c = SHIFT
    bb = s00 + EPS
    beta = jnp.sqrt(bb)
    h11 = (s01 + c * s00) / bb
    a = c - h11
    n2 = (s11 + 2 * a * s01 + a * a * s00) / bb
    h21s = jnp.maximum(n2, 0.0) + EPS
    h21 = jnp.sqrt(h21s)
    full = bb * h21s
    v0i = s01 + c * s00
    h12 = (s02 + a * v0i) / (bb * h21)
    cross = (s01 + a * s00) / (bb * h21)
    b2i = (s12 + a * s02 + a * (s11 + c * s01) + a * a * v0i) / full
    h22 = b2i - h12 * cross
    ii = (s22 + 2 * a * (s12 + c * s02) + a * a * (s11 + 2 * c * s01 + c * c * s00)) / full
    rest = (
        ii + h12 * h12 * (s00 / bb) + h22 * h22 * (n2 / h21s)
        - 2 * h12 * h12 - 2 * h22 * b2i + 2 * h12 * h22 * cross
    )
    h32s = jnp.maximum(rest, 0.0) + EPS
    g00 = h11 * h11 + h21s
    g01 = h11 * h12 + h21 * h22
    g11 = h12 * h12 + h22 * h22 + h32s
    det = g00 * g11 - g01 * g01
    y1 = beta * (g11 * h11 - g01 * h12) / det
    y2 = beta * (g00 * h12 - g01 * h11) / det
    two = y2 / (beta * h21)
    one = y1 / beta + a * two
    copies = []
    for begin, size in PARTS:
        for s in range(NS):
            p, r = p0[s, begin : begin + size, :], q[s, begin : begin + size, :]
            out[pl.ds(begin * NS + s, size, stride=NS), :] = one * p + two * r
        rows = pl.ds(begin * NS, size * NS)
        copies.append(pltpu.make_async_copy(out.at[rows, :], out_ref.at[rows, :], sems.at[len(copies)]))
        copies[-1].start()
    for copy in copies:
        copy.wait()


def permuted(x, target):
    parts = lax.axis_size("rhs")
    pairs = [(i, j) for i in range(NSUB) for j in range(parts)]
    return lax.ppermute(
        x, ("sub", "rhs"), [(i * parts + j, t[0] * parts + t[1]) for i, j in pairs for t in [target(i, j)]]
    )


def to_inner(x):
    return permuted(x, lambda i, j: (i ^ 1, j))


def to_outer(x):
    return permuted(x, lambda i, j: (i, j ^ 1) if i in (0, NSUB - 1) else (((i + 1) ^ 1) - 1, j))


def to_far(x):
    def target(i, j):
        if i in (0, NSUB - 1):
            return i ^ 1, j
        return i + (2 if i % 2 else -2), j

    return permuted(x, target)


def body(right_side, coupling, neighbours, inverse, margin, counts):
    here = lax.axis_index("sub").astype(jnp.int32).reshape(1)
    flat_right = right_side.transpose(1, 0, 2).reshape(W * NS, R)
    block, one = (NS, WP, R), (1, WP, R)
    v0, v0b = call(start_kernel, [(block, F32), (block, BF16)], [SM, VM])(counts, flat_right)
    outer, inner = to_outer(v0b), to_inner(v0b)

    coupling = pltpu.with_memory_space_constraint(coupling, pltpu.HBM)
    inverse, margin, neighbours = (
        pltpu.with_memory_space_constraint(a, pltpu.HBM) for a in (inverse, margin, neighbours)
    )

    def matrices(first, *more):
        lanes = GROUP * W
        blocks = (0, SPLIT) if first else (SPLIT, NB)
        begin = blocks[0] * W // GROUP
        end = -(-blocks[1] * W // GROUP)
        count = -(-(end - begin) // CHUNK) * CHUNK
        groups = (begin, begin + count) if first else (end - count, end)
        outs = [((NS * (blocks[1] - blocks[0]), WP, WP), BF16, pltpu.VMEM)]
        if first:
            outs += [((6 * W, 6 * W), BF16, pltpu.VMEM), ((TABLE,), jnp.int32, pltpu.SMEM)]
        return call(
            functools.partial(coupling_kernel, blocks, groups, first),
            outs,
            [ANY, ANY] + [SM] * (len(more) - 1),
            [
                pltpu.VMEM((NS, count * lanes), BF16),
                pltpu.VMEM((4 * NS, lanes), BF16),
                pltpu.VMEM((count * GROUP * NS + SPARE, 128), F32),
                pltpu.VMEM((count * GROUP * NS + SPARE, 128), F32),
                pltpu.SemaphoreType.DMA((count // CHUNK + 1,)),
            ],
            limit=24,
            cost=pl.CostEstimate(flops=1 << 20, bytes_accessed=12 << 20, transcendentals=0),
        )(coupling, *more)

    first_part, held, table = matrices(True, inverse, here, counts, margin, neighbours)
    table = pltpu.with_memory_space_constraint(table, pltpu.SMEM)
    held = pltpu.with_memory_space_constraint(held, pltpu.VMEM)
    first_part = pltpu.with_memory_space_constraint(first_part, pltpu.VMEM)

    def solve(own, inner, outer):
        (part,) = call(
            own_kernel, [((6 * W + 8, R), F32, pltpu.VMEM)], [VM, VM], [pltpu.VMEM((OWN, R), F32)],
            cost=pl.CostEstimate(flops=1 << 30, bytes_accessed=4 << 20, transcendentals=0),
        )(held, own)
        depth = 6 * W - FROM
        spill_in, ext = call(
            margin_kernel,
            [(one, BF16), ((depth, R), BF16)],
            [SM] + [VM] * 5,
            [pltpu.VMEM((depth + 8, R), F32)],
        )(table, held, part, own, inner, outer)
        got_in = to_inner(spill_in)
        out, spill_out = call(
            solve_kernel,
            [(block, F32), (one, BF16)],
            [SM] + [VM] * 3,
            [pltpu.VMEM((NS * W + 8, R), F32)],
            cost=pl.CostEstimate(flops=1 << 30, bytes_accessed=4 << 20, transcendentals=0),
        )(table, held, part, ext)
        return out, got_in, spill_out

    def system(first, out, got_in, spill_out, *more):
        part, sent, near = call(
            inner_kernel, [(block, F32), ((NS + 1, WP, R), BF16), (block, BF16)], [VM] * 3
        )(out, got_in, spill_out)
        got, near, far = to_outer(sent), to_inner(near), to_far(spill_out)
        if first:
            (made,) = matrices(False, sent)
            matrix_parts.append(pltpu.with_memory_space_constraint(made, pltpu.VMEM))
        outs = [(block, F32)] + ([(block, F32), (one, BF16)] if first else [])
        return call(
            functools.partial(system_kernel, first),
            outs + [((6, R), F32)],
            [SM] + [VM] * (7 + len(more)),
            [pltpu.VMEM((3 * NS, WP, R), BF16)],
        )(table, *matrix_parts, part, got, near, far, spill_out, *more)

    matrix_parts = [first_part]
    out, got_in, spill_out = solve(v0, inner, outer)
    p0, w, w_out, sums_one = system(True, out, got_in, spill_out, v0)
    outer = to_outer(w_out)
    (w_in,) = call(pick_kernel, [(one, BF16)], [VM] * 2)(w, got_in)
    q, sums = system(False, *solve(w, to_inner(w_in), outer), v0, w, sums_one)
    sums = sums + to_inner(sums)
    gathered = lax.all_to_all(
        jnp.broadcast_to(sums[None], (NSUB // 2, 6, R)), "sub", 0, 0,
        axis_index_groups=[list(range(c, NSUB, 2)) for c in range(2)],
    )
    (flat,) = call(
        finish_kernel,
        [((W * NS, R), F32, pltpu.HBM)],
        [VM] * 3,
        [pltpu.VMEM((W * NS + SPARE, R), F32), pltpu.SemaphoreType.DMA((len(PARTS),))],
    )(gathered, p0, q)
    return flat.reshape(W, NS, R).transpose(1, 0, 2)


def solution(mesh):
    placed = (
        P("sub", None, "rhs"),
        P("sub", None),
        P("sub", None),
        P("sub", None, None),
        P("sub", None),
        P("sub"),
    )
    return jax.shard_map(
        body, mesh=mesh, in_specs=placed, out_specs=P("sub", None, "rhs"), check_vma=False
    )
```

```python
import functools
import jax
import jax.numpy as jnp
from jax import lax
from jax.experimental import pallas as pl
from jax.experimental.pallas import tpu as pltpu
from jax.sharding import PartitionSpec as P

EPS = 1e-06
W = 252
WP = 256
NS = 4
NB = 8
R = 128
NSUB = 64
SHIFT = 1.0
ROWS = NB * W
GROUP = 32
F32 = jnp.float32
BF16 = jnp.bfloat16
CHUNK = 8
SPLIT = 4
EVEN, FIRST, LAST, LOW, HIGH, COUNT, ENDS, NEXT, OUT, SLOTS = range(10)
TABLE = SLOTS + NS * NB
SPARE = 32
OWN = 1024
FROM = 896
ANY = pl.BlockSpec(memory_space=pl.ANY)
PARTS = ((0, 64), (64, 64), (128, 64), (192, 60))
VM = pl.BlockSpec(memory_space=pltpu.VMEM)
SM = pl.BlockSpec(memory_space=pltpu.SMEM)


def call(kernel, outs, ins, scratch=(), limit=24, cost=None):
    return pl.pallas_call(
        kernel,
        out_shape=[keep[0](s, d) if keep else jax.ShapeDtypeStruct(s, d) for s, d, *keep in outs],
        in_specs=ins,
        out_specs=[{pltpu.SMEM: SM, pltpu.HBM: ANY}.get(keep[0], VM) if keep else VM for _, _, *keep in outs],
        scratch_shapes=list(scratch),
        compiler_params=pltpu.CompilerParams(vmem_limit_bytes=limit << 20),
        cost_estimate=cost,
    )


def start_kernel(counts, right, v0_ref, v0b_ref):
    whole = W // 8 * 8
    tail = right[whole * NS :, :]
    for s in range(NS):
        alive = jnp.where(counts[0] > s, 1.0, 0.0)
        v0_ref[s, :whole, :] = right[pl.ds(s, whole, stride=NS), :] * alive
        last = [tail[NS * i + s : NS * i + s + 1, :] * alive for i in range(W - whole)]
        v0_ref[s, whole:, :] = jnp.concatenate(last + [jnp.zeros((WP - W, R), F32)], axis=0)
        v0b_ref[s] = v0_ref[s].astype(BF16)


def fill_table(table, place, counts, margin, neighbours):
    here = place[0]
    even = here % 2 == 0
    first, last = here == 0, here == NSUB - 1
    low = jnp.clip(margin[0, 0] - NS * jnp.maximum(here - 1, 0), 0, NS - 1)
    high = jnp.clip(margin[0, 1] - NS * jnp.minimum(here + 1, NSUB - 1), 0, NS - 1)
    table[EVEN] = jnp.where(even, 1, 0)
    table[FIRST] = jnp.where(first, 1, 0)
    table[LAST] = jnp.where(last, 1, 0)
    table[LOW] = low
    table[HIGH] = high
    table[COUNT] = counts[0]
    table[ENDS] = jnp.where(jnp.logical_or(first, last), 1, 0)
    table[NEXT] = jnp.where(jnp.logical_or(here == 1, here == NSUB - 2), 1, 0)
    table[OUT] = jnp.where(even, low, high)
    for s in range(NS):
        for k in range(NB):
            slot = jnp.clip(neighbours[s, k] - NS * (here - 1), 0, 3 * NS - 1)
            table[SLOTS + s * NB + k] = jnp.where(even, slot, slot + 2 * NS * (1 - slot // NS))


def coupling_kernel(blocks, groups, first, flat, *rest):
    if first:
        inverse, place, counts, margin, neighbours, c_ref, inverse_ref, table, raw, x, lo, hi, sems = rest
    else:
        _, c_ref, raw, x, lo, hi, sems = rest
    lanes = GROUP * W
    count = groups[1] - groups[0]
    step = CHUNK * lanes
    chunks = count // CHUNK
    copies = [
        pltpu.make_async_copy(
            flat.at[:, pl.ds(groups[0] * lanes + c * step, step)],
            raw.at[:, pl.ds(c * step, step)],
            sems.at[c],
        )
        for c in range(chunks)
    ]
    if first:
        copies.append(pltpu.make_async_copy(inverse.at[0], inverse_ref, sems.at[chunks]))
    for copy in copies:
        copy.start()
    if first:
        fill_table(table, place, counts, margin, neighbours)
    lane = lax.broadcasted_iota(jnp.int32, (4 * NS, 128), 1)

    def four(i, carry):
        for h in range(4):
            at = pl.multiple_of((4 * i + h) * lanes, 128)
            x[NS * h : NS * h + NS, :] = raw[:, pl.ds(at, lanes)]
        base = pl.multiple_of(4 * i * (GROUP * NS), 8)
        for s in range(GROUP):
            def rolled(t):
                piece = x[:, 128 * t : 128 * t + 128]
                return pltpu.roll(piece, 4 * s, 1) if s else piece

            middle = rolled(2 * s)
            if s == 0:
                left, right = middle, rolled(1)
            else:
                early = lane < 4 * s
                left = jnp.where(early, rolled(2 * s - 1), middle)
                right = jnp.where(early, middle, rolled(2 * s + 1)) if s < GROUP - 1 else middle
            left, right = left.astype(F32), right.astype(F32)
            for h in range(4):
                at = base + (h * GROUP + s) * NS
                lo[pl.ds(at, NS), :] = left[NS * h : NS * h + NS]
                hi[pl.ds(at, NS), :] = right[NS * h : NS * h + NS]
        return carry

    for c in range(chunks):
        copies[c].wait()
        lax.fori_loop(c * CHUNK // 4, (c + 1) * CHUNK // 4, four, 0)
    keep = lax.broadcasted_iota(jnp.int32, (WP, 128), 1) < W - 128
    pad = jnp.zeros((WP - W, 128), F32)
    skip = (blocks[0] * W - groups[0] * GROUP) * NS
    number = blocks[1] - blocks[0]

    def place(k, carry):
        for p in range(NS):
            row = skip + k * (W * NS) + p
            left = lo[pl.ds(row, W, stride=NS), :]
            right = hi[pl.ds(row, W, stride=NS), :]
            right = jnp.where(keep, jnp.concatenate([right, pad], axis=0), 0.0)
            c_ref[p * number + k, :, :128] = jnp.concatenate([left, pad], axis=0).astype(BF16)
            c_ref[p * number + k, :, 128:] = right.astype(BF16)
        return carry

    lax.fori_loop(0, number, place, 0)
    if first:
        copies[chunks].wait()


def own_kernel(inverse, own, part_ref, ext):
    for s in range(NS):
        ext[s * W : (s + 1) * W, :] = own[s, :W, :]
    ext[NS * W :, :] = jnp.zeros((OWN - NS * W, R), F32)
    part_ref[: 6 * W, :] = jnp.dot(inverse[:, :OWN], ext[...].astype(BF16), preferred_element_type=F32)


def places(table):
    return table[EVEN] == 1, table[FIRST] == 1, table[LAST] == 1, table[LOW], table[HIGH]


def spilled(inverse, part, ext, block, index):
    begin = block * W // 16 * 16
    end = -(-(block + 1) * W // 16) * 16
    end = min(end, 6 * W)
    rows = jnp.dot(inverse[begin:end, FROM:], ext, preferred_element_type=F32)
    rows = rows[block * W - begin : (block + 1) * W - begin] + part[block * W : (block + 1) * W, :]
    mark = jnp.ones((WP - W, R), F32) * index.astype(F32)
    return jnp.concatenate([rows, mark], axis=0)


def margin_kernel(table, inverse, part, own, inner, outer, in_ref, ext_ref, ext):
    even, first, last, low, high = places(table)
    odd = jnp.logical_not(even)
    ext[: NS * W - FROM, :] = jnp.zeros((NS * W - FROM, R), F32)
    some = inner.shape[0] > 1

    def put(when, block, source, index):
        @pl.when(when)
        def _():
            ext[block * W - FROM : (block + 1) * W - FROM, :] = source[index].astype(F32)[:W]

    put(first, NS, own, low)
    put(jnp.logical_and(even, jnp.logical_not(first)), NS, outer, low if some else 0)
    put(odd, NS, inner, low if some else 0)
    put(last, NS + 1, own, high)
    put(jnp.logical_and(odd, jnp.logical_not(last)), NS + 1, outer, high if some else 0)
    put(even, NS + 1, inner, high if some else 0)
    ext_ref[...] = ext[: 6 * W - FROM, :].astype(BF16)

    @pl.when(even)
    def _():
        in_ref[0] = spilled(inverse, part, ext_ref[...], NS + 1, high).astype(BF16)

    @pl.when(odd)
    def _():
        in_ref[0] = spilled(inverse, part, ext_ref[...], NS, low).astype(BF16)


def solve_kernel(table, inverse, part, ext, out_ref, out2_ref, res):
    even, first, last, low, high = places(table)
    mine = NS * W
    res[:mine, :] = part[:mine, :] + jnp.dot(inverse[:mine, FROM:], ext[...], preferred_element_type=F32)
    pad = jnp.zeros((WP - W, R), F32)
    for s in range(NS):
        out_ref[s] = jnp.concatenate([res[s * W : (s + 1) * W, :], pad], axis=0)
    keep = lax.broadcasted_iota(jnp.int32, (WP, R), 0) < W

    def spill(when, ends, block, index):
        @pl.when(when)
        def _():
            rows = spilled(inverse, part, ext[...], block, index)
            out2_ref[0] = rows.astype(BF16)

            @pl.when(ends)
            def _():
                out_ref[index] += jnp.where(keep, rows, 0.0)

    spill(even, first, NS, low)
    spill(jnp.logical_not(even), last, NS + 1, high)


def opened(block):
    x = block.astype(F32)
    rows = lax.broadcasted_iota(jnp.int32, x.shape, 0)
    return jnp.where(rows < W, x, 0.0), x[W : W + 1, :]


def inner_kernel(out, spill_in, spill_out, part_ref, sent_ref, near_ref):
    values, index = opened(spill_in[0])
    for s in range(NS):
        part = out[s] + jnp.where(index == s, values, 0.0)
        part_ref[s] = part
        sent_ref[s] = part.astype(BF16)
        near_ref[s] = part.astype(BF16)
    sent_ref[NS] = spill_out[0]


def system_kernel(
    first, table, ca, cb, part, got, near, far, spill_out, v0, *rest
):
    if first:
        p_ref, w_ref, wout_ref, u = rest
    else:
        w, sums_one, p_ref, sums_ref, u = rest
    got_values, got_index = opened(got[NS])
    got_index = jnp.where(table[ENDS] == 1, -1.0, got_index)
    far_index = jnp.where(table[NEXT] == 1, -1.0, far[0, W : W + 1, :].astype(F32))
    inside = lax.broadcasted_iota(jnp.int32, (WP, R), 0) < W
    far_values = jnp.where(inside, far[0], jnp.zeros((), BF16))
    count = table[COUNT]
    for s in range(NS):
        alive = jnp.where(count > s, 1.0, 0.0)
        p = (part[s] + jnp.where(got_index == s, got_values, 0.0)) * alive
        p_ref[s] = p
        u[s] = got[s]
        u[NS + s] = p.astype(BF16)
        u[2 * NS + s] = near[s] + jnp.where(
            jnp.broadcast_to(far_index, (WP, R)) == s, far_values, jnp.zeros((), BF16)
        )
    index = table[OUT]
    u[index] = (got[index].astype(F32) + opened(spill_out[0])[0]).astype(BF16)
    if not first:
        sums_ref[...] = sums_one[...]
    if first:
        w_ref[...] = jnp.zeros((NS, WP, R), F32)

    def one(s):
        acc = p_ref[s]
        for k in range(NB):
            slot = table[SLOTS + s * NB + k]
            matrix = ca[s * SPLIT + k] if k < SPLIT else cb[s * (NB - SPLIT) + k - SPLIT]
            acc += jnp.dot(matrix, u[slot], preferred_element_type=F32)
        image = acc
        start = v0[s]
        if first:
            w_ref[s] = image - SHIFT * start
        else:
            add_sums(sums_ref, 3, (start * image, w[s] * image, image * image))

    for s in range(NS):
        pl.when(count > s)(functools.partial(one, s))
    if first:
        picked(wout_ref, w_ref, got_index)


def add_sums(ref, row, terms):
    ref[row : row + 3, :] += jnp.concatenate([jnp.sum(x, axis=0, keepdims=True) for x in terms], axis=0)


def first_sums_kernel(v0, w, _, sums_ref):
    sums_ref[...] = jnp.zeros((6, R), F32)
    for s in range(NS):
        add_sums(sums_ref, 0, (v0[s] * v0[s], v0[s] * w[s], w[s] * w[s]))


def picked(ref, w, index):
    chosen = jnp.zeros((WP, R), F32)
    for s in range(NS):
        chosen = chosen + jnp.where(index == s, w[s], 0.0)
    ref[0] = chosen.astype(BF16)


def pick_kernel(w, spill_in, win_ref):
    picked(win_ref, w, opened(spill_in[0])[1])


def finish_kernel(gathered, p0, q, out_ref, out, sems):
    total = jnp.sum(gathered[...], axis=0)
    s00, s01, s11, s02, s12, s22 = (total[i : i + 1, :] for i in range(6))
    c = SHIFT
    bb = s00 + EPS
    beta = jnp.sqrt(bb)
    h11 = (s01 + c * s00) / bb
    a = c - h11
    n2 = (s11 + 2 * a * s01 + a * a * s00) / bb
    h21s = jnp.maximum(n2, 0.0) + EPS
    h21 = jnp.sqrt(h21s)
    full = bb * h21s
    v0i = s01 + c * s00
    h12 = (s02 + a * v0i) / (bb * h21)
    cross = (s01 + a * s00) / (bb * h21)
    b2i = (s12 + a * s02 + a * (s11 + c * s01) + a * a * v0i) / full
    h22 = b2i - h12 * cross
    ii = (s22 + 2 * a * (s12 + c * s02) + a * a * (s11 + 2 * c * s01 + c * c * s00)) / full
    rest = (
        ii + h12 * h12 * (s00 / bb) + h22 * h22 * (n2 / h21s)
        - 2 * h12 * h12 - 2 * h22 * b2i + 2 * h12 * h22 * cross
    )
    h32s = jnp.maximum(rest, 0.0) + EPS
    g00 = h11 * h11 + h21s
    g01 = h11 * h12 + h21 * h22
    g11 = h12 * h12 + h22 * h22 + h32s
    det = g00 * g11 - g01 * g01
    y1 = beta * (g11 * h11 - g01 * h12) / det
    y2 = beta * (g00 * h12 - g01 * h11) / det
    two = y2 / (beta * h21)
    one = y1 / beta + a * two
    copies = []
    for begin, size in PARTS:
        for s in range(NS):
            p, r = p0[s, begin : begin + size, :], q[s, begin : begin + size, :]
            out[pl.ds(begin * NS + s, size, stride=NS), :] = one * p + two * r
        rows = pl.ds(begin * NS, size * NS)
        copies.append(pltpu.make_async_copy(out.at[rows, :], out_ref.at[rows, :], sems.at[len(copies)]))
        copies[-1].start()
    for copy in copies:
        copy.wait()


def permuted(x, target):
    parts = lax.axis_size("rhs")
    pairs = [(i, j) for i in range(NSUB) for j in range(parts)]
    return lax.ppermute(
        x, ("sub", "rhs"), [(i * parts + j, t[0] * parts + t[1]) for i, j in pairs for t in [target(i, j)]]
    )


def to_inner(x):
    return permuted(x, lambda i, j: (i ^ 1, j))


def to_outer(x):
    return permuted(x, lambda i, j: (i, j ^ 1) if i in (0, NSUB - 1) else (((i + 1) ^ 1) - 1, j))


def to_far(x):
    def target(i, j):
        if i in (0, NSUB - 1):
            return i ^ 1, j
        return i + (2 if i % 2 else -2), j

    return permuted(x, target)


def body(right_side, coupling, neighbours, inverse, margin, counts):
    here = lax.axis_index("sub").astype(jnp.int32).reshape(1)
    flat_right = right_side.transpose(1, 0, 2).reshape(W * NS, R)
    block, one = (NS, WP, R), (1, WP, R)
    v0, v0b = call(start_kernel, [(block, F32), (block, BF16)], [SM, VM])(counts, flat_right)
    outer, inner = to_outer(v0b), to_inner(v0b)

    coupling = pltpu.with_memory_space_constraint(coupling, pltpu.HBM)
    inverse, margin, neighbours = (
        pltpu.with_memory_space_constraint(a, pltpu.HBM) for a in (inverse, margin, neighbours)
    )

    def matrices(first, *more):
        lanes = GROUP * W
        blocks = (0, SPLIT) if first else (SPLIT, NB)
        begin = blocks[0] * W // GROUP
        end = -(-blocks[1] * W // GROUP)
        count = -(-(end - begin) // CHUNK) * CHUNK
        groups = (begin, begin + count) if first else (end - count, end)
        outs = [((NS * (blocks[1] - blocks[0]), WP, WP), BF16, pltpu.VMEM)]
        if first:
            outs += [((6 * W, 6 * W), BF16, pltpu.VMEM), ((TABLE,), jnp.int32, pltpu.SMEM)]
        return call(
            functools.partial(coupling_kernel, blocks, groups, first),
            outs,
            [ANY, ANY] + [SM] * (len(more) - 1),
            [
                pltpu.VMEM((NS, count * lanes), BF16),
                pltpu.VMEM((4 * NS, lanes), BF16),
                pltpu.VMEM((count * GROUP * NS + SPARE, 128), F32),
                pltpu.VMEM((count * GROUP * NS + SPARE, 128), F32),
                pltpu.SemaphoreType.DMA((count // CHUNK + 1,)),
            ],
            limit=24,
            cost=pl.CostEstimate(flops=1 << 20, bytes_accessed=12 << 20, transcendentals=0),
        )(coupling, *more)

    first_part, held, table = matrices(True, inverse, here, counts, margin, neighbours)
    table = pltpu.with_memory_space_constraint(table, pltpu.SMEM)
    held = pltpu.with_memory_space_constraint(held, pltpu.VMEM)
    first_part = pltpu.with_memory_space_constraint(first_part, pltpu.VMEM)

    def solve(own, inner, outer):
        (part,) = call(
            own_kernel, [((6 * W + 8, R), F32, pltpu.VMEM)], [VM, VM], [pltpu.VMEM((OWN, R), F32)],
            cost=pl.CostEstimate(flops=1 << 30, bytes_accessed=4 << 20, transcendentals=0),
        )(held, own)
        depth = 6 * W - FROM
        spill_in, ext = call(
            margin_kernel,
            [(one, BF16), ((depth, R), BF16)],
            [SM] + [VM] * 5,
            [pltpu.VMEM((depth + 8, R), F32)],
        )(table, held, part, own, inner, outer)
        got_in = to_inner(spill_in)
        out, spill_out = call(
            solve_kernel,
            [(block, F32), (one, BF16)],
            [SM] + [VM] * 3,
            [pltpu.VMEM((NS * W + 8, R), F32)],
            cost=pl.CostEstimate(flops=1 << 30, bytes_accessed=4 << 20, transcendentals=0),
        )(table, held, part, ext)
        return out, got_in, spill_out

    def system(first, out, got_in, spill_out, *more):
        part, sent, near = call(
            inner_kernel, [(block, F32), ((NS + 1, WP, R), BF16), (block, BF16)], [VM] * 3
        )(out, got_in, spill_out)
        got, near, far = to_outer(sent), to_inner(near), to_far(spill_out)
        if first:
            (made,) = matrices(False, sent)
            matrix_parts.append(pltpu.with_memory_space_constraint(made, pltpu.VMEM))
        if not first:
            more += tuple(call(first_sums_kernel, [((6, R), F32)], [VM, VM, ANY])(*more, sent))
        outs = [(block, F32)] + ([(block, F32), (one, BF16)] if first else [])
        return call(
            functools.partial(system_kernel, first),
            outs if first else outs + [((6, R), F32)],
            [SM] + [VM] * (7 + len(more)),
            [pltpu.VMEM((3 * NS, WP, R), BF16)],
        )(table, *matrix_parts, part, got, near, far, spill_out, *more)

    matrix_parts = [first_part]
    out, got_in, spill_out = solve(v0, inner, outer)
    p0, w, w_out = system(True, out, got_in, spill_out, v0)
    outer = to_outer(w_out)
    (w_in,) = call(pick_kernel, [(one, BF16)], [VM] * 2)(w, got_in)
    q, sums = system(False, *solve(w, to_inner(w_in), outer), v0, w)
    sums = sums + to_inner(sums)
    gathered = lax.all_to_all(
        jnp.broadcast_to(sums[None], (NSUB // 2, 6, R)), "sub", 0, 0,
        axis_index_groups=[list(range(c, NSUB, 2)) for c in range(2)],
    )
    (flat,) = call(
        finish_kernel,
        [((W * NS, R), F32, pltpu.HBM)],
        [VM] * 3,
        [pltpu.VMEM((W * NS + SPARE, R), F32), pltpu.SemaphoreType.DMA((len(PARTS),))],
    )(gathered, p0, q)
    return flat.reshape(W, NS, R).transpose(1, 0, 2)


def solution(mesh):
    placed = (
        P("sub", None, "rhs"),
        P("sub", None),
        P("sub", None),
        P("sub", None, None),
        P("sub", None),
        P("sub"),
    )
    return jax.shard_map(
        body, mesh=mesh, in_specs=placed, out_specs=P("sub", None, "rhs"), check_vma=False
    )
```

```python
import functools
import jax
import jax.numpy as jnp
from jax import lax
from jax.experimental import pallas as pl
from jax.experimental.pallas import tpu as pltpu
from jax.sharding import PartitionSpec as P

EPS = 1e-06
W = 252
WP = 256
NS = 4
NB = 8
R = 128
NSUB = 64
SHIFT = 1.0
ROWS = NB * W
GROUP = 32
F32 = jnp.float32
BF16 = jnp.bfloat16
CHUNK = 8
SPLIT = 4
EVEN, FIRST, LAST, LOW, HIGH, COUNT, ENDS, NEXT, OUT, SLOTS = range(10)
TABLE = SLOTS + NS * NB
SPARE = 32
OWN = 1024
FROM = 896
ANY = pl.BlockSpec(memory_space=pl.ANY)
PARTS = ((0, 64), (64, 64), (128, 64), (192, 60))
VM = pl.BlockSpec(memory_space=pltpu.VMEM)
SM = pl.BlockSpec(memory_space=pltpu.SMEM)


def call(kernel, outs, ins, scratch=(), limit=24, cost=None):
    return pl.pallas_call(
        kernel,
        out_shape=[keep[0](s, d) if keep else jax.ShapeDtypeStruct(s, d) for s, d, *keep in outs],
        in_specs=ins,
        out_specs=[{pltpu.SMEM: SM, pltpu.HBM: ANY}.get(keep[0], VM) if keep else VM for _, _, *keep in outs],
        scratch_shapes=list(scratch),
        compiler_params=pltpu.CompilerParams(vmem_limit_bytes=limit << 20),
        cost_estimate=cost,
    )


def start_kernel(counts, right, v0_ref, v0b_ref):
    whole = W // 8 * 8
    tail = right[whole * NS :, :]
    for s in range(NS):
        alive = jnp.where(counts[0] > s, 1.0, 0.0)
        v0_ref[s, :whole, :] = right[pl.ds(s, whole, stride=NS), :] * alive
        last = [tail[NS * i + s : NS * i + s + 1, :] * alive for i in range(W - whole)]
        v0_ref[s, whole:, :] = jnp.concatenate(last + [jnp.zeros((WP - W, R), F32)], axis=0)
        v0b_ref[s] = v0_ref[s].astype(BF16)


def fill_table(table, place, counts, margin, neighbours):
    here = place[0]
    even = here % 2 == 0
    first, last = here == 0, here == NSUB - 1
    low = jnp.clip(margin[0, 0] - NS * jnp.maximum(here - 1, 0), 0, NS - 1)
    high = jnp.clip(margin[0, 1] - NS * jnp.minimum(here + 1, NSUB - 1), 0, NS - 1)
    table[EVEN] = jnp.where(even, 1, 0)
    table[FIRST] = jnp.where(first, 1, 0)
    table[LAST] = jnp.where(last, 1, 0)
    table[LOW] = low
    table[HIGH] = high
    table[COUNT] = counts[0]
    table[ENDS] = jnp.where(jnp.logical_or(first, last), 1, 0)
    table[NEXT] = jnp.where(jnp.logical_or(here == 1, here == NSUB - 2), 1, 0)
    table[OUT] = jnp.where(even, low, high)
    for s in range(NS):
        for k in range(NB):
            slot = jnp.clip(neighbours[s, k] - NS * (here - 1), 0, 3 * NS - 1)
            table[SLOTS + s * NB + k] = jnp.where(even, slot, slot + 2 * NS * (1 - slot // NS))


def coupling_kernel(blocks, groups, first, flat, *rest):
    if first:
        inverse, place, counts, margin, neighbours, c_ref, inverse_ref, table, raw, x, lo, hi, sems = rest
    else:
        _, c_ref, raw, x, lo, hi, sems = rest
    lanes = GROUP * W
    count = groups[1] - groups[0]
    step = CHUNK * lanes
    chunks = count // CHUNK
    copies = [
        pltpu.make_async_copy(
            flat.at[:, pl.ds(groups[0] * lanes + c * step, step)],
            raw.at[:, pl.ds(c * step, step)],
            sems.at[c],
        )
        for c in range(chunks)
    ]
    if first:
        copies.append(pltpu.make_async_copy(inverse.at[0], inverse_ref, sems.at[chunks]))
    for copy in copies:
        copy.start()
    if first:
        fill_table(table, place, counts, margin, neighbours)
    lane = lax.broadcasted_iota(jnp.int32, (4 * NS, 128), 1)

    def four(i, carry):
        for h in range(4):
            at = pl.multiple_of((4 * i + h) * lanes, 128)
            x[NS * h : NS * h + NS, :] = raw[:, pl.ds(at, lanes)]
        base = pl.multiple_of(4 * i * (GROUP * NS), 8)
        for s in range(GROUP):
            def rolled(t):
                piece = x[:, 128 * t : 128 * t + 128]
                return pltpu.roll(piece, 4 * s, 1) if s else piece

            middle = rolled(2 * s)
            if s == 0:
                left, right = middle, rolled(1)
            else:
                early = lane < 4 * s
                left = jnp.where(early, rolled(2 * s - 1), middle)
                right = jnp.where(early, middle, rolled(2 * s + 1)) if s < GROUP - 1 else middle
            left, right = left.astype(F32), right.astype(F32)
            for h in range(4):
                at = base + (h * GROUP + s) * NS
                lo[pl.ds(at, NS), :] = left[NS * h : NS * h + NS]
                hi[pl.ds(at, NS), :] = right[NS * h : NS * h + NS]
        return carry

    for c in range(chunks):
        copies[c].wait()
        lax.fori_loop(c * CHUNK // 4, (c + 1) * CHUNK // 4, four, 0)
    keep = lax.broadcasted_iota(jnp.int32, (WP, 128), 1) < W - 128
    pad = jnp.zeros((WP - W, 128), F32)
    skip = (blocks[0] * W - groups[0] * GROUP) * NS
    number = blocks[1] - blocks[0]

    def place(k, carry):
        for p in range(NS):
            row = skip + k * (W * NS) + p
            left = lo[pl.ds(row, W, stride=NS), :]
            right = hi[pl.ds(row, W, stride=NS), :]
            right = jnp.where(keep, jnp.concatenate([right, pad], axis=0), 0.0)
            c_ref[p * number + k, :, :128] = jnp.concatenate([left, pad], axis=0).astype(BF16)
            c_ref[p * number + k, :, 128:] = right.astype(BF16)
        return carry

    lax.fori_loop(0, number, place, 0)
    if first:
        copies[chunks].wait()


def own_kernel(inverse, own, part_ref, ext):
    for s in range(NS):
        ext[s * W : (s + 1) * W, :] = own[s, :W, :]
    ext[NS * W :, :] = jnp.zeros((OWN - NS * W, R), F32)
    part_ref[: 6 * W, :] = jnp.dot(inverse[:, :OWN], ext[...].astype(BF16), preferred_element_type=F32)


def places(table):
    return table[EVEN] == 1, table[FIRST] == 1, table[LAST] == 1, table[LOW], table[HIGH]


def spilled(inverse, part, ext, block, index):
    begin = block * W // 16 * 16
    end = -(-(block + 1) * W // 16) * 16
    end = min(end, 6 * W)
    rows = jnp.dot(inverse[begin:end, FROM:], ext, preferred_element_type=F32)
    rows = rows[block * W - begin : (block + 1) * W - begin] + part[block * W : (block + 1) * W, :]
    mark = jnp.ones((WP - W, R), F32) * index.astype(F32)
    return jnp.concatenate([rows, mark], axis=0)


def margin_kernel(table, inverse, part, own, inner, outer, in_ref, ext_ref, ext):
    even, first, last, low, high = places(table)
    odd = jnp.logical_not(even)
    ext[: NS * W - FROM, :] = jnp.zeros((NS * W - FROM, R), F32)
    some = inner.shape[0] > 1

    def put(when, block, source, index):
        @pl.when(when)
        def _():
            ext[block * W - FROM : (block + 1) * W - FROM, :] = source[index].astype(F32)[:W]

    put(first, NS, own, low)
    put(jnp.logical_and(even, jnp.logical_not(first)), NS, outer, low if some else 0)
    put(odd, NS, inner, low if some else 0)
    put(last, NS + 1, own, high)
    put(jnp.logical_and(odd, jnp.logical_not(last)), NS + 1, outer, high if some else 0)
    put(even, NS + 1, inner, high if some else 0)
    ext_ref[...] = ext[: 6 * W - FROM, :].astype(BF16)

    @pl.when(even)
    def _():
        in_ref[0] = spilled(inverse, part, ext_ref[...], NS + 1, high).astype(BF16)

    @pl.when(odd)
    def _():
        in_ref[0] = spilled(inverse, part, ext_ref[...], NS, low).astype(BF16)


def solve_kernel(table, inverse, part, ext, out_ref, out2_ref, res):
    even, first, last, low, high = places(table)
    mine = NS * W
    res[:mine, :] = part[:mine, :] + jnp.dot(inverse[:mine, FROM:], ext[...], preferred_element_type=F32)
    pad = jnp.zeros((WP - W, R), F32)
    for s in range(NS):
        out_ref[s] = jnp.concatenate([res[s * W : (s + 1) * W, :], pad], axis=0)
    keep = lax.broadcasted_iota(jnp.int32, (WP, R), 0) < W

    def spill(when, ends, block, index):
        @pl.when(when)
        def _():
            rows = spilled(inverse, part, ext[...], block, index)
            out2_ref[0] = rows.astype(BF16)

            @pl.when(ends)
            def _():
                out_ref[index] += jnp.where(keep, rows, 0.0)

    spill(even, first, NS, low)
    spill(jnp.logical_not(even), last, NS + 1, high)


def opened(block):
    x = block.astype(F32)
    rows = lax.broadcasted_iota(jnp.int32, x.shape, 0)
    return jnp.where(rows < W, x, 0.0), x[W : W + 1, :]


def inner_kernel(out, spill_in, spill_out, part_ref, sent_ref, near_ref):
    values, index = opened(spill_in[0])
    for s in range(NS):
        part = out[s] + jnp.where(index == s, values, 0.0)
        part_ref[s] = part
        sent_ref[s] = part.astype(BF16)
        near_ref[s] = part.astype(BF16)
    sent_ref[NS] = spill_out[0]


def system_kernel(
    first, table, ca, cb, part, got, near, far, spill_out, v0, *rest
):
    if first:
        p_ref, w_ref, wout_ref, sums_ref, u = rest
    else:
        w, sums_one, p_ref, sums_ref, u = rest
    got_values, got_index = opened(got[NS])
    got_index = jnp.where(table[ENDS] == 1, -1.0, got_index)
    far_index = jnp.where(table[NEXT] == 1, -1.0, far[0, W : W + 1, :].astype(F32))
    inside = lax.broadcasted_iota(jnp.int32, (WP, R), 0) < W
    far_values = jnp.where(inside, far[0], jnp.zeros((), BF16))
    count = table[COUNT]
    for s in range(NS):
        alive = jnp.where(count > s, 1.0, 0.0)
        p = (part[s] + jnp.where(got_index == s, got_values, 0.0)) * alive
        p_ref[s] = p
        u[s] = got[s]
        u[NS + s] = p.astype(BF16)
        u[2 * NS + s] = near[s] + jnp.where(
            jnp.broadcast_to(far_index, (WP, R)) == s, far_values, jnp.zeros((), BF16)
        )
    index = table[OUT]
    u[index] = (got[index].astype(F32) + opened(spill_out[0])[0]).astype(BF16)
    if first:
        sums_ref[...] = jnp.zeros((6, R), F32)
    else:
        sums_ref[...] = sums_one[...]
    if first:
        w_ref[...] = jnp.zeros((NS, WP, R), F32)

    def one(s):
        acc = p_ref[s]
        for k in range(NB):
            slot = table[SLOTS + s * NB + k]
            matrix = ca[s * SPLIT + k] if k < SPLIT else cb[s * (NB - SPLIT) + k - SPLIT]
            acc += jnp.dot(matrix, u[slot], preferred_element_type=F32)
        image = acc
        start = v0[s]
        if first:
            image = image - SHIFT * start
            w_ref[s] = image
            terms = (start * start, start * image, image * image)
        else:
            terms = (start * image, w[s] * image, image * image)
        sums = [jnp.sum(x, axis=0, keepdims=True) for x in terms]
        rest_of_six = [jnp.zeros((3, R), F32)]
        sums_ref[...] += jnp.concatenate(sums + rest_of_six if first else rest_of_six + sums, axis=0)

    for s in range(NS):
        pl.when(count > s)(functools.partial(one, s))
    if first:
        picked(wout_ref, w_ref, got_index)


def picked(ref, w, index):
    chosen = jnp.zeros((WP, R), F32)
    for s in range(NS):
        chosen = chosen + jnp.where(index == s, w[s], 0.0)
    ref[0] = chosen.astype(BF16)


def pick_kernel(w, spill_in, win_ref):
    picked(win_ref, w, opened(spill_in[0])[1])


def finish_kernel(gathered, p0, q, out_ref, out, sems):
    total = jnp.sum(gathered[...], axis=0)
    s00, s01, s11, s02, s12, s22 = (total[i : i + 1, :] for i in range(6))
    c = SHIFT
    bb = s00 + EPS
    beta = jnp.sqrt(bb)
    h11 = (s01 + c * s00) / bb
    a = c - h11
    n2 = (s11 + 2 * a * s01 + a * a * s00) / bb
    h21s = jnp.maximum(n2, 0.0) + EPS
    h21 = jnp.sqrt(h21s)
    full = bb * h21s
    v0i = s01 + c * s00
    h12 = (s02 + a * v0i) / (bb * h21)
    cross = (s01 + a * s00) / (bb * h21)
    b2i = (s12 + a * s02 + a * (s11 + c * s01) + a * a * v0i) / full
    h22 = b2i - h12 * cross
    ii = (s22 + 2 * a * (s12 + c * s02) + a * a * (s11 + 2 * c * s01 + c * c * s00)) / full
    rest = (
        ii + h12 * h12 * (s00 / bb) + h22 * h22 * (n2 / h21s)
        - 2 * h12 * h12 - 2 * h22 * b2i + 2 * h12 * h22 * cross
    )
    h32s = jnp.maximum(rest, 0.0) + EPS
    g00 = h11 * h11 + h21s
    g01 = h11 * h12 + h21 * h22
    g11 = h12 * h12 + h22 * h22 + h32s
    det = g00 * g11 - g01 * g01
    y1 = beta * (g11 * h11 - g01 * h12) / det
    y2 = beta * (g00 * h12 - g01 * h11) / det
    two = y2 / (beta * h21)
    one = y1 / beta + a * two
    copies = []
    for begin, size in PARTS:
        for s in range(NS):
            p, r = p0[s, begin : begin + size, :], q[s, begin : begin + size, :]
            out[pl.ds(begin * NS + s, size, stride=NS), :] = one * p + two * r
        rows = pl.ds(begin * NS, size * NS)
        copies.append(pltpu.make_async_copy(out.at[rows, :], out_ref.at[rows, :], sems.at[len(copies)]))
        copies[-1].start()
    for copy in copies:
        copy.wait()


def permuted(x, target):
    parts = lax.axis_size("rhs")
    pairs = [(i, j) for i in range(NSUB) for j in range(parts)]
    return lax.ppermute(
        x, ("sub", "rhs"), [(i * parts + j, t[0] * parts + t[1]) for i, j in pairs for t in [target(i, j)]]
    )


def to_inner(x):
    return permuted(x, lambda i, j: (i ^ 1, j))


def to_outer(x):
    return permuted(x, lambda i, j: (i, j ^ 1) if i in (0, NSUB - 1) else (((i + 1) ^ 1) - 1, j))


def to_far(x):
    def target(i, j):
        if i in (0, NSUB - 1):
            return i ^ 1, j
        return i + (2 if i % 2 else -2), j

    return permuted(x, target)


def body(right_side, coupling, neighbours, inverse, margin, counts):
    here = lax.axis_index("sub").astype(jnp.int32).reshape(1)
    flat_right = right_side.transpose(1, 0, 2).reshape(W * NS, R)
    block, one = (NS, WP, R), (1, WP, R)
    v0, v0b = call(start_kernel, [(block, F32), (block, BF16)], [SM, VM])(counts, flat_right)
    outer, inner = to_outer(v0b), to_inner(v0b)

    coupling = pltpu.with_memory_space_constraint(coupling, pltpu.HBM)
    inverse, margin, neighbours = (
        pltpu.with_memory_space_constraint(a, pltpu.HBM) for a in (inverse, margin, neighbours)
    )

    def matrices(first, *more):
        lanes = GROUP * W
        blocks = (0, SPLIT) if first else (SPLIT, NB)
        begin = blocks[0] * W // GROUP
        end = -(-blocks[1] * W // GROUP)
        count = -(-(end - begin) // CHUNK) * CHUNK
        groups = (begin, begin + count) if first else (end - count, end)
        outs = [((NS * (blocks[1] - blocks[0]), WP, WP), BF16, pltpu.VMEM)]
        if first:
            outs += [((6 * W, 6 * W), BF16, pltpu.VMEM), ((TABLE,), jnp.int32, pltpu.SMEM)]
        return call(
            functools.partial(coupling_kernel, blocks, groups, first),
            outs,
            [ANY, ANY] + [SM] * (len(more) - 1),
            [
                pltpu.VMEM((NS, count * lanes), BF16),
                pltpu.VMEM((4 * NS, lanes), BF16),
                pltpu.VMEM((count * GROUP * NS + SPARE, 128), F32),
                pltpu.VMEM((count * GROUP * NS + SPARE, 128), F32),
                pltpu.SemaphoreType.DMA((count // CHUNK + 1,)),
            ],
            limit=24,
            cost=pl.CostEstimate(flops=1 << 20, bytes_accessed=12 << 20, transcendentals=0),
        )(coupling, *more)

    first_part, held, table = matrices(True, inverse, here, counts, margin, neighbours)
    table = pltpu.with_memory_space_constraint(table, pltpu.SMEM)
    held = pltpu.with_memory_space_constraint(held, pltpu.VMEM)
    first_part = pltpu.with_memory_space_constraint(first_part, pltpu.VMEM)

    def solve(own, inner, outer):
        (part,) = call(
            own_kernel, [((6 * W + 8, R), F32, pltpu.VMEM)], [VM, VM], [pltpu.VMEM((OWN, R), F32)],
            cost=pl.CostEstimate(flops=1 << 30, bytes_accessed=4 << 20, transcendentals=0),
        )(held, own)
        depth = 6 * W - FROM
        spill_in, ext = call(
            margin_kernel,
            [(one, BF16), ((depth, R), BF16)],
            [SM] + [VM] * 5,
            [pltpu.VMEM((depth + 8, R), F32)],
        )(table, held, part, own, inner, outer)
        got_in = to_inner(spill_in)
        out, spill_out = call(
            solve_kernel,
            [(block, F32), (one, BF16)],
            [SM] + [VM] * 3,
            [pltpu.VMEM((NS * W + 8, R), F32)],
            cost=pl.CostEstimate(flops=1 << 30, bytes_accessed=4 << 20, transcendentals=0),
        )(table, held, part, ext)
        return out, got_in, spill_out

    def system(first, out, got_in, spill_out, *more):
        part, sent, near = call(
            inner_kernel, [(block, F32), ((NS + 1, WP, R), BF16), (block, BF16)], [VM] * 3
        )(out, got_in, spill_out)
        got, near, far = to_outer(sent), to_inner(near), to_far(spill_out)
        if first:
            (made,) = matrices(False, sent)
            matrix_parts.append(pltpu.with_memory_space_constraint(made, pltpu.VMEM))
        outs = [(block, F32)] + ([(block, F32), (one, BF16)] if first else [])
        return call(
            functools.partial(system_kernel, first),
            outs + [((6, R), F32)],
            [SM] + [VM] * (7 + len(more)),
            [pltpu.VMEM((3 * NS, WP, R), BF16)],
        )(table, *matrix_parts, part, got, near, far, spill_out, *more)

    matrix_parts = [first_part]
    out, got_in, spill_out = solve(v0, inner, outer)
    p0, w, w_out, sums_one = system(True, out, got_in, spill_out, v0)
    outer = to_outer(w_out)
    (w_in,) = call(pick_kernel, [(one, BF16)], [VM] * 2)(w, got_in)
    q, sums = system(False, *solve(w, to_inner(w_in), outer), v0, w, sums_one)
    gathered = lax.all_to_all(jnp.broadcast_to(sums[None], (NSUB, 6, R)), "sub", 0, 0)
    (flat,) = call(
        finish_kernel,
        [((W * NS, R), F32, pltpu.HBM)],
        [VM] * 3,
        [pltpu.VMEM((W * NS + SPARE, R), F32), pltpu.SemaphoreType.DMA((len(PARTS),))],
    )(gathered, p0, q)
    return flat.reshape(W, NS, R).transpose(1, 0, 2)


def solution(mesh):
    placed = (
        P("sub", None, "rhs"),
        P("sub", None),
        P("sub", None),
        P("sub", None, None),
        P("sub", None),
        P("sub"),
    )
    return jax.shard_map(
        body, mesh=mesh, in_specs=placed, out_specs=P("sub", None, "rhs"), check_vma=False
    )
```
